128 devices in a mesh: ctx: 64 (over z, x, y), tensor: 2 (over core).
Axes of the slice: x: 4, y: 4, z: 4, core: 2. Of those that a mesh axis runs over, the one named last changes fastest.
Arguments:
- queries: bfloat16 [16384, 2048], P('ctx', 'tensor'), may hold values from -4 to 4
- keys: bfloat16 [16384, 2048], P('ctx', 'tensor'), may hold values from -4 to 4
- values: bfloat16 [16384, 2048], P('ctx', 'tensor'), may hold values from -48 to 48
- rates: float32 [16, 16384], P('tensor', 'ctx'), as said below
- init_weight: float32 [16, 128, 128], P('tensor'), may hold values from -0.5 to 0.5
- gain: float32 [2048], P('tensor'), may hold values from 0.5 to 1.5
- cotangent: bfloat16 [16384, 2048], P('ctx', 'tensor'), may hold values from -5 to 5
Outputs:
- normed: bfloat16 [16384, 2048], P('ctx', 'tensor')
- grad_queries: bfloat16 [16384, 2048], P('ctx', 'tensor')
- grad_keys: bfloat16 [16384, 2048], P('ctx', 'tensor')
- grad_values: bfloat16 [16384, 2048], P('ctx', 'tensor')
- grad_rates: float32 [16, 16384], P('tensor', 'ctx')
- grad_init: float32 [16, 16384], P('tensor', 'ctx')
The draws below stay inside these ranges and needn't reach their ends.
Inputs may be any that keep to these rules, and one draw needn't show every extreme that they name: `rates`: every rate times 128 lies between 0.0006 and 1.12.
All inputs are finite; a program needn't handle non-finite values.
Results may differ from the reference program's by a relative error of at most 0.022.
Values sent between devices are 32-bit elements; how exact they have to be, the bound alone decides.
No kernel may reach another device: no remote copies, remote signals or barrier semaphores. Data moves between devices by JAX's collectives and lax.ppermute only.
A program may use at most 256 MiB of HBM per device.

```python
import jax
import jax.numpy as jnp
from jax import lax

HEADS = 16
HEAD = 128
MB = 16
WINDOW_TOKENS = 16384
WIDTH = 2048


def draw_values(key, part):
    key = jax.random.fold_in(key, 5)
    key_base, key_cols, key_rows = jax.random.split(key, 3)
    full_width = HEADS * HEAD
    column = jnp.arange(full_width, dtype=jnp.float32) / full_width
    col_scale = jnp.exp(column * jnp.log(3.0)) * jnp.exp(jax.random.uniform(key_cols, (full_width,), minval=-0.69, maxval=0.69))
    base_draw = jax.random.truncated_normal(key_base, -4.0, 4.0, (WINDOW_TOKENS, full_width))
    row_scale = jnp.exp(jax.random.uniform(key_rows, (WINDOW_TOKENS, 1), minval=-0.69, maxval=0.69))
    return (base_draw * row_scale * col_scale[None, :]).astype(jnp.bfloat16)


def draw_rates(key, part):
    key = jax.random.fold_in(key, 9)
    key_head, key_token, key_position = jax.random.split(key, 3)
    rate_per_head = jnp.exp(jax.random.uniform(key_head, (HEADS, 1), minval=jnp.log(0.001), maxval=jnp.log(0.8)))
    token_multiplier = jnp.exp(jax.random.uniform(key_token, (HEADS, WINDOW_TOKENS), minval=jnp.log(0.6), maxval=jnp.log(1.4)))
    spike_positions = jax.random.randint(key_position, (8,), 0, WINDOW_TOKENS)
    spike_mask = jnp.any(jnp.arange(WINDOW_TOKENS)[:, None] == spike_positions[None, :], axis=1)
    rescaled_values = jnp.where(spike_mask[None, :], 0.8, rate_per_head * token_multiplier)
    return (rescaled_values / HEAD).astype(jnp.float32)


def levels(stream_key, dims, cuts, smallest, largest):
    level = 1.0
    for axis_at, parts in cuts:
        draws = jax.random.uniform(jax.random.fold_in(jax.random.fold_in(stream_key, 6), axis_at), (parts,), jnp.float32, smallest / len(cuts), largest / len(cuts))
        level = level * jnp.repeat(jnp.exp(draws), dims[axis_at] // parts).reshape((-1,) + (1,) * (len(dims) - 1 - axis_at))
    return level


def centred(stream_key, extent, scale, most, cuts=(), kind=jnp.bfloat16):
    loudness = levels(stream_key, extent, cuts, -0.22, 0.18) if cuts else 1.0
    entries = jax.random.normal(stream_key, extent, jnp.float32) * scale * loudness
    return jnp.minimum(jnp.maximum(entries, -most), most).astype(kind)


def setup_inputs(seed: int = 0) -> dict:
    seeds = jax.random.split(jax.random.key(seed), 8)
    return {
        "queries": centred(seeds[0], (WINDOW_TOKENS, WIDTH), 1.0, 4.0, ((0, 64), (1, 2))),
        "keys": centred(seeds[1], (WINDOW_TOKENS, WIDTH), 1.0, 4.0, ((0, 64), (1, 2))),
        "values": draw_values(jax.random.fold_in(seeds[7], 71), 0),
        "rates": draw_rates(jax.random.fold_in(seeds[7], 71), 0),
        "init_weight": centred(seeds[4], (HEADS, HEAD, HEAD), HEAD ** -0.5, 0.5, ((0, 2),), jnp.float32),
        "gain": jnp.clip(1.0 + 0.1 * jax.random.normal(seeds[5], (WIDTH,), jnp.float32), 0.5, 1.5),
        "cotangent": centred(seeds[6], (WINDOW_TOKENS, WIDTH), 1.0, 5.0, ((0, 64), (1, 2))),
    }


epsilon = 1e-06
highest = lax.Precision.HIGHEST

def blocks(array):
    row_count = array.shape[0]
    head_count = array.shape[1] // HEAD
    shaped = array.astype(jnp.float32).reshape(row_count // MB, MB, head_count, HEAD)
    return jnp.transpose(shaped, (0, 2, 1, 3))

def rate_layout(array):
    head_count, row_count = array.shape
    return jnp.transpose(array.reshape(head_count, row_count // MB, MB), (1, 0, 2))

def unblock(array):
    count, head_count, size, depth = array.shape
    return jnp.transpose(array, (0, 2, 1, 3)).reshape(count * size, head_count * depth)

def split_product(form, data, state):
    data_low = data.astype(jnp.bfloat16)
    high_part = lax.optimization_barrier(state.astype(jnp.bfloat16))
    low_part = (state - high_part.astype(jnp.float32)).astype(jnp.bfloat16)
    return jnp.einsum(form, data_low, high_part, preferred_element_type=jnp.float32) + jnp.einsum(form, data_low, low_part, preferred_element_type=jnp.float32)

def gram(query_blocks, key_blocks):
    return jnp.einsum('htc,hsc->hts', query_blocks.astype(jnp.bfloat16), key_blocks.astype(jnp.bfloat16), preferred_element_type=jnp.float32)

def inner_step(inner_state, minibatch):
    query_blocks, key_blocks, value_blocks, rate_blocks = minibatch
    residual = split_product('hsc,hcd->hsd', key_blocks, inner_state) - value_blocks
    scores = gram(query_blocks, key_blocks) * rate_blocks[:, None, :]
    size = query_blocks.shape[1]
    causal = jnp.tril(jnp.ones((size, size), scores.dtype))
    scores = scores * causal
    output = split_product('htc,hcd->htd', query_blocks, inner_state) - jnp.einsum('hts,hsd->htd', scores, residual, precision=highest)
    scaled_residual = residual * rate_blocks[:, :, None]
    inner_state = inner_state - split_product('hsc,hsd->hcd', key_blocks, scaled_residual)
    return (inner_state, output)

def inner_pass(start_state, query_blocks, key_blocks, value_blocks, rate_blocks):
    final_state, outputs = lax.scan(inner_step, start_state, (query_blocks, key_blocks, value_blocks, rate_blocks))
    return (outputs, final_state)

def ttt_layer(queries, keys, values, rates, init_weight, gain):
    outputs, final_state = inner_pass(init_weight, blocks(queries), blocks(keys), blocks(values), rate_layout(rates))
    hidden = unblock(outputs)
    inv_scale = lax.rsqrt(lax.optimization_barrier(jnp.mean(hidden * hidden, axis=1, keepdims=True)) + epsilon)
    return hidden * inv_scale * gain[None, :]

def reference(queries, keys, values, rates, init_weight, gain, cotangent):
    result, pullback = jax.vjp(ttt_layer, queries, keys, values, rates, init_weight, gain)
    grads = pullback(cotangent.astype(result.dtype))
    head_count = grads[4].shape[0]
    return (result.astype(jnp.bfloat16), grads[0].astype(jnp.bfloat16), grads[1].astype(jnp.bfloat16), grads[2].astype(jnp.bfloat16), grads[3], grads[4].reshape(head_count, HEAD * HEAD))
```

```python
import jax
import jax.numpy as jnp
from jax import lax
from jax.experimental import pallas as pl
from jax.experimental.pallas import tpu as pltpu
from jax.sharding import PartitionSpec as P

HEAD = 128
MB = 16
EPSILON = 1e-06
GROUP = 8
F32 = jnp.float32
BF16 = jnp.bfloat16


def low(a):
    return a.astype(BF16)


def dot(a, b):
    return jnp.dot(a, b, preferred_element_type=F32)


def dot_nt(a, b):
    return lax.dot_general(a, b, (((1,), (1,)), ((), ())), preferred_element_type=F32)


def dot_tn(a, b):
    return lax.dot_general(a, b, (((0,), (0,)), ((), ())), preferred_element_type=F32)


def halves(a):
    high = low(a)
    return high, low(a - high.astype(F32))


def exact(a, b, product=dot):
    (ah, al), (bh, bl) = a, b
    return product(ah, bh) + (product(ah, bl) + product(al, bh))


def call(kernel, outs, args, smem=0, scratch=(), limit=32):
    specs = [pl.BlockSpec(memory_space=pltpu.SMEM)] * smem
    specs += [pl.BlockSpec(memory_space=pltpu.VMEM)] * (len(args) - smem)
    size = sum(a.size * a.dtype.itemsize for a in args)
    size += sum(o.size * o.dtype.itemsize for o in outs)
    return pl.pallas_call(
        kernel,
        out_shape=outs,
        in_specs=specs,
        out_specs=[pl.BlockSpec(memory_space=pltpu.VMEM)] * len(outs),
        scratch_shapes=list(scratch),
        compiler_params=pltpu.CompilerParams(vmem_limit_bytes=limit * 2**20),
        cost_estimate=pl.CostEstimate(flops=2 * 10**9, bytes_accessed=size, transcendentals=0),
        name=kernel.__name__,
    )(*args)


def columns(h):
    return slice(h * HEAD, (h + 1) * HEAD)


def map_kernel(k_ref, v_ref, e_ref, ab_ref, t_ref, tkv_ref):
    n = k_ref.shape[0]
    heads = e_ref.shape[0]
    row = lax.broadcasted_iota(jnp.int32, (n, n), 0)
    col = lax.broadcasted_iota(jnp.int32, (n, n), 1)
    eye = (row == col).astype(F32)
    small = (
        lax.broadcasted_iota(jnp.int32, (HEAD, HEAD), 0)
        == lax.broadcasted_iota(jnp.int32, (HEAD, HEAD), 1)
    ).astype(F32)
    masks = []
    width = MB
    while width < n:
        masks.append((row // (2 * width) == col // (2 * width)) & (row // width > col // width))
        width *= 2
    for first in range(0, heads, 4):
        batch = range(first, first + 4)
        ks = [k_ref[:, columns(h)] for h in batch]
        rates = [e_ref[h : h + 1, :] for h in batch]
        grams = [dot_nt(k, k) * e for k, e in zip(ks, rates)]
        inverses = [eye - jnp.where(masks[0], g, 0.0) for g in grams]
        for mask in masks[1:]:
            lows = [low(t) for t in inverses]
            mids = [dot(low(jnp.where(mask, g, 0.0)), t) for g, t in zip(grams, lows)]
            inverses = [t - dot(b, low(m)) for t, b, m in zip(inverses, lows, mids)]
        lows = [low(t) for t in inverses]
        tkvs = [
            low(dot(t, jnp.concatenate([k, v_ref[:, columns(h)]], axis=1)))
            for t, k, h in zip(lows, ks, batch)
        ]
        scaled = [low(jnp.transpose(k.astype(F32)) * e) for k, e in zip(ks, rates)]
        abs_ = [dot(s, x) for s, x in zip(scaled, tkvs)]
        for i, h in enumerate(batch):
            ab_ref[h, :, :HEAD] = small - abs_[i][:, :HEAD]
            ab_ref[h, :, HEAD:] = abs_[i][:, HEAD:]
            t_ref[h] = lows[i]
            tkv_ref[h] = tkvs[i]


def prepare_kernel(q_ref, k_ref, e_ref, t_ref, tkv_ref, qt_ref, c_ref, se_ref, tek_ref):
    n = k_ref.shape[0]
    heads = e_ref.shape[0]
    row = lax.broadcasted_iota(jnp.int32, (n, n), 0)
    col = lax.broadcasted_iota(jnp.int32, (n, n), 1)
    causal = row >= col
    for h in range(heads):
        q = q_ref[:, columns(h)]
        k = k_ref[:, columns(h)]
        e = e_ref[h : h + 1, :]
        se = low(jnp.where(causal, dot_nt(q, k) * e, 0.0))
        sx = dot(se, tkv_ref[h])
        qt_ref[h] = low(q.astype(F32) - sx[:, :HEAD])
        c_ref[h] = sx[:, HEAD:]
        se_ref[h] = se
        wide = jnp.transpose(jnp.broadcast_to(e, (HEAD, n)))
        tek_ref[h] = low(dot_tn(t_ref[h], low(k.astype(F32) * wide)))


def compose(early, late):
    wide = exact(halves(late[:, :HEAD]), halves(early))
    return jnp.concatenate([wide[:, :HEAD], wide[:, HEAD:] + late[:, HEAD:]], axis=1)


def group_kernel(ab_ref, all_ref, tree_ref):
    pairs = [compose(ab_ref[2 * i], ab_ref[2 * i + 1]) for i in range(4)]
    quads = [compose(pairs[2 * i], pairs[2 * i + 1]) for i in range(2)]
    whole = compose(quads[0], quads[1])
    for i, a in enumerate(pairs + quads):
        tree_ref[i] = a
    for i in range(GROUP):
        all_ref[i] = whole


def apply_map(ab, w):
    return exact(halves(ab[:, :HEAD]), halves(w)) + ab[:, HEAD:]


def start_kernel(group_ref, ab_ref, tree_ref, groups_ref, init_ref, w_ref):
    w0 = lax.fori_loop(
        0, group_ref[0], lambda g, w: apply_map(groups_ref[g], w), init_ref[...]
    )
    w4 = apply_map(tree_ref[4], w0)
    w2 = apply_map(tree_ref[0], w0)
    w6 = apply_map(tree_ref[2], w4)
    for i, w in zip((0, 2, 4, 6), (w0, w2, w4, w6)):
        w_ref[i] = w
        w_ref[i + 1] = apply_map(ab_ref[i], w)


def hidden_kernel(qt_ref, c_ref, w_ref, cot_ref, gain_ref, z_ref, stats_ref):
    heads, n = qt_ref.shape[:2]
    squares = jnp.zeros((n, HEAD), F32)
    products = jnp.zeros((n, HEAD), F32)
    for h in range(heads):
        z = dot(qt_ref[h], low(w_ref[h])) + c_ref[h]
        z_ref[:, columns(h)] = z
        squares += z * z
        products += z * (cot_ref[:, columns(h)].astype(F32) * gain_ref[:, columns(h)])
    lane = lax.broadcasted_iota(jnp.int32, (n, HEAD), 1)
    stats_ref[...] = jnp.where(
        lane < HEAD // 2,
        jnp.sum(squares, axis=1, keepdims=True),
        jnp.sum(products, axis=1, keepdims=True),
    )


def norm_kernel(z_ref, cot_ref, gain_ref, own_ref, other_ref, qt_ref, normed_ref, dz_ref, g_ref):
    heads = qt_ref.shape[0]
    width = 2 * z_ref.shape[1]
    stats = own_ref[...] + other_ref[...]
    inv = lax.rsqrt(stats[:, 0:1] / width + EPSILON)
    shift = inv * inv * inv * stats[:, HEAD // 2 : HEAD // 2 + 1] / width
    for h in range(heads):
        z = z_ref[:, columns(h)]
        gain = gain_ref[:, columns(h)]
        normed_ref[:, columns(h)] = low(z * inv * gain)
        dz = low(inv * (cot_ref[:, columns(h)].astype(F32) * gain) - z * shift)
        dz_ref[:, columns(h)] = dz
        g_ref[h] = dot_tn(qt_ref[h], dz)


def query_kernel(
    q_ref, k_ref, e_ref, t_ref, tkv_ref, se_ref, w_ref, dz_ref, dq_ref, u_ref, dk_ref, r_ref
):
    n = k_ref.shape[0]
    heads = e_ref.shape[0]
    row = lax.broadcasted_iota(jnp.int32, (n, n), 0)
    col = lax.broadcasted_iota(jnp.int32, (n, n), 1)
    causal = row >= col
    for h in range(heads):
        e = e_ref[h : h + 1, :]
        w = low(w_ref[h])
        dz = dz_ref[:, columns(h)]
        r = low(dot(tkv_ref[h, :, :HEAD], w) - tkv_ref[h, :, HEAD:].astype(F32))
        r_ref[h] = r
        ds = low(jnp.where(causal, dot_nt(dz, r) * -e, 0.0))
        dq_ref[:, columns(h)] = low(dot_nt(dz, w) + dot(ds, k_ref[:, columns(h)]))
        dk_ref[h] = dot_tn(ds, q_ref[:, columns(h)])
        u_ref[h] = -dot_tn(t_ref[h], low(dot_tn(se_ref[h], dz)))


def transposed_map(a, later, own):
    return exact(halves(a), halves(later), dot_tn) + own


def gather_kernel(ab_ref, tree_ref, g_ref, all_ref, sums_ref):
    pairs = [
        transposed_map(ab_ref[2 * i, :, :HEAD], g_ref[2 * i + 1], g_ref[2 * i]) for i in range(4)
    ]
    quads = [
        transposed_map(tree_ref[2 * i, :, :HEAD], pairs[2 * i + 1], pairs[2 * i])
        for i in range(2)
    ]
    whole = transposed_map(tree_ref[4, :, :HEAD], quads[1], quads[0])
    for i, a in enumerate(pairs + quads):
        sums_ref[i] = a
    for i in range(GROUP):
        all_ref[i] = whole


def end_kernel(
    group_ref, ab_ref, tree_ref, groups_ref, g_ref, sums_ref, later_ref, d_ref, init_ref
):
    group = group_ref[0]

    def step(i, d):
        g = GROUP - 1 - i
        return transposed_map(groups_ref[g, :, :HEAD], d, later_ref[g])

    d7 = lax.fori_loop(0, GROUP - 1 - group, step, jnp.zeros((HEAD, HEAD), F32))
    init_ref[...] = lax.fori_loop(GROUP - 1 - group, GROUP, step, d7)
    d3 = transposed_map(tree_ref[5, :, :HEAD], d7, sums_ref[5])
    d1 = transposed_map(tree_ref[1, :, :HEAD], d3, sums_ref[1])
    d5 = transposed_map(tree_ref[3, :, :HEAD], d7, sums_ref[3])
    for i, d in zip((1, 3, 5, 7), (d1, d3, d5, d7)):
        d_ref[i, :HEAD, :] = d
        d_ref[i - 1, :HEAD, :] = transposed_map(ab_ref[i, :, :HEAD], d, g_ref[i])
    rows = init_ref[pl.ds(pl.multiple_of(group * 16, 16), 16), :]
    for i in range(GROUP):
        d_ref[i, HEAD:, :] = jnp.zeros((8, HEAD), F32)
        d_ref[i, HEAD : HEAD + 2, :] = rows[2 * i : 2 * i + 2]


def key_kernel(
    k_ref, e_ref, tek_ref, w_ref, r_ref, u_ref, dkp_ref, d_ref, dk_ref, dv_ref, de_ref, gi_ref
):
    n = k_ref.shape[0]
    heads = e_ref.shape[0]
    row = lax.broadcasted_iota(jnp.int32, (n, n), 0)
    col = lax.broadcasted_iota(jnp.int32, (n, n), 1)
    before = row // MB > col // MB
    ones = jnp.ones((8, HEAD), BF16)
    for h in range(heads):
        e = e_ref[h : h + 1, :]
        k = k_ref[:, columns(h)]
        r = r_ref[h]
        d = low(d_ref[h, :HEAD, :])
        uf = u_ref[h] - dot(tek_ref[h], d)
        u = low(uf)
        dv_ref[:, columns(h)] = low(-uf)
        ph, pl_ = halves(uf * r.astype(F32))
        de_ref[h : h + 1, :] = (dot_nt(ones, ph) + dot_nt(ones, pl_))[0:1] / e
        x = low(jnp.where(before, dot_nt(u, r) * e, 0.0))
        wide = jnp.transpose(jnp.broadcast_to(e, (HEAD, n)))
        dk = dkp_ref[h] + dot_nt(u, low(w_ref[h])) - wide * dot_nt(r, d)
        dk_ref[:, columns(h)] = low(dk - dot(x, k) - dot_tn(x, k))
        gi_ref[h : h + 1, :HEAD] = d_ref[h, HEAD : HEAD + 1, :]
        gi_ref[h : h + 1, HEAD:] = d_ref[h, HEAD + 1 : HEAD + 2, :]


def local(queries, keys, values, rates, init_weight, gain, cotangent):
    n, width = keys.shape
    heads = width // HEAD
    count = lax.axis_size("ctx") // GROUP
    near = [[g * GROUP + i for i in range(GROUP)] for g in range(count)]
    far = [[g * GROUP + i for g in range(count)] for i in range(GROUP)]
    place = lax.axis_index("ctx")
    group = (place // GROUP).astype(jnp.int32).reshape(1)
    own_init = lax.dynamic_index_in_dim(init_weight, place % GROUP, 0, False)
    gain_row = gain.reshape(1, width)

    def shape(dims, dtype=F32):
        return jax.ShapeDtypeStruct(dims, dtype)

    def swap(a, groups):
        return lax.all_to_all(a, "ctx", 0, 0, axis_index_groups=groups)

    square = (GROUP, HEAD, HEAD)
    wide = (GROUP, HEAD, 2 * HEAD)
    tall = (heads, n, HEAD)
    full = (heads, n, n)

    maps, inverse, tkv = call(
        map_kernel, [shape(wide), shape(full, BF16), shape((heads, n, 2 * HEAD), BF16)],
        [keys, values, rates],
    )
    own_maps = swap(maps, near)
    qt, offset, scores, tek = call(
        prepare_kernel, [shape(tall, BF16), shape(tall), shape(full, BF16), shape(tall, BF16)],
        [queries, keys, rates, inverse, tkv],
    )
    sent, tree = call(group_kernel, [shape(wide), shape((6, HEAD, 2 * HEAD))], [own_maps])
    group_maps = swap(sent, far)
    (starts,) = call(
        start_kernel, [shape(square)], [group, own_maps, tree, group_maps, own_init], smem=1
    )
    weights = swap(starts, near)
    hidden, stats = call(
        hidden_kernel, [shape((n, width)), shape((n, HEAD))],
        [qt, offset, weights, cotangent, gain_row],
    )
    other = lax.ppermute(stats, "tensor", [(0, 1), (1, 0)])
    normed, dz, local_grad = call(
        norm_kernel, [shape((n, width), BF16), shape((n, width), BF16), shape(square)],
        [hidden, cotangent, gain_row, stats, other, qt],
    )
    own_grads = swap(local_grad, near)
    grad_queries, u, dk_part, residual = call(
        query_kernel,
        [shape((n, width), BF16), shape(tall), shape(tall), shape(tall, BF16)],
        [queries, keys, rates, inverse, tkv, scores, weights, dz],
    )
    sent, sums = call(
        gather_kernel, [shape(square), shape((6, HEAD, HEAD))], [own_maps, tree, own_grads]
    )
    group_grads = swap(sent, far)
    (ends,) = call(
        end_kernel, [shape((GROUP, HEAD + 8, HEAD))],
        [group, own_maps, tree, group_maps, own_grads, sums, group_grads], smem=1,
        scratch=[pltpu.VMEM((HEAD, HEAD), F32)],
    )
    adjoint = swap(ends, near)
    grad_keys, grad_values, grad_rates, grad_init = call(
        key_kernel,
        [shape((n, width), BF16), shape((n, width), BF16), shape((heads, n)), shape((heads, n))],
        [keys, rates, tek, weights, residual, u, dk_part, adjoint],
    )
    return (normed, grad_queries, grad_keys, grad_values, grad_rates, grad_init)


def solution(mesh):
    in_specs = (
        P("ctx", "tensor"),
        P("ctx", "tensor"),
        P("ctx", "tensor"),
        P("tensor", "ctx"),
        P("tensor", None, None),
        P("tensor"),
        P("ctx", "tensor"),
    )
    out_specs = (
        P("ctx", "tensor"),
        P("ctx", "tensor"),
        P("ctx", "tensor"),
        P("ctx", "tensor"),
        P("tensor", "ctx"),
        P("tensor", "ctx"),
    )
    return jax.shard_map(local, mesh=mesh, in_specs=in_specs, out_specs=out_specs, check_vma=False)
```

```python
import jax
import jax.numpy as jnp
from jax import lax
from jax.experimental import pallas as pl
from jax.experimental.pallas import tpu as pltpu
from jax.sharding import PartitionSpec as P

HEAD = 128
MB = 16
EPSILON = 1e-06
GROUP = 8
F32 = jnp.float32
BF16 = jnp.bfloat16


def low(a):
    return a.astype(BF16)


def dot(a, b):
    return jnp.dot(a, b, preferred_element_type=F32)


def dot_nt(a, b):
    return lax.dot_general(a, b, (((1,), (1,)), ((), ())), preferred_element_type=F32)


def dot_tn(a, b):
    return lax.dot_general(a, b, (((0,), (0,)), ((), ())), preferred_element_type=F32)


def halves(a):
    high = low(a)
    return high, low(a - high.astype(F32))


def exact(a, b, product=dot):
    (ah, al), (bh, bl) = a, b
    return product(ah, bh) + (product(ah, bl) + product(al, bh))


def call(kernel, outs, args, scratch=(), copies=0, limit=24):
    spaces = {"s": pltpu.SMEM, "v": pltpu.VMEM, "h": pltpu.HBM, "a": pltpu.VMEM}
    values = [pltpu.with_memory_space_constraint(a, pltpu.HBM) if p in "ha" else a for a, p in args]
    results = [
        pltpu.HBM(shape, dtype) if p in "ha" else jax.ShapeDtypeStruct(shape, dtype)
        for shape, dtype, p in outs
    ]
    size = sum(a.size * a.dtype.itemsize for a in values)
    scratch = list(scratch)
    if copies:
        scratch.append(pltpu.SemaphoreType.DMA((copies,)))
    return pl.pallas_call(
        kernel,
        out_shape=results,
        in_specs=[pl.BlockSpec(memory_space=spaces[p]) for _, p in args],
        out_specs=[pl.BlockSpec(memory_space=spaces[p]) for _, _, p in outs],
        scratch_shapes=scratch,
        compiler_params=pltpu.CompilerParams(vmem_limit_bytes=limit * 2**20),
        cost_estimate=pl.CostEstimate(
            flops=2 * 10**9, bytes_accessed=2 * size, transcendentals=0
        ),
        name=kernel.__name__,
    )(*values)


class Copies:
    def __init__(self, semaphores):
        self.semaphores = semaphores
        self.started = []

    def start(self, source, target):
        copy = pltpu.make_async_copy(source, target, self.semaphores.at[len(self.started)])
        copy.start()
        self.started.append(copy)
        return copy


def columns(h):
    return slice(h * HEAD, (h + 1) * HEAD)


def span(first, last):
    return slice(first * HEAD, last * HEAD)


BATCH = 4


def map_kernel(
    k_hbm, v_hbm, e_hbm, ab_hbm, t_hbm, n_hbm, tkv_hbm,
    k_ref, v_ref, e_ref, ab_ref, t_ref, n_ref, tkv_ref, sems,
):
    heads = e_ref.shape[0]
    half = t_ref.shape[-1]
    copies = Copies(sems)
    arrivals = []
    for first in range(0, heads, BATCH):
        part = span(first, first + BATCH)
        key = copies.start(k_hbm.at[:, part], k_ref.at[:, part])
        if first == 0:
            rates = copies.start(e_hbm, e_ref)
        arrivals.append((key, copies.start(v_hbm.at[:, part], v_ref.at[:, part])))
    row = lax.broadcasted_iota(jnp.int32, (half, half), 0)
    col = lax.broadcasted_iota(jnp.int32, (half, half), 1)
    eye = (row == col).astype(F32)
    masks = []
    width = MB
    while width < half:
        masks.append((row // (2 * width) == col // (2 * width)) & (row // width > col // width))
        width *= 2
    sent = []
    ks, es, blocks, crosses, scaled = [], [], [], [], []
    for first, (key, _) in zip(range(0, heads, BATCH), arrivals):
        key.wait()
        if first == 0:
            rates.wait()
        for h in range(first, first + BATCH):
            k = k_ref[:, columns(h)]
            e = e_ref[h : h + 1, :]
            top = -(dot_nt(k[:half], k[:half]) * e[:, :half])
            bottom = -(dot_nt(k[half:], k) * e)
            blocks += [top, bottom[:, half:]]
            crosses.append(low(bottom[:, :half]))
            ks.append(k)
            es.append(e)
    inverses = [low(eye + jnp.where(masks[0], b, 0.0)) for b in blocks]
    for mask in masks[1:]:
        mids = [low(dot(low(jnp.where(mask, b, 0.0)), t)) for b, t in zip(blocks, inverses)]
        inverses = [t + low(dot(t, m)) for t, m in zip(inverses, mids)]
    for h in range(heads):
        t_ref[h, 0] = inverses[2 * h]
        t_ref[h, 1] = inverses[2 * h + 1]
        n_ref[h] = crosses[h]
    sent.append(copies.start(t_ref, t_hbm))
    sent.append(copies.start(n_ref, n_hbm))
    for _, value in arrivals:
        value.wait()
    kvs = [jnp.concatenate([ks[h], v_ref[:, columns(h)]], axis=1) for h in range(heads)]
    tops = [low(dot(t, kv[:half])) for t, kv in zip(inverses[::2], kvs)]
    scaled = [low(jnp.transpose(k.astype(F32)) * e) for k, e in zip(ks, es)]
    mids = [low(kv[half:].astype(F32) + dot(c, x)) for kv, c, x in zip(kvs, crosses, tops)]
    bottoms = [low(dot(t, m)) for t, m in zip(inverses[1::2], mids)]
    for h in range(heads):
        tkv_ref[h, :half] = tops[h]
        tkv_ref[h, half:] = bottoms[h]
    sent.append(copies.start(tkv_ref, tkv_hbm))
    for h in range(heads):
        ab = dot(scaled[h], tkv_ref[h])
        ab_ref[h, :, :HEAD] = eye - ab[:, :HEAD]
        ab_ref[h, :, HEAD:] = ab[:, HEAD:]
        if h % 2 == 1:
            sent.append(copies.start(ab_ref.at[h - 1 : h + 1], ab_hbm.at[h - 1 : h + 1]))
    for copy in sent:
        copy.wait()


def prepare_kernel(
    q_ref, k_ref, e_ref, t_ref, n_ref, tkv_ref, init_hbm,
    qt_ref, qtt_ref, c_ref, st_ref, tek_ref, own_hbm, token_ref, sems,
):
    initial = Copies(sems).start(init_hbm.at[lax.axis_index("ctx") % GROUP], own_hbm)
    n = k_ref.shape[0]
    half = n // 2
    heads = e_ref.shape[0]
    row = lax.broadcasted_iota(jnp.int32, (n, n), 0)
    col = lax.broadcasted_iota(jnp.int32, (n, n), 1)
    causal = row >= col
    token_ref[...] = jnp.zeros_like(token_ref)
    for h in range(heads):
        q = q_ref[:, columns(h)]
        k = k_ref[:, columns(h)]
        e = e_ref[h : h + 1, :]
        se = low(jnp.where(causal, dot_nt(q, k) * e, 0.0))
        sx = dot(se, tkv_ref[h])
        qt = q.astype(F32) - sx[:, :HEAD]
        qt_ref[h] = low(qt)
        qtt_ref[h] = low(jnp.transpose(qt))
        c_ref[h] = sx[:, HEAD:]
        top, bottom = t_ref[h, 0], t_ref[h, 1]
        cross = low(dot(bottom, low(dot(n_ref[h], top))))
        t = jnp.concatenate(
            [
                jnp.concatenate([top, jnp.zeros((half, half), BF16)], axis=1),
                jnp.concatenate([cross, bottom], axis=1),
            ],
            axis=0,
        )
        st_ref[h] = low(-dot(se, t))
        wide = jnp.transpose(jnp.broadcast_to(e, (HEAD, n)))
        tek_ref[h] = low(dot_tn(t, low(k.astype(F32) * wide)))
    initial.wait()


def compose(early, late):
    wide = exact(halves(late[:, :HEAD]), halves(early))
    return jnp.concatenate([wide[:, :HEAD], wide[:, HEAD:] + late[:, HEAD:]], axis=1)


def broadcast(copies, source, targets):
    sent = [copies.start(source, targets.at[i]) for i in range(GROUP)]
    for copy in sent:
        copy.wait()


def group_kernel(ab_ref, token_ref, all_ref, tree_hbm, tree_ref, sems):
    copies = Copies(sems)
    pairs = [compose(ab_ref[2 * i], ab_ref[2 * i + 1]) for i in range(4)]
    quads = [compose(pairs[2 * i], pairs[2 * i + 1]) for i in range(2)]
    for i, a in enumerate(pairs + quads):
        tree_ref[i] = a
    tree = copies.start(tree_ref, tree_hbm)
    whole = compose(quads[0], quads[1])
    for i in range(GROUP):
        all_ref[i] = whole
    tree.wait()


def apply_map(ab, w):
    return exact(halves(ab[:, :HEAD]), halves(w)) + ab[:, HEAD:]


def start_kernel(ab_ref, tree_ref, groups_ref, init_ref, w_ref):
    group = lax.axis_index("ctx") // GROUP
    w0 = lax.fori_loop(0, group, lambda g, w: apply_map(groups_ref[g], w), init_ref[...])
    w4 = apply_map(tree_ref[4], w0)
    w2 = apply_map(tree_ref[0], w0)
    w6 = apply_map(tree_ref[2], w4)
    for i, w in zip((0, 2, 4, 6), (w0, w2, w4, w6)):
        w_ref[i] = w
        w_ref[i + 1] = apply_map(ab_ref[i], w)


def adjoint_kernel(ab_ref, groups_ref, inside_ref, after_ref, first_ref, token_ref):
    eye = (
        lax.broadcasted_iota(jnp.int32, (HEAD, HEAD), 0)
        == lax.broadcasted_iota(jnp.int32, (HEAD, HEAD), 1)
    ).astype(F32)
    token_ref[...] = jnp.zeros_like(token_ref)
    inside = first = after = eye
    group = lax.axis_index("ctx") // GROUP
    for i in range(GROUP):
        own = GROUP - 1 - i
        inside_ref[own] = inside
        first_ref[i] = first
        later = i > group
        after_ref[i] = jnp.where(later, after, 0.0)
        if i < GROUP - 1:
            inside = exact(halves(ab_ref[own, :, :HEAD]), halves(inside), dot_tn)
            step = halves(groups_ref[i, :, :HEAD])
            first = exact(halves(first), step, dot_nt)
            after = jnp.where(later, exact(halves(after), step, dot_nt), eye)


def hidden_kernel(qt_ref, c_ref, cot_ref, gain_ref, w_ref, z_ref, stats_ref):
    heads, n = qt_ref.shape[:2]
    squares = jnp.zeros((n, HEAD), F32)
    products = jnp.zeros((n, HEAD), F32)
    for h in range(heads):
        z = dot(qt_ref[h], low(w_ref[h])) + c_ref[h]
        z_ref[:, columns(h)] = z
        squares += z * z
        products += z * (cot_ref[:, columns(h)].astype(F32) * gain_ref[:, columns(h)])
    lane = lax.broadcasted_iota(jnp.int32, (n, HEAD), 1)
    stats_ref[...] = jnp.where(
        lane < HEAD // 2,
        jnp.sum(squares, axis=1, keepdims=True),
        jnp.sum(products, axis=1, keepdims=True),
    )


def norm_kernel(
    z_ref, cot_ref, gain_ref, own_ref, other_ref, qtt_ref,
    normed_hbm, dz_hbm, g_hbm, normed_ref, dz_ref, g_ref, sems,
):
    heads = qtt_ref.shape[0]
    width = 2 * z_ref.shape[1]
    copies = Copies(sems)
    stats = own_ref[...] + other_ref[...]
    inv = lax.rsqrt(stats[:, 0:1] / width + EPSILON)
    shift = inv * inv * inv * stats[:, HEAD // 2 : HEAD // 2 + 1] / width
    for h in range(heads):
        go = cot_ref[:, columns(h)].astype(F32) * gain_ref[:, columns(h)]
        dz = low(inv * go - z_ref[:, columns(h)] * shift)
        dz_ref[:, columns(h)] = dz
        g_ref[h] = dot(qtt_ref[h], dz)
        if h % BATCH == BATCH - 1:
            part = slice(h + 1 - BATCH, h + 1)
            copies.start(g_ref.at[part], g_hbm.at[part])
    copies.start(dz_ref, dz_hbm)
    for h in range(heads):
        normed_ref[:, columns(h)] = low(z_ref[:, columns(h)] * inv * gain_ref[:, columns(h)])
    copies.start(normed_ref, normed_hbm)
    for copy in copies.started:
        copy.wait()


def query_kernel(
    q_ref, k_ref, e_ref, tkv_ref, st_ref, w_ref, dz_ref,
    dq_ref, u_ref, dk_ref, er_ref, token_ref,
):
    n = k_ref.shape[0]
    heads = e_ref.shape[0]
    row = lax.broadcasted_iota(jnp.int32, (n, n), 0)
    col = lax.broadcasted_iota(jnp.int32, (n, n), 1)
    causal = row >= col
    token_ref[...] = jnp.zeros_like(token_ref)
    for h in range(heads):
        e = e_ref[h : h + 1, :]
        w = low(w_ref[h])
        dz = dz_ref[:, columns(h)]
        r = dot(tkv_ref[h, :, :HEAD], w) - tkv_ref[h, :, HEAD:].astype(F32)
        er = low(r * jnp.transpose(jnp.broadcast_to(e, (HEAD, n))))
        er_ref[h] = er
        ds = low(jnp.where(causal, -dot_nt(dz, er), 0.0))
        dq_ref[:, columns(h)] = low(dot_nt(dz, w) + dot(ds, k_ref[:, columns(h)]))
        dk_ref[h] = low(dot_tn(ds, q_ref[:, columns(h)]))
        u_ref[h] = low(dot_tn(st_ref[h], dz))


def transposed_map(a, later, own):
    return exact(halves(a), halves(later), dot_tn) + own


def gather_kernel(ab_ref, tree_ref, g_ref, token_ref, all_hbm, whole_ref, sems):
    pairs = [
        transposed_map(ab_ref[2 * i, :, :HEAD], g_ref[2 * i + 1], g_ref[2 * i]) for i in range(4)
    ]
    quads = [
        transposed_map(tree_ref[2 * i, :, :HEAD], pairs[2 * i + 1], pairs[2 * i])
        for i in range(2)
    ]
    whole_ref[...] = transposed_map(tree_ref[4, :, :HEAD], quads[1], quads[0])
    broadcast(Copies(sems), whole_ref, all_hbm)


def tail_kernel(ab_ref, g_ref, sums_ref):
    tail = jnp.zeros((HEAD, HEAD), F32)
    sums_ref[GROUP - 1] = tail
    for i in range(GROUP - 1, 0, -1):
        if i < GROUP - 1:
            tail = transposed_map(ab_ref[i, :, :HEAD], tail, g_ref[i])
        else:
            tail = g_ref[i]
        sums_ref[i - 1] = tail


def end_kernel(
    after_hbm, first_hbm, inside_hbm, sums_hbm, later_ref, d_ref,
    init_ref, after_ref, first_ref, inside_ref, sums_ref, sems,
):
    copies = Copies(sems)
    arrivals = [
        copies.start(source, target)
        for source, target in (
            (after_hbm, after_ref), (first_hbm, first_ref), (inside_hbm, inside_ref),
            (sums_hbm, sums_ref),
        )
    ]
    parts = [halves(later_ref[g]) for g in range(GROUP)]
    arrivals[0].wait()
    end = exact(halves(after_ref[1]), parts[1])
    for g in range(2, GROUP):
        end += exact(halves(after_ref[g]), parts[g])
    arrivals[1].wait()
    start = later_ref[0]
    for g in range(1, GROUP):
        start += exact(halves(first_ref[g]), parts[g])
    init_ref[...] = start
    ends = halves(end)
    for copy in arrivals[2:]:
        copy.wait()
    rows = init_ref[pl.ds(pl.multiple_of(lax.axis_index("ctx") // GROUP * 16, 16), 16), :]
    for i in range(GROUP):
        d = end
        if i < GROUP - 1:
            d = exact(halves(inside_ref[i]), ends) + sums_ref[i]
        d_ref[i, :HEAD, :] = d
        d_ref[i, HEAD:, :] = jnp.zeros((8, HEAD), F32)
        d_ref[i, HEAD : HEAD + 2, :] = rows[2 * i : 2 * i + 2]


def key_kernel(
    k_ref, e_ref, tek_ref, er_ref, u_ref, dkp_ref, w_ref, d_ref,
    dk_hbm, dv_hbm, de_ref, gi_ref, dk_ref, dv_ref, sems,
):
    n = k_ref.shape[0]
    heads = e_ref.shape[0]
    copies = Copies(sems)
    row = lax.broadcasted_iota(jnp.int32, (n, n), 0) // MB
    col = lax.broadcasted_iota(jnp.int32, (n, n), 1) // MB
    before = row > col
    after = row < col
    ones = jnp.ones((8, HEAD), BF16)
    for h in range(heads):
        gi_ref[h : h + 1, :HEAD] = d_ref[h, HEAD : HEAD + 1, :]
        gi_ref[h : h + 1, HEAD:] = d_ref[h, HEAD + 1 : HEAD + 2, :]
    for first in range(0, heads, BATCH):
        batch = range(first, first + BATCH)
        ds = [low(d_ref[h, :HEAD, :]) for h in batch]
        both = [jnp.concatenate([low(w_ref[h]), -d], axis=1) for h, d in zip(batch, ds)]
        ers = [er_ref[h] for h in batch]
        us = [u_ref[h].astype(F32) - dot(tek_ref[h], d) for h, d in zip(batch, ds)]
        lows = [low(u) for u in us]
        for h, u in zip(batch, lows):
            dv_ref[:, columns(h)] = -u
        flat = span(first, first + BATCH)
        copies.start(dv_ref.at[:, flat], dv_hbm.at[:, flat])
        ps = [low(u * er.astype(F32)) for u, er in zip(us, ers)]
        xs = [
            low(jnp.where(before, dot_nt(u, er), jnp.where(after, dot_nt(er, u), 0.0)))
            for u, er in zip(lows, ers)
        ]
        dks = [
            dkp_ref[h].astype(F32) + dot_nt(jnp.concatenate([u, er], axis=1), b)
            for h, u, er, b in zip(batch, lows, ers, both)
        ]
        for h, dk, x, p in zip(batch, dks, xs, ps):
            e = e_ref[h : h + 1, :]
            dk_ref[:, columns(h)] = low(dk - dot(x, k_ref[:, columns(h)]))
            de_ref[h : h + 1, :] = dot_nt(ones, p)[0:1] / (e * e)
        copies.start(dk_ref.at[:, flat], dk_hbm.at[:, flat])
    for copy in copies.started:
        copy.wait()


def local(queries, keys, values, rates, init_weight, gain, cotangent):
    n, width = keys.shape
    heads = width // HEAD
    count = lax.axis_size("ctx") // GROUP
    near = [[g * GROUP + i for i in range(GROUP)] for g in range(count)]
    far = [[g * GROUP + i for g in range(count)] for i in range(GROUP)]
    gain_row = gain.reshape(1, width)

    def swap(a, groups):
        return lax.all_to_all(a, "ctx", 0, 0, axis_index_groups=groups)

    square = (GROUP, HEAD, HEAD)
    wide = (GROUP, HEAD, 2 * HEAD)
    tall = (heads, n, HEAD)
    full = (heads, n, n)
    flat = (n, width)
    branches = (6, HEAD, 2 * HEAD)
    token = ((8, HEAD), F32, "v")
    parts = heads // BATCH
    vm = pltpu.VMEM

    half = n // 2
    inner = (heads, 2, half, half)
    corner = (heads, half, half)
    turned = (heads, HEAD, n)
    maps, inverse, cross, tkv = call(
        map_kernel,
        [
            (wide, F32, "h"), (inner, BF16, "h"), (corner, BF16, "h"),
            ((heads, n, 2 * HEAD), BF16, "h"),
        ],
        [(keys, "h"), (values, "h"), (rates, "h")],
        [
            vm(flat, BF16), vm(flat, BF16), vm((heads, n), F32),
            vm(wide, F32), vm(inner, BF16), vm(corner, BF16), vm((heads, n, 2 * HEAD), BF16),
        ],
        copies=4 + 2 * parts + heads // 2,
    )
    own_maps = swap(maps, near)
    qt, qt_turned, offset, scores, tek, own_init, prepared = call(
        prepare_kernel,
        [
            (tall, BF16, "a"), (turned, BF16, "a"), (tall, F32, "a"), (full, BF16, "a"),
            (tall, BF16, "a"), ((HEAD, HEAD), F32, "h"), token,
        ],
        [
            (queries, "a"), (keys, "a"), (rates, "a"), (inverse, "a"), (cross, "a"), (tkv, "a"),
            (init_weight, "h"),
        ],
        copies=1,
    )
    sent, tree = call(
        group_kernel,
        [(wide, F32, "v"), (branches, F32, "h")],
        [(own_maps, "v"), (prepared, "v")],
        [vm(branches, F32)],
        copies=1,
    )
    group_maps = swap(sent, far)
    (starts,) = call(
        start_kernel,
        [(square, F32, "v")],
        [(own_maps, "v"), (tree, "v"), (group_maps, "v"), (own_init, "v")],
    )
    weights = swap(starts, near)
    hidden, stats = call(
        hidden_kernel,
        [(flat, F32, "v"), ((n, HEAD), F32, "v")],
        [(qt, "v"), (offset, "v"), (cotangent, "v"), (gain_row, "v"), (weights, "v")],
    )
    other = lax.ppermute(stats, "tensor", [(0, 1), (1, 0)])
    normed, dz, local_grad = call(
        norm_kernel,
        [(flat, BF16, "h"), (flat, BF16, "h"), (square, F32, "h")],
        [
            (hidden, "v"), (cotangent, "v"), (gain_row, "v"), (stats, "v"), (other, "v"),
            (qt_turned, "v"),
        ],
        [vm(flat, BF16), vm(flat, BF16), vm(square, F32)],
        copies=2 + parts,
    )
    own_grads = swap(local_grad, near)
    grad_queries, u, dk_part, scaled_residual, queried = call(
        query_kernel,
        [(flat, BF16, "a"), (tall, BF16, "a"), (tall, BF16, "a"), (tall, BF16, "a"), token],
        [
            (queries, "a"), (keys, "a"), (rates, "a"), (tkv, "a"), (scores, "a"),
            (weights, "v"), (dz, "a"),
        ],
    )
    (sent,) = call(
        gather_kernel,
        [(square, F32, "h")],
        [(own_maps, "v"), (tree, "v"), (own_grads, "v"), (queried, "v")],
        [vm((HEAD, HEAD), F32)],
        copies=GROUP,
    )
    group_grads = swap(sent, far)
    inside, after, first = call(
        adjoint_kernel,
        [(square, F32, "a"), (square, F32, "a"), (square, F32, "a"), token],
        [(own_maps, "v"), (group_maps, "v")],
    )[:3]
    (sums,) = call(tail_kernel, [(square, F32, "a")], [(own_maps, "v"), (own_grads, "v")])
    ending = (GROUP, HEAD + 8, HEAD)
    (ends,) = call(
        end_kernel,
        [(ending, F32, "v")],
        [(after, "h"), (first, "h"), (inside, "h"), (sums, "h"), (group_grads, "v")],
        [vm((HEAD, HEAD), F32)] + [vm(square, F32)] * 4,
        copies=4,
    )
    adjoint = swap(ends, near)
    grad_keys, grad_values, grad_rates, grad_init = call(
        key_kernel,
        [(flat, BF16, "h"), (flat, BF16, "h"), ((heads, n), F32, "v"), ((heads, n), F32, "v")],
        [
            (keys, "v"), (rates, "v"), (tek, "v"), (scaled_residual, "v"), (u, "v"),
            (dk_part, "v"), (weights, "v"), (adjoint, "v"),
        ],
        [vm(flat, BF16), vm(flat, BF16)],
        copies=2 * parts,
    )
    return (normed, grad_queries, grad_keys, grad_values, grad_rates, grad_init)


def solution(mesh):
    in_specs = (
        P("ctx", "tensor"),
        P("ctx", "tensor"),
        P("ctx", "tensor"),
        P("tensor", "ctx"),
        P("tensor", None, None),
        P("tensor"),
        P("ctx", "tensor"),
    )
    out_specs = (
        P("ctx", "tensor"),
        P("ctx", "tensor"),
        P("ctx", "tensor"),
        P("ctx", "tensor"),
        P("tensor", "ctx"),
        P("tensor", "ctx"),
    )
    return jax.shard_map(local, mesh=mesh, in_specs=in_specs, out_specs=out_specs, check_vma=False)
```

```python
import jax
import jax.numpy as jnp
from jax import lax
from jax.experimental import pallas as pl
from jax.experimental.pallas import tpu as pltpu
from jax.sharding import PartitionSpec as P

HEAD = 128
MB = 16
EPSILON = 1e-06
GROUP = 8
F32 = jnp.float32
BF16 = jnp.bfloat16


def low(a):
    return a.astype(BF16)


def dot(a, b):
    return jnp.dot(a, b, preferred_element_type=F32)


def dot_nt(a, b):
    return lax.dot_general(a, b, (((1,), (1,)), ((), ())), preferred_element_type=F32)


def dot_tn(a, b):
    return lax.dot_general(a, b, (((0,), (0,)), ((), ())), preferred_element_type=F32)


def halves(a):
    high = low(a)
    return high, low(a - high.astype(F32))


def exact(a, b, product=dot):
    (ah, al), (bh, bl) = a, b
    return product(ah, bh) + (product(ah, bl) + product(al, bh))


def call(kernel, outs, args, scratch=(), copies=0, limit=24):
    spaces = {"s": pltpu.SMEM, "v": pltpu.VMEM, "h": pltpu.HBM, "a": pltpu.VMEM}
    values = [pltpu.with_memory_space_constraint(a, pltpu.HBM) if p in "ha" else a for a, p in args]
    results = [
        pltpu.HBM(shape, dtype) if p in "ha" else jax.ShapeDtypeStruct(shape, dtype)
        for shape, dtype, p in outs
    ]
    size = sum(a.size * a.dtype.itemsize for a in values)
    scratch = list(scratch)
    if copies:
        scratch.append(pltpu.SemaphoreType.DMA((copies,)))
    return pl.pallas_call(
        kernel,
        out_shape=results,
        in_specs=[pl.BlockSpec(memory_space=spaces[p]) for _, p in args],
        out_specs=[pl.BlockSpec(memory_space=spaces[p]) for _, _, p in outs],
        scratch_shapes=scratch,
        compiler_params=pltpu.CompilerParams(vmem_limit_bytes=limit * 2**20),
        cost_estimate=pl.CostEstimate(
            flops=2 * 10**9, bytes_accessed=2 * size, transcendentals=0
        ),
        name=kernel.__name__,
    )(*values)


class Copies:
    def __init__(self, semaphores):
        self.semaphores = semaphores
        self.started = []

    def start(self, source, target):
        copy = pltpu.make_async_copy(source, target, self.semaphores.at[len(self.started)])
        copy.start()
        self.started.append(copy)
        return copy


def columns(h):
    return slice(h * HEAD, (h + 1) * HEAD)


def span(first, last):
    return slice(first * HEAD, last * HEAD)


BATCH = 4


def map_kernel(
    k_hbm, v_hbm, e_hbm, ab_hbm, t_hbm, n_hbm, tkv_hbm,
    k_ref, v_ref, e_ref, ab_ref, t_ref, n_ref, tkv_ref, sems,
):
    heads = e_ref.shape[0]
    half = t_ref.shape[-1]
    copies = Copies(sems)
    arrivals = []
    for first in range(0, heads, BATCH):
        part = span(first, first + BATCH)
        key = copies.start(k_hbm.at[:, part], k_ref.at[:, part])
        if first == 0:
            rates = copies.start(e_hbm, e_ref)
        arrivals.append((key, copies.start(v_hbm.at[:, part], v_ref.at[:, part])))
    row = lax.broadcasted_iota(jnp.int32, (half, half), 0)
    col = lax.broadcasted_iota(jnp.int32, (half, half), 1)
    eye = (row == col).astype(F32)
    masks = []
    width = MB
    while width < half:
        masks.append((row // (2 * width) == col // (2 * width)) & (row // width > col // width))
        width *= 2
    sent = []
    ks, es, blocks, crosses, scaled = [], [], [], [], []
    for first, (key, _) in zip(range(0, heads, BATCH), arrivals):
        key.wait()
        if first == 0:
            rates.wait()
        for h in range(first, first + BATCH):
            k = k_ref[:, columns(h)]
            e = e_ref[h : h + 1, :]
            top = -(dot_nt(k[:half], k[:half]) * e[:, :half])
            bottom = -(dot_nt(k[half:], k) * e)
            blocks += [top, bottom[:, half:]]
            crosses.append(low(bottom[:, :half]))
            ks.append(k)
            es.append(e)
    inverses = [low(eye + jnp.where(masks[0], b, 0.0)) for b in blocks]
    for mask in masks[1:]:
        mids = [low(dot(low(jnp.where(mask, b, 0.0)), t)) for b, t in zip(blocks, inverses)]
        inverses = [t + low(dot(t, m)) for t, m in zip(inverses, mids)]
    for h in range(heads):
        t_ref[h, 0] = inverses[2 * h]
        t_ref[h, 1] = inverses[2 * h + 1]
        n_ref[h] = crosses[h]
    sent.append(copies.start(t_ref, t_hbm))
    sent.append(copies.start(n_ref, n_hbm))
    for _, value in arrivals:
        value.wait()
    kvs = [jnp.concatenate([ks[h], v_ref[:, columns(h)]], axis=1) for h in range(heads)]
    tops = [low(dot(t, kv[:half])) for t, kv in zip(inverses[::2], kvs)]
    scaled = [low(jnp.transpose(k.astype(F32)) * e) for k, e in zip(ks, es)]
    mids = [low(kv[half:].astype(F32) + dot(c, x)) for kv, c, x in zip(kvs, crosses, tops)]
    bottoms = [low(dot(t, m)) for t, m in zip(inverses[1::2], mids)]
    for h in range(heads):
        tkv_ref[h, :half] = tops[h]
        tkv_ref[h, half:] = bottoms[h]
    sent.append(copies.start(tkv_ref, tkv_hbm))
    for h in range(heads):
        ab = dot(scaled[h], tkv_ref[h])
        ab_ref[h, :, :HEAD] = eye - ab[:, :HEAD]
        ab_ref[h, :, HEAD:] = ab[:, HEAD:]
        if h % 2 == 1:
            sent.append(copies.start(ab_ref.at[h - 1 : h + 1], ab_hbm.at[h - 1 : h + 1]))
    for copy in sent:
        copy.wait()


def prepare_kernel(
    q_ref, k_ref, e_ref, t_ref, n_ref, tkv_ref, init_hbm,
    qt_ref, qtt_ref, c_ref, st_ref, tek_ref, own_hbm, token_ref, sems,
):
    initial = Copies(sems).start(init_hbm.at[lax.axis_index("ctx") % GROUP], own_hbm)
    n = k_ref.shape[0]
    half = n // 2
    heads = e_ref.shape[0]
    row = lax.broadcasted_iota(jnp.int32, (n, n), 0)
    col = lax.broadcasted_iota(jnp.int32, (n, n), 1)
    causal = row >= col
    token_ref[...] = jnp.zeros_like(token_ref)
    for h in range(heads):
        q = q_ref[:, columns(h)]
        k = k_ref[:, columns(h)]
        e = e_ref[h : h + 1, :]
        se = low(jnp.where(causal, dot_nt(q, k) * e, 0.0))
        sx = dot(se, tkv_ref[h])
        qt = q.astype(F32) - sx[:, :HEAD]
        qt_ref[h] = low(qt)
        qtt_ref[h] = low(jnp.transpose(qt))
        c_ref[h] = sx[:, HEAD:]
        top, bottom = t_ref[h, 0], t_ref[h, 1]
        cross = low(dot(bottom, low(dot(n_ref[h], top))))
        t = jnp.concatenate(
            [
                jnp.concatenate([top, jnp.zeros((half, half), BF16)], axis=1),
                jnp.concatenate([cross, bottom], axis=1),
            ],
            axis=0,
        )
        st_ref[h] = low(-dot(se, t))
        wide = jnp.transpose(jnp.broadcast_to(e, (HEAD, n)))
        tek_ref[h] = low(dot_tn(t, low(k.astype(F32) * wide)))
    initial.wait()


def compose(early, late):
    wide = exact(halves(late[:, :HEAD]), halves(early))
    return jnp.concatenate([wide[:, :HEAD], wide[:, HEAD:] + late[:, HEAD:]], axis=1)


def broadcast(copies, source, targets):
    sent = [copies.start(source, targets.at[i]) for i in range(GROUP)]
    for copy in sent:
        copy.wait()


def group_kernel(ab_ref, token_ref, all_ref, tree_hbm, tree_ref, sems):
    copies = Copies(sems)
    pairs = [compose(ab_ref[2 * i], ab_ref[2 * i + 1]) for i in range(4)]
    quads = [compose(pairs[2 * i], pairs[2 * i + 1]) for i in range(2)]
    for i, a in enumerate(pairs + quads):
        tree_ref[i] = a
    tree = copies.start(tree_ref, tree_hbm)
    whole = compose(quads[0], quads[1])
    for i in range(GROUP):
        all_ref[i] = whole
    tree.wait()


def apply_map(ab, w):
    return exact(halves(ab[:, :HEAD]), halves(w)) + ab[:, HEAD:]


def start_kernel(ab_ref, tree_ref, groups_ref, init_ref, gain_hbm, w_ref, gain_ref, sems):
    weight = Copies(sems).start(gain_hbm, gain_ref)
    group = lax.axis_index("ctx") // GROUP
    w0 = lax.fori_loop(0, group, lambda g, w: apply_map(groups_ref[g], w), init_ref[...])
    w4 = apply_map(tree_ref[4], w0)
    w2 = apply_map(tree_ref[0], w0)
    w6 = apply_map(tree_ref[2], w4)
    for i, w in zip((0, 2, 4, 6), (w0, w2, w4, w6)):
        w_ref[i] = w
        w_ref[i + 1] = apply_map(ab_ref[i], w)
    weight.wait()


def adjoint_kernel(groups_ref, after_ref, first_ref, token_ref):
    eye = (
        lax.broadcasted_iota(jnp.int32, (HEAD, HEAD), 0)
        == lax.broadcasted_iota(jnp.int32, (HEAD, HEAD), 1)
    ).astype(F32)
    token_ref[...] = jnp.zeros_like(token_ref)
    first = after = eye
    group = lax.axis_index("ctx") // GROUP
    for i in range(GROUP):
        first_ref[i] = first
        later = i > group
        after_ref[i] = jnp.where(later, after, 0.0)
        if i < GROUP - 1:
            step = halves(groups_ref[i, :, :HEAD])
            first = exact(halves(first), step, dot_nt)
            after = jnp.where(later, exact(halves(after), step, dot_nt), eye)


def hidden_kernel(qt_ref, c_ref, cot_ref, gain_ref, w_ref, z_ref, stats_ref):
    heads, n = qt_ref.shape[:2]
    squares = jnp.zeros((n, HEAD), F32)
    products = jnp.zeros((n, HEAD), F32)
    for h in range(heads):
        z = dot(qt_ref[h], low(w_ref[h])) + c_ref[h]
        z_ref[:, columns(h)] = z
        squares += z * z
        products += z * (cot_ref[:, columns(h)].astype(F32) * gain_ref[:, columns(h)])
    lane = lax.broadcasted_iota(jnp.int32, (n, HEAD), 1)
    stats_ref[...] = jnp.where(
        lane < HEAD // 2,
        jnp.sum(squares, axis=1, keepdims=True),
        jnp.sum(products, axis=1, keepdims=True),
    )


def norm_kernel(
    z_ref, cot_ref, gain_ref, own_ref, other_ref, qtt_ref,
    normed_hbm, dz_hbm, g_hbm, normed_ref, dz_ref, g_ref, sems,
):
    heads = qtt_ref.shape[0]
    width = 2 * z_ref.shape[1]
    copies = Copies(sems)
    stats = own_ref[...] + other_ref[...]
    inv = lax.rsqrt(stats[:, 0:1] / width + EPSILON)
    shift = inv * inv * inv * stats[:, HEAD // 2 : HEAD // 2 + 1] / width
    for h in range(heads):
        go = cot_ref[:, columns(h)].astype(F32) * gain_ref[:, columns(h)]
        dz = low(inv * go - z_ref[:, columns(h)] * shift)
        dz_ref[:, columns(h)] = dz
        g_ref[h] = dot(qtt_ref[h], dz)
        if h % BATCH == BATCH - 1:
            part = slice(h + 1 - BATCH, h + 1)
            copies.start(g_ref.at[part], g_hbm.at[part])
    copies.start(dz_ref, dz_hbm)
    for h in range(heads):
        normed_ref[:, columns(h)] = low(z_ref[:, columns(h)] * inv * gain_ref[:, columns(h)])
    copies.start(normed_ref, normed_hbm)
    for copy in copies.started:
        copy.wait()


def query_kernel(
    q_hbm, k_hbm, e_hbm, tkv_hbm, st_hbm, dz_hbm, w_ref,
    dq_hbm, u_hbm, dk_hbm, er_hbm, token_ref,
    q_ref, k_ref, e_ref, tkv_ref, st_ref, dz_ref, dq_ref, u_ref, dk_ref, er_ref, sems,
):
    n = k_ref.shape[0]
    heads = e_ref.shape[0]
    copies = Copies(sems)
    rates = copies.start(e_hbm, e_ref)
    arrivals = []
    for first in range(0, heads, BATCH):
        part = slice(first, first + BATCH)
        flat = span(first, first + BATCH)
        arrivals.append((
            copies.start(tkv_hbm.at[part], tkv_ref.at[part]),
            copies.start(dz_hbm.at[:, flat], dz_ref.at[:, flat]),
            copies.start(k_hbm.at[:, flat], k_ref.at[:, flat]),
            copies.start(q_hbm.at[:, flat], q_ref.at[:, flat]),
            copies.start(st_hbm.at[part], st_ref.at[part]),
        ))
    row = lax.broadcasted_iota(jnp.int32, (n, n), 0)
    col = lax.broadcasted_iota(jnp.int32, (n, n), 1)
    causal = row >= col
    token_ref[...] = jnp.zeros_like(token_ref)
    rates.wait()
    sent = []
    for first, arrival in zip(range(0, heads, BATCH), arrivals):
        batch = range(first, first + BATCH)
        ws = [low(w_ref[h]) for h in batch]
        rates_wide = [
            jnp.transpose(jnp.broadcast_to(e_ref[h : h + 1, :], (HEAD, n))) for h in batch
        ]
        for copy in arrival:
            copy.wait()
        for h, w, wide in zip(batch, ws, rates_wide):
            r = dot(tkv_ref[h, :, :HEAD], w) - tkv_ref[h, :, HEAD:].astype(F32)
            er_ref[h] = low(r * wide)
        dss = [
            low(jnp.where(causal, -dot_nt(dz_ref[:, columns(h)], er_ref[h]), 0.0)) for h in batch
        ]
        for h, w, ds in zip(batch, ws, dss):
            dq_ref[:, columns(h)] = low(
                dot_nt(dz_ref[:, columns(h)], w) + dot(ds, k_ref[:, columns(h)])
            )
            dk_ref[h] = low(dot_tn(ds, q_ref[:, columns(h)]))
            u_ref[h] = low(dot_tn(st_ref[h], dz_ref[:, columns(h)]))
        part = slice(first, first + BATCH)
        flat = span(first, first + BATCH)
        sent.append(copies.start(dq_ref.at[:, flat], dq_hbm.at[:, flat]))
        for source, target in ((u_ref, u_hbm), (dk_ref, dk_hbm), (er_ref, er_hbm)):
            sent.append(copies.start(source.at[part], target.at[part]))
    for copy in sent:
        copy.wait()


def transposed_map(a, later, own):
    return exact(halves(a), halves(later), dot_tn) + own


def gather_kernel(
    ab_ref, tree_hbm, g_ref, query_token, adjoint_token, all_ref, sums_ref, tree_ref, sems
):
    tree = Copies(sems).start(tree_hbm.at[:, :, :HEAD], tree_ref)
    pairs = [
        transposed_map(ab_ref[2 * i, :, :HEAD], g_ref[2 * i + 1], g_ref[2 * i]) for i in range(4)
    ]
    tree.wait()
    quads = [transposed_map(tree_ref[2 * i], pairs[2 * i + 1], pairs[2 * i]) for i in range(2)]
    for i, a in enumerate(pairs + quads):
        sums_ref[i] = a
    whole = transposed_map(tree_ref[4], quads[1], quads[0])
    for i in range(GROUP):
        all_ref[i] = whole


def end_kernel(
    after_ref, first_ref, ab_ref, tree_ref, g_ref, sums_ref, later_ref, d_ref, init_ref
):
    parts = [halves(later_ref[g]) for g in range(GROUP)]
    d7 = exact(halves(after_ref[1]), parts[1])
    for g in range(2, GROUP):
        d7 += exact(halves(after_ref[g]), parts[g])
    d3 = transposed_map(tree_ref[5, :, :HEAD], d7, sums_ref[5])
    d5 = transposed_map(tree_ref[3, :, :HEAD], d7, sums_ref[3])
    d1 = transposed_map(tree_ref[1, :, :HEAD], d3, sums_ref[1])
    start = later_ref[0]
    for g in range(1, GROUP):
        start += exact(halves(first_ref[g]), parts[g])
    init_ref[...] = start
    rows = init_ref[pl.ds(pl.multiple_of(lax.axis_index("ctx") // GROUP * 16, 16), 16), :]
    for i, d in zip((7, 5, 3, 1), (d7, d5, d3, d1)):
        d_ref[i, :HEAD, :] = d
        d_ref[i - 1, :HEAD, :] = transposed_map(ab_ref[i, :, :HEAD], d, g_ref[i])
    for i in range(GROUP):
        d_ref[i, HEAD:, :] = jnp.zeros((8, HEAD), F32)
        d_ref[i, HEAD : HEAD + 2, :] = rows[2 * i : 2 * i + 2]


def key_kernel(
    k_ref, e_ref, tek_ref, er_ref, u_ref, dkp_ref, w_ref, d_ref,
    dk_hbm, dv_hbm, de_ref, gi_ref, dk_ref, dv_ref, sems,
):
    n = k_ref.shape[0]
    heads = e_ref.shape[0]
    copies = Copies(sems)
    row = lax.broadcasted_iota(jnp.int32, (n, n), 0) // MB
    col = lax.broadcasted_iota(jnp.int32, (n, n), 1) // MB
    before = row > col
    after = row < col
    ones = jnp.ones((8, HEAD), BF16)
    for h in range(heads):
        gi_ref[h : h + 1, :HEAD] = d_ref[h, HEAD : HEAD + 1, :]
        gi_ref[h : h + 1, HEAD:] = d_ref[h, HEAD + 1 : HEAD + 2, :]
    for first in range(0, heads, BATCH):
        batch = range(first, first + BATCH)
        ds = [low(d_ref[h, :HEAD, :]) for h in batch]
        both = [jnp.concatenate([low(w_ref[h]), -d], axis=1) for h, d in zip(batch, ds)]
        ers = [er_ref[h] for h in batch]
        us = [u_ref[h].astype(F32) - dot(tek_ref[h], d) for h, d in zip(batch, ds)]
        lows = [low(u) for u in us]
        for h, u in zip(batch, lows):
            dv_ref[:, columns(h)] = -u
        flat = span(first, first + BATCH)
        copies.start(dv_ref.at[:, flat], dv_hbm.at[:, flat])
        ps = [low(u * er.astype(F32)) for u, er in zip(us, ers)]
        xs = [
            low(jnp.where(before, dot_nt(u, er), jnp.where(after, dot_nt(er, u), 0.0)))
            for u, er in zip(lows, ers)
        ]
        dks = [
            dkp_ref[h].astype(F32) + dot_nt(jnp.concatenate([u, er], axis=1), b)
            for h, u, er, b in zip(batch, lows, ers, both)
        ]
        for h, dk, x, p in zip(batch, dks, xs, ps):
            e = e_ref[h : h + 1, :]
            dk_ref[:, columns(h)] = low(dk - dot(x, k_ref[:, columns(h)]))
            de_ref[h : h + 1, :] = dot_nt(ones, p)[0:1] / (e * e)
        copies.start(dk_ref.at[:, flat], dk_hbm.at[:, flat])
    for copy in copies.started:
        copy.wait()


def local(queries, keys, values, rates, init_weight, gain, cotangent):
    n, width = keys.shape
    heads = width // HEAD
    count = lax.axis_size("ctx") // GROUP
    near = [[g * GROUP + i for i in range(GROUP)] for g in range(count)]
    far = [[g * GROUP + i for g in range(count)] for i in range(GROUP)]
    gain_row = gain.reshape(1, width)

    def swap(a, groups):
        return lax.all_to_all(a, "ctx", 0, 0, axis_index_groups=groups)

    square = (GROUP, HEAD, HEAD)
    wide = (GROUP, HEAD, 2 * HEAD)
    tall = (heads, n, HEAD)
    full = (heads, n, n)
    flat = (n, width)
    branches = (6, HEAD, 2 * HEAD)
    token = ((8, HEAD), F32, "v")
    parts = heads // BATCH
    vm = pltpu.VMEM

    half = n // 2
    inner = (heads, 2, half, half)
    corner = (heads, half, half)
    turned = (heads, HEAD, n)
    maps, inverse, cross, tkv = call(
        map_kernel,
        [
            (wide, F32, "h"), (inner, BF16, "h"), (corner, BF16, "h"),
            ((heads, n, 2 * HEAD), BF16, "h"),
        ],
        [(keys, "h"), (values, "h"), (rates, "h")],
        [
            vm(flat, BF16), vm(flat, BF16), vm((heads, n), F32),
            vm(wide, F32), vm(inner, BF16), vm(corner, BF16), vm((heads, n, 2 * HEAD), BF16),
        ],
        copies=4 + 2 * parts + heads // 2,
    )
    own_maps = swap(maps, near)
    qt, qt_turned, offset, scores, tek, own_init, prepared = call(
        prepare_kernel,
        [
            (tall, BF16, "a"), (turned, BF16, "a"), (tall, F32, "a"), (full, BF16, "a"),
            (tall, BF16, "a"), ((HEAD, HEAD), F32, "h"), token,
        ],
        [
            (queries, "a"), (keys, "a"), (rates, "a"), (inverse, "a"), (cross, "a"), (tkv, "a"),
            (init_weight, "h"),
        ],
        copies=1,
    )
    sent, tree = call(
        group_kernel,
        [(wide, F32, "v"), (branches, F32, "h")],
        [(own_maps, "v"), (prepared, "v")],
        [vm(branches, F32)],
        copies=1,
    )
    group_maps = swap(sent, far)
    starts, gain_row = call(
        start_kernel,
        [(square, F32, "v"), ((1, width), F32, "v")],
        [(own_maps, "v"), (tree, "v"), (group_maps, "v"), (own_init, "v"), (gain_row, "h")],
        copies=1,
    )
    weights = swap(starts, near)
    hidden, stats = call(
        hidden_kernel,
        [(flat, F32, "v"), ((n, HEAD), F32, "v")],
        [(qt, "v"), (offset, "v"), (cotangent, "v"), (gain_row, "v"), (weights, "v")],
    )
    other = lax.ppermute(stats, "tensor", [(0, 1), (1, 0)])
    normed, dz, local_grad = call(
        norm_kernel,
        [(flat, BF16, "h"), (flat, BF16, "h"), (square, F32, "h")],
        [
            (hidden, "v"), (cotangent, "v"), (gain_row, "v"), (stats, "v"), (other, "v"),
            (qt_turned, "v"),
        ],
        [vm(flat, BF16), vm(flat, BF16), vm(square, F32)],
        copies=2 + parts,
    )
    own_grads = swap(local_grad, near)
    pair = (heads, n, 2 * HEAD)
    grad_queries, u, dk_part, scaled_residual, queried = call(
        query_kernel,
        [(flat, BF16, "h"), (tall, BF16, "h"), (tall, BF16, "h"), (tall, BF16, "h"), token],
        [
            (queries, "h"), (keys, "h"), (rates, "h"), (tkv, "h"), (scores, "h"), (dz, "h"),
            (weights, "v"),
        ],
        [
            vm(flat, BF16), vm(flat, BF16), vm((heads, n), F32), vm(pair, BF16), vm(full, BF16),
            vm(flat, BF16), vm(flat, BF16), vm(tall, BF16), vm(tall, BF16), vm(tall, BF16),
        ],
        copies=1 + 9 * parts,
    )
    after, first, adjoint_ready = call(
        adjoint_kernel, [(square, F32, "a"), (square, F32, "a"), token], [(group_maps, "v")]
    )
    sent, sums = call(
        gather_kernel,
        [(square, F32, "v"), ((6, HEAD, HEAD), F32, "v")],
        [(own_maps, "v"), (tree, "h"), (own_grads, "v"), (queried, "v"), (adjoint_ready, "v")],
        [vm((6, HEAD, HEAD), F32)],
        copies=1,
    )
    group_grads = swap(sent, far)
    (ends,) = call(
        end_kernel,
        [((GROUP, HEAD + 8, HEAD), F32, "v")],
        [
            (after, "v"), (first, "v"), (own_maps, "v"), (tree, "v"), (own_grads, "v"),
            (sums, "v"), (group_grads, "v"),
        ],
        [vm((HEAD, HEAD), F32)],
    )
    adjoint = swap(ends, near)
    grad_keys, grad_values, grad_rates, grad_init = call(
        key_kernel,
        [(flat, BF16, "h"), (flat, BF16, "h"), ((heads, n), F32, "v"), ((heads, n), F32, "v")],
        [
            (keys, "v"), (rates, "v"), (tek, "v"), (scaled_residual, "v"), (u, "v"),
            (dk_part, "v"), (weights, "v"), (adjoint, "v"),
        ],
        [vm(flat, BF16), vm(flat, BF16)],
        copies=2 * parts,
    )
    return (normed, grad_queries, grad_keys, grad_values, grad_rates, grad_init)


def solution(mesh):
    in_specs = (
        P("ctx", "tensor"),
        P("ctx", "tensor"),
        P("ctx", "tensor"),
        P("tensor", "ctx"),
        P("tensor", None, None),
        P("tensor"),
        P("ctx", "tensor"),
    )
    out_specs = (
        P("ctx", "tensor"),
        P("ctx", "tensor"),
        P("ctx", "tensor"),
        P("ctx", "tensor"),
        P("tensor", "ctx"),
        P("tensor", "ctx"),
    )
    return jax.shard_map(local, mesh=mesh, in_specs=in_specs, out_specs=out_specs, check_vma=False)
```

```python
import jax
import jax.numpy as jnp
from jax import lax
from jax.experimental import pallas as pl
from jax.experimental.pallas import tpu as pltpu
from jax.sharding import PartitionSpec as P

HEAD = 128
MB = 16
EPSILON = 1e-06
GROUP = 8
PLANES = 4
F32 = jnp.float32
BF16 = jnp.bfloat16


def low(a):
    return a.astype(BF16)


def dot(a, b):
    return jnp.dot(a, b, preferred_element_type=F32)


def dot_nt(a, b):
    return lax.dot_general(a, b, (((1,), (1,)), ((), ())), preferred_element_type=F32)


def dot_tn(a, b):
    return lax.dot_general(a, b, (((0,), (0,)), ((), ())), preferred_element_type=F32)


def halves(a):
    high = low(a)
    return high, low(a - high.astype(F32))


def exact(a, b, product=dot):
    (ah, al), (bh, bl) = a, b
    return product(ah, bh) + (product(ah, bl) + product(al, bh))


def call(kernel, outs, args, scratch=(), copies=0, limit=24):
    spaces = {"s": pltpu.SMEM, "v": pltpu.VMEM, "h": pltpu.HBM, "a": pltpu.VMEM}
    values = [pltpu.with_memory_space_constraint(a, pltpu.HBM) if p in "ha" else a for a, p in args]
    results = [
        pltpu.HBM(shape, dtype) if p in "ha" else jax.ShapeDtypeStruct(shape, dtype)
        for shape, dtype, p in outs
    ]
    size = sum(a.size * a.dtype.itemsize for a in values)
    scratch = list(scratch)
    if copies:
        scratch.append(pltpu.SemaphoreType.DMA((copies,)))
    return pl.pallas_call(
        kernel,
        out_shape=results,
        in_specs=[pl.BlockSpec(memory_space=spaces[p]) for _, p in args],
        out_specs=[pl.BlockSpec(memory_space=spaces[p]) for _, _, p in outs],
        scratch_shapes=scratch,
        compiler_params=pltpu.CompilerParams(vmem_limit_bytes=limit * 2**20),
        cost_estimate=pl.CostEstimate(
            flops=2 * 10**9, bytes_accessed=2 * size, transcendentals=0
        ),
        name=kernel.__name__,
    )(*values)


class Copies:
    def __init__(self, semaphores):
        self.semaphores = semaphores
        self.started = []

    def start(self, source, target):
        copy = pltpu.make_async_copy(source, target, self.semaphores.at[len(self.started)])
        copy.start()
        self.started.append(copy)
        return copy


def columns(h):
    return slice(h * HEAD, (h + 1) * HEAD)


def span(first, last):
    return slice(first * HEAD, last * HEAD)


BATCH = 4


def map_kernel(
    k_hbm, v_hbm, e_hbm, ab_hbm, t_hbm, n_hbm, tkv_hbm,
    k_ref, v_ref, e_ref, ab_ref, t_ref, n_ref, tkv_ref, sems,
):
    heads = e_ref.shape[0]
    half = t_ref.shape[-1]
    copies = Copies(sems)
    arrivals = []
    for first in range(0, heads, BATCH):
        part = span(first, first + BATCH)
        key = copies.start(k_hbm.at[:, part], k_ref.at[:, part])
        if first == 0:
            rates = copies.start(e_hbm, e_ref)
        arrivals.append((key, copies.start(v_hbm.at[:, part], v_ref.at[:, part])))
    row = lax.broadcasted_iota(jnp.int32, (half, half), 0)
    col = lax.broadcasted_iota(jnp.int32, (half, half), 1)
    eye = (row == col).astype(F32)
    masks = []
    width = MB
    while width < half:
        masks.append((row // (2 * width) == col // (2 * width)) & (row // width > col // width))
        width *= 2
    sent = []
    ks, es, blocks, crosses, scaled = [], [], [], [], []
    for first, (key, _) in zip(range(0, heads, BATCH), arrivals):
        key.wait()
        if first == 0:
            rates.wait()
        for h in range(first, first + BATCH):
            k = k_ref[:, columns(h)]
            e = e_ref[h : h + 1, :]
            top = -(dot_nt(k[:half], k[:half]) * e[:, :half])
            bottom = -(dot_nt(k[half:], k) * e)
            blocks += [top, bottom[:, half:]]
            crosses.append(low(bottom[:, :half]))
            ks.append(k)
            es.append(e)
    inverses = [low(eye + jnp.where(masks[0], b, 0.0)) for b in blocks]
    for mask in masks[1:]:
        mids = [low(dot(low(jnp.where(mask, b, 0.0)), t)) for b, t in zip(blocks, inverses)]
        inverses = [t + low(dot(t, m)) for t, m in zip(inverses, mids)]
    for h in range(heads):
        t_ref[h, 0] = inverses[2 * h]
        t_ref[h, 1] = inverses[2 * h + 1]
        n_ref[h] = crosses[h]
    sent.append(copies.start(t_ref, t_hbm))
    sent.append(copies.start(n_ref, n_hbm))
    for _, value in arrivals:
        value.wait()
    kvs = [jnp.concatenate([ks[h], v_ref[:, columns(h)]], axis=1) for h in range(heads)]
    tops = [low(dot(t, kv[:half])) for t, kv in zip(inverses[::2], kvs)]
    scaled = [low(jnp.transpose(k.astype(F32)) * e) for k, e in zip(ks, es)]
    mids = [low(kv[half:].astype(F32) + dot(c, x)) for kv, c, x in zip(kvs, crosses, tops)]
    bottoms = [low(dot(t, m)) for t, m in zip(inverses[1::2], mids)]
    for h in range(heads):
        tkv_ref[h, :half] = tops[h]
        tkv_ref[h, half:] = bottoms[h]
    sent.append(copies.start(tkv_ref, tkv_hbm))
    for h in range(heads):
        ab = dot(scaled[h], tkv_ref[h])
        ab_ref[h, :, :HEAD] = eye - ab[:, :HEAD]
        ab_ref[h, :, HEAD:] = ab[:, HEAD:]
        if h % 2 == 1:
            sent.append(copies.start(ab_ref.at[h - 1 : h + 1], ab_hbm.at[h - 1 : h + 1]))
    for copy in sent:
        copy.wait()


def prepare_kernel(
    q_ref, k_ref, e_ref, t_ref, n_ref, tkv_ref, init_hbm,
    qt_ref, qtt_ref, c_ref, st_ref, tek_ref, own_hbm, token_ref, sems,
):
    initial = Copies(sems).start(init_hbm.at[lax.axis_index("ctx") % GROUP], own_hbm)
    n = k_ref.shape[0]
    half = n // 2
    heads = e_ref.shape[0]
    row = lax.broadcasted_iota(jnp.int32, (n, n), 0)
    col = lax.broadcasted_iota(jnp.int32, (n, n), 1)
    causal = row >= col
    token_ref[...] = jnp.zeros_like(token_ref)
    for h in range(heads):
        q = q_ref[:, columns(h)]
        k = k_ref[:, columns(h)]
        e = e_ref[h : h + 1, :]
        se = low(jnp.where(causal, dot_nt(q, k) * e, 0.0))
        sx = dot(se, tkv_ref[h])
        qt = q.astype(F32) - sx[:, :HEAD]
        qt_ref[h] = low(qt)
        qtt_ref[h] = low(jnp.transpose(qt))
        c_ref[h] = sx[:, HEAD:]
        top, bottom = t_ref[h, 0], t_ref[h, 1]
        cross = low(dot(bottom, low(dot(n_ref[h], top))))
        t = jnp.concatenate(
            [
                jnp.concatenate([top, jnp.zeros((half, half), BF16)], axis=1),
                jnp.concatenate([cross, bottom], axis=1),
            ],
            axis=0,
        )
        st_ref[h] = low(-dot(se, t))
        wide = jnp.transpose(jnp.broadcast_to(e, (HEAD, n)))
        tek_ref[h] = low(dot_tn(t, low(k.astype(F32) * wide)))
    initial.wait()


def compose(early, late):
    wide = exact(halves(late[:, :HEAD]), halves(early))
    return jnp.concatenate([wide[:, :HEAD], wide[:, HEAD:] + late[:, HEAD:]], axis=1)


def broadcast(copies, source, targets):
    sent = [copies.start(source, targets.at[i]) for i in range(GROUP)]
    for copy in sent:
        copy.wait()


def level():
    group = lax.axis_index("ctx") // GROUP
    return group // 2, group % 2


def group_kernel(ab_ref, token_ref, whole_ref, tree_hbm, tree_ref, sems):
    copies = Copies(sems)
    pairs = [compose(ab_ref[2 * i], ab_ref[2 * i + 1]) for i in range(4)]
    quads = [compose(pairs[2 * i], pairs[2 * i + 1]) for i in range(2)]
    for i, a in enumerate(pairs + quads):
        tree_ref[i] = a
    tree = copies.start(tree_ref, tree_hbm)
    whole_ref[...] = compose(quads[0], quads[1])
    tree.wait()


def pair_kernel(own_ref, other_ref, all_ref):
    _, late = level()
    own, other = own_ref[...], other_ref[...]
    early = jnp.where(late == 1, other, own)
    pair = compose(early, jnp.where(late == 1, own, other))
    for i in range(PLANES):
        all_ref[i] = pair


def apply_map(ab, w):
    return exact(halves(ab[:, :HEAD]), halves(w)) + ab[:, HEAD:]


def start_kernel(
    ab_ref, tree_ref, pairs_ref, other_ref, init_ref, gain_hbm, w_ref, gain_ref, sems
):
    weight = Copies(sems).start(gain_hbm, gain_ref)
    plane, late = level()
    w0 = lax.fori_loop(0, plane, lambda z, w: apply_map(pairs_ref[z], w), init_ref[...])
    w0 = lax.fori_loop(0, late, lambda _, w: apply_map(other_ref[...], w), w0)
    w4 = apply_map(tree_ref[4], w0)
    w2 = apply_map(tree_ref[0], w0)
    w6 = apply_map(tree_ref[2], w4)
    for i, w in zip((0, 2, 4, 6), (w0, w2, w4, w6)):
        w_ref[i] = w
        w_ref[i + 1] = apply_map(ab_ref[i], w)
    weight.wait()


def adjoint_kernel(
    pairs_ref, ab_ref, tree_ref, other_ref, after_ref, first_ref, early_ref, up_ref
):
    eye = (
        lax.broadcasted_iota(jnp.int32, (HEAD, HEAD), 0)
        == lax.broadcasted_iota(jnp.int32, (HEAD, HEAD), 1)
    ).astype(F32)
    first = after = eye
    plane, late = level()
    own = exact(halves(tree_ref[5, :, :HEAD]), halves(tree_ref[4, :, :HEAD]))
    early_ref[...] = jnp.transpose(jnp.where(late == 1, other_ref[:, :HEAD], own))
    for i in range(4):
        up_ref[i] = jnp.transpose(ab_ref[2 * i, :, :HEAD])
    for i, a in enumerate((0, 2, 4)):
        up_ref[4 + i] = jnp.transpose(tree_ref[a, :, :HEAD])
    for z in range(PLANES):
        first_ref[z] = first
        later = z > plane
        after_ref[z] = jnp.where(later, after, 0.0)
        if z < PLANES - 1:
            step = halves(pairs_ref[z, :, :HEAD])
            first = exact(halves(first), step, dot_nt)
            after = jnp.where(later, exact(halves(after), step, dot_nt), eye)


def hidden_kernel(qt_ref, c_ref, cot_ref, gain_ref, w_ref, z_ref, stats_ref):
    heads, n = qt_ref.shape[:2]
    squares = jnp.zeros((n, HEAD), F32)
    products = jnp.zeros((n, HEAD), F32)
    for h in range(heads):
        z = dot(qt_ref[h], low(w_ref[h])) + c_ref[h]
        z_ref[:, columns(h)] = z
        squares += z * z
        products += z * (cot_ref[:, columns(h)].astype(F32) * gain_ref[:, columns(h)])
    lane = lax.broadcasted_iota(jnp.int32, (n, HEAD), 1)
    stats_ref[...] = jnp.where(
        lane < HEAD // 2,
        jnp.sum(squares, axis=1, keepdims=True),
        jnp.sum(products, axis=1, keepdims=True),
    )


def norm_kernel(
    z_ref, cot_ref, gain_ref, own_ref, other_ref, qtt_ref,
    normed_hbm, dz_hbm, g_hbm, normed_ref, dz_ref, g_ref, sems,
):
    heads = qtt_ref.shape[0]
    width = 2 * z_ref.shape[1]
    copies = Copies(sems)
    stats = own_ref[...] + other_ref[...]
    inv = lax.rsqrt(stats[:, 0:1] / width + EPSILON)
    shift = inv * inv * inv * stats[:, HEAD // 2 : HEAD // 2 + 1] / width
    for h in range(heads):
        go = cot_ref[:, columns(h)].astype(F32) * gain_ref[:, columns(h)]
        dz = low(inv * go - z_ref[:, columns(h)] * shift)
        dz_ref[:, columns(h)] = dz
        g_ref[h] = dot(qtt_ref[h], dz)
        if h % BATCH == BATCH - 1:
            part = slice(h + 1 - BATCH, h + 1)
            copies.start(g_ref.at[part], g_hbm.at[part])
    copies.start(dz_ref, dz_hbm)
    for h in range(heads):
        normed_ref[:, columns(h)] = low(z_ref[:, columns(h)] * inv * gain_ref[:, columns(h)])
    copies.start(normed_ref, normed_hbm)
    for copy in copies.started:
        copy.wait()


def query_kernel(
    q_hbm, k_hbm, e_hbm, tkv_hbm, st_hbm, dz_hbm, w_ref,
    dq_hbm, u_hbm, dk_hbm, er_hbm, token_ref,
    q_ref, k_ref, e_ref, tkv_ref, st_ref, dz_ref, dq_ref, u_ref, dk_ref, er_ref, sems,
):
    n = k_ref.shape[0]
    heads = e_ref.shape[0]
    copies = Copies(sems)
    rates = copies.start(e_hbm, e_ref)
    arrivals = []
    for first in range(0, heads, BATCH):
        part = slice(first, first + BATCH)
        flat = span(first, first + BATCH)
        arrivals.append((
            copies.start(tkv_hbm.at[part], tkv_ref.at[part]),
            copies.start(dz_hbm.at[:, flat], dz_ref.at[:, flat]),
            copies.start(k_hbm.at[:, flat], k_ref.at[:, flat]),
            copies.start(q_hbm.at[:, flat], q_ref.at[:, flat]),
            copies.start(st_hbm.at[part], st_ref.at[part]),
        ))
    row = lax.broadcasted_iota(jnp.int32, (n, n), 0)
    col = lax.broadcasted_iota(jnp.int32, (n, n), 1)
    causal = row >= col
    token_ref[...] = jnp.zeros_like(token_ref)
    rates.wait()
    sent = []
    for first, arrival in zip(range(0, heads, BATCH), arrivals):
        batch = range(first, first + BATCH)
        ws = [low(w_ref[h]) for h in batch]
        rates_wide = [
            jnp.transpose(jnp.broadcast_to(e_ref[h : h + 1, :], (HEAD, n))) for h in batch
        ]
        for copy in arrival:
            copy.wait()
        for h, w, wide in zip(batch, ws, rates_wide):
            r = dot(tkv_ref[h, :, :HEAD], w) - tkv_ref[h, :, HEAD:].astype(F32)
            er_ref[h] = low(r * wide)
        dss = [
            low(jnp.where(causal, -dot_nt(dz_ref[:, columns(h)], er_ref[h]), 0.0)) for h in batch
        ]
        for h, w, ds in zip(batch, ws, dss):
            dq_ref[:, columns(h)] = low(
                dot_nt(dz_ref[:, columns(h)], w) + dot(ds, k_ref[:, columns(h)])
            )
            dk_ref[h] = low(dot_tn(ds, q_ref[:, columns(h)]))
            u_ref[h] = low(dot_tn(st_ref[h], dz_ref[:, columns(h)]))
        part = slice(first, first + BATCH)
        flat = span(first, first + BATCH)
        sent.append(copies.start(dq_ref.at[:, flat], dq_hbm.at[:, flat]))
        for source, target in ((u_ref, u_hbm), (dk_ref, dk_hbm), (er_ref, er_hbm)):
            sent.append(copies.start(source.at[part], target.at[part]))
    for copy in sent:
        copy.wait()


def transposed_map(a, later, own):
    return exact(halves(a), halves(later), dot_tn) + own


def turned_map(a, later, own):
    return exact(halves(a), halves(later)) + own


def gather_kernel(up_ref, g_ref, token_ref, whole_ref, sums_ref):
    pairs = [turned_map(up_ref[i], g_ref[2 * i + 1], g_ref[2 * i]) for i in range(4)]
    quads = [turned_map(up_ref[4 + i], pairs[2 * i + 1], pairs[2 * i]) for i in range(2)]
    for i, a in enumerate(pairs + quads):
        sums_ref[i] = a
    whole_ref[...] = turned_map(up_ref[6], quads[1], quads[0])


def pair_gradient_kernel(early_ref, own_ref, other_ref, all_ref):
    _, late = level()
    own, other = own_ref[...], other_ref[...]
    pair = turned_map(
        early_ref[...], jnp.where(late == 1, own, other), jnp.where(late == 1, other, own)
    )
    for i in range(PLANES):
        all_ref[i] = pair


def end_kernel(
    after_ref, first_ref, ab_ref, tree_ref, g_ref, sums_ref, other_map_ref, other_ref, later_ref,
    d_ref, init_ref,
):
    parts = [halves(later_ref[z]) for z in range(PLANES)]
    _, late = level()
    end = exact(halves(after_ref[1]), parts[1])
    for z in range(2, PLANES):
        end += exact(halves(after_ref[z]), parts[z])
    inner = transposed_map(other_map_ref[:, :HEAD], end, other_ref[...])
    d7 = jnp.where(late == 1, end, inner)
    d3 = transposed_map(tree_ref[5, :, :HEAD], d7, sums_ref[5])
    d5 = transposed_map(tree_ref[3, :, :HEAD], d7, sums_ref[3])
    d1 = transposed_map(tree_ref[1, :, :HEAD], d3, sums_ref[1])
    start = later_ref[0]
    for z in range(1, PLANES):
        start += exact(halves(first_ref[z]), parts[z])
    init_ref[...] = start
    rows = init_ref[pl.ds(pl.multiple_of(lax.axis_index("ctx") // GROUP * 16, 16), 16), :]
    for i, d in zip((7, 5, 3, 1), (d7, d5, d3, d1)):
        d_ref[i, :HEAD, :] = d
        d_ref[i - 1, :HEAD, :] = transposed_map(ab_ref[i, :, :HEAD], d, g_ref[i])
    for i in range(GROUP):
        d_ref[i, HEAD:, :] = jnp.zeros((8, HEAD), F32)
        d_ref[i, HEAD : HEAD + 2, :] = rows[2 * i : 2 * i + 2]


def key_kernel(
    k_ref, e_ref, tek_ref, er_ref, u_ref, dkp_ref, w_ref, d_ref,
    dk_hbm, dv_hbm, de_ref, gi_ref, dk_ref, dv_ref, sems,
):
    n = k_ref.shape[0]
    heads = e_ref.shape[0]
    copies = Copies(sems)
    row = lax.broadcasted_iota(jnp.int32, (n, n), 0) // MB
    col = lax.broadcasted_iota(jnp.int32, (n, n), 1) // MB
    before = row > col
    after = row < col
    ones = jnp.ones((8, HEAD), BF16)
    for h in range(heads):
        gi_ref[h : h + 1, :HEAD] = d_ref[h, HEAD : HEAD + 1, :]
        gi_ref[h : h + 1, HEAD:] = d_ref[h, HEAD + 1 : HEAD + 2, :]
    for first in range(0, heads, BATCH):
        batch = range(first, first + BATCH)
        ds = [low(d_ref[h, :HEAD, :]) for h in batch]
        both = [jnp.concatenate([low(w_ref[h]), -d], axis=1) for h, d in zip(batch, ds)]
        ers = [er_ref[h] for h in batch]
        us = [u_ref[h].astype(F32) - dot(tek_ref[h], d) for h, d in zip(batch, ds)]
        lows = [low(u) for u in us]
        for h, u in zip(batch, lows):
            dv_ref[:, columns(h)] = -u
        flat = span(first, first + BATCH)
        copies.start(dv_ref.at[:, flat], dv_hbm.at[:, flat])
        ps = [low(u * er.astype(F32)) for u, er in zip(us, ers)]
        xs = [
            low(jnp.where(before, dot_nt(u, er), jnp.where(after, dot_nt(er, u), 0.0)))
            for u, er in zip(lows, ers)
        ]
        dks = [
            dkp_ref[h].astype(F32) + dot_nt(jnp.concatenate([u, er], axis=1), b)
            for h, u, er, b in zip(batch, lows, ers, both)
        ]
        for h, dk, x, p in zip(batch, dks, xs, ps):
            e = e_ref[h : h + 1, :]
            dk_ref[:, columns(h)] = low(dk - dot(x, k_ref[:, columns(h)]))
            de_ref[h : h + 1, :] = dot_nt(ones, p)[0:1] / (e * e)
        copies.start(dk_ref.at[:, flat], dk_hbm.at[:, flat])
    for copy in copies.started:
        copy.wait()


def local(queries, keys, values, rates, init_weight, gain, cotangent):
    n, width = keys.shape
    heads = width // HEAD
    count = lax.axis_size("ctx") // GROUP
    near = [[g * GROUP + i for i in range(GROUP)] for g in range(count)]
    stride = 2 * GROUP
    far = [[z * stride + i for z in range(PLANES)] for i in range(stride)]
    across = [(i, i + GROUP if i % stride < GROUP else i - GROUP) for i in range(count * GROUP)]
    gain_row = gain.reshape(1, width)

    def swap(a, groups):
        return lax.all_to_all(a, "ctx", 0, 0, axis_index_groups=groups)

    square = (GROUP, HEAD, HEAD)
    wide = (GROUP, HEAD, 2 * HEAD)
    tall = (heads, n, HEAD)
    full = (heads, n, n)
    flat = (n, width)
    branches = (6, HEAD, 2 * HEAD)
    token = ((8, HEAD), F32, "v")
    parts = heads // BATCH
    vm = pltpu.VMEM

    half = n // 2
    inner = (heads, 2, half, half)
    corner = (heads, half, half)
    turned = (heads, HEAD, n)
    maps, inverse, cross, tkv = call(
        map_kernel,
        [
            (wide, F32, "h"), (inner, BF16, "h"), (corner, BF16, "h"),
            ((heads, n, 2 * HEAD), BF16, "h"),
        ],
        [(keys, "h"), (values, "h"), (rates, "h")],
        [
            vm(flat, BF16), vm(flat, BF16), vm((heads, n), F32),
            vm(wide, F32), vm(inner, BF16), vm(corner, BF16), vm((heads, n, 2 * HEAD), BF16),
        ],
        copies=4 + 2 * parts + heads // 2,
    )
    own_maps = swap(maps, near)
    qt, qt_turned, offset, scores, tek, own_init, prepared = call(
        prepare_kernel,
        [
            (tall, BF16, "a"), (turned, BF16, "a"), (tall, F32, "a"), (full, BF16, "a"),
            (tall, BF16, "a"), ((HEAD, HEAD), F32, "h"), token,
        ],
        [
            (queries, "a"), (keys, "a"), (rates, "a"), (inverse, "a"), (cross, "a"), (tkv, "a"),
            (init_weight, "h"),
        ],
        copies=1,
    )
    slab = (HEAD, 2 * HEAD)
    block = (HEAD, HEAD)
    whole, tree = call(
        group_kernel,
        [(slab, F32, "v"), (branches, F32, "h")],
        [(own_maps, "v"), (prepared, "v")],
        [vm(branches, F32)],
        copies=1,
    )
    other_map = lax.ppermute(whole, "ctx", across)
    (sent,) = call(
        pair_kernel,
        [((PLANES, HEAD, 2 * HEAD), F32, "v")],
        [(whole, "v"), (other_map, "v")],
    )
    pair_maps = swap(sent, far)
    starts, gain_row = call(
        start_kernel,
        [(square, F32, "v"), ((1, width), F32, "v")],
        [
            (own_maps, "v"), (tree, "v"), (pair_maps, "v"), (other_map, "v"), (own_init, "v"),
            (gain_row, "h"),
        ],
        copies=1,
    )
    weights = swap(starts, near)
    hidden, stats = call(
        hidden_kernel,
        [(flat, F32, "v"), ((n, HEAD), F32, "v")],
        [(qt, "v"), (offset, "v"), (cotangent, "v"), (gain_row, "v"), (weights, "v")],
    )
    other = lax.ppermute(stats, "tensor", [(0, 1), (1, 0)])
    normed, dz, local_grad = call(
        norm_kernel,
        [(flat, BF16, "h"), (flat, BF16, "h"), (square, F32, "h")],
        [
            (hidden, "v"), (cotangent, "v"), (gain_row, "v"), (stats, "v"), (other, "v"),
            (qt_turned, "v"),
        ],
        [vm(flat, BF16), vm(flat, BF16), vm(square, F32)],
        copies=2 + parts,
    )
    own_grads = swap(local_grad, near)
    pair = (heads, n, 2 * HEAD)
    grad_queries, u, dk_part, scaled_residual, queried = call(
        query_kernel,
        [(flat, BF16, "h"), (tall, BF16, "h"), (tall, BF16, "h"), (tall, BF16, "h"), token],
        [
            (queries, "h"), (keys, "h"), (rates, "h"), (tkv, "h"), (scores, "h"), (dz, "h"),
            (weights, "v"),
        ],
        [
            vm(flat, BF16), vm(flat, BF16), vm((heads, n), F32), vm(pair, BF16), vm(full, BF16),
            vm(flat, BF16), vm(flat, BF16), vm(tall, BF16), vm(tall, BF16), vm(tall, BF16),
        ],
        copies=1 + 9 * parts,
    )
    steps = (PLANES, HEAD, HEAD)
    after, first, early, up = call(
        adjoint_kernel,
        [(steps, F32, "a"), (steps, F32, "a"), (block, F32, "a"), ((7, HEAD, HEAD), F32, "v")],
        [(pair_maps, "v"), (own_maps, "v"), (tree, "a"), (other_map, "v")],
    )
    whole, sums = call(
        gather_kernel,
        [(block, F32, "v"), ((6, HEAD, HEAD), F32, "v")],
        [(up, "v"), (own_grads, "v"), (queried, "v")],
    )
    other_grad = lax.ppermute(whole, "ctx", across)
    (sent,) = call(
        pair_gradient_kernel,
        [(steps, F32, "v")],
        [(early, "v"), (whole, "v"), (other_grad, "v")],
    )
    pair_grads = swap(sent, far)
    (ends,) = call(
        end_kernel,
        [((GROUP, HEAD + 8, HEAD), F32, "v")],
        [
            (after, "v"), (first, "v"), (own_maps, "v"), (tree, "v"), (own_grads, "v"),
            (sums, "v"), (other_map, "v"), (other_grad, "v"), (pair_grads, "v"),
        ],
        [vm(block, F32)],
    )
    adjoint = swap(ends, near)
    grad_keys, grad_values, grad_rates, grad_init = call(
        key_kernel,
        [(flat, BF16, "h"), (flat, BF16, "h"), ((heads, n), F32, "v"), ((heads, n), F32, "v")],
        [
            (keys, "v"), (rates, "v"), (tek, "v"), (scaled_residual, "v"), (u, "v"),
            (dk_part, "v"), (weights, "v"), (adjoint, "v"),
        ],
        [vm(flat, BF16), vm(flat, BF16)],
        copies=2 * parts,
    )
    return (normed, grad_queries, grad_keys, grad_values, grad_rates, grad_init)


def solution(mesh):
    in_specs = (
        P("ctx", "tensor"),
        P("ctx", "tensor"),
        P("ctx", "tensor"),
        P("tensor", "ctx"),
        P("tensor", None, None),
        P("tensor"),
        P("ctx", "tensor"),
    )
    out_specs = (
        P("ctx", "tensor"),
        P("ctx", "tensor"),
        P("ctx", "tensor"),
        P("ctx", "tensor"),
        P("tensor", "ctx"),
        P("tensor", "ctx"),
    )
    return jax.shard_map(local, mesh=mesh, in_specs=in_specs, out_specs=out_specs, check_vma=False)
```

```python
import jax
import jax.numpy as jnp
from jax import lax
from jax.experimental import pallas as pl
from jax.experimental.pallas import tpu as pltpu
from jax.sharding import PartitionSpec as P

HEAD = 128
MB = 16
EPSILON = 1e-06
GROUP = 8
PLANES = 4
F32 = jnp.float32
BF16 = jnp.bfloat16


def low(a):
    return a.astype(BF16)


def dot(a, b):
    return jnp.dot(a, b, preferred_element_type=F32)


def dot_nt(a, b):
    return lax.dot_general(a, b, (((1,), (1,)), ((), ())), preferred_element_type=F32)


def dot_tn(a, b):
    return lax.dot_general(a, b, (((0,), (0,)), ((), ())), preferred_element_type=F32)


def halves(a):
    high = low(a)
    return high, low(a - high.astype(F32))


def exact(a, b, product=dot):
    (ah, al), (bh, bl) = a, b
    return product(ah, bh) + (product(ah, bl) + product(al, bh))


def call(kernel, outs, args, scratch=(), copies=0, limit=24):
    spaces = {"s": pltpu.SMEM, "v": pltpu.VMEM, "h": pltpu.HBM, "a": pltpu.VMEM}
    values = [pltpu.with_memory_space_constraint(a, pltpu.HBM) if p in "ha" else a for a, p in args]
    results = [
        pltpu.HBM(shape, dtype) if p in "ha" else jax.ShapeDtypeStruct(shape, dtype)
        for shape, dtype, p in outs
    ]
    size = sum(a.size * a.dtype.itemsize for a in values)
    scratch = list(scratch)
    if copies:
        scratch.append(pltpu.SemaphoreType.DMA((copies,)))
    return pl.pallas_call(
        kernel,
        out_shape=results,
        in_specs=[pl.BlockSpec(memory_space=spaces[p]) for _, p in args],
        out_specs=[pl.BlockSpec(memory_space=spaces[p]) for _, _, p in outs],
        scratch_shapes=scratch,
        compiler_params=pltpu.CompilerParams(vmem_limit_bytes=limit * 2**20),
        cost_estimate=pl.CostEstimate(
            flops=2 * 10**9, bytes_accessed=2 * size, transcendentals=0
        ),
        name=kernel.__name__,
    )(*values)


class Copies:
    def __init__(self, semaphores):
        self.semaphores = semaphores
        self.started = []

    def start(self, source, target):
        copy = pltpu.make_async_copy(source, target, self.semaphores.at[len(self.started)])
        copy.start()
        self.started.append(copy)
        return copy


def columns(h):
    return slice(h * HEAD, (h + 1) * HEAD)


def span(first, last):
    return slice(first * HEAD, last * HEAD)


BATCH = 4


def map_kernel(
    k_hbm, v_hbm, e_hbm, ab_hbm, t_hbm, n_hbm, tkv_hbm,
    k_ref, v_ref, e_ref, ab_ref, t_ref, n_ref, tkv_ref, sems,
):
    heads = e_ref.shape[0]
    half = t_ref.shape[-1]
    copies = Copies(sems)
    arrivals = []
    for first in range(0, heads, BATCH):
        part = span(first, first + BATCH)
        key = copies.start(k_hbm.at[:, part], k_ref.at[:, part])
        if first == 0:
            rates = copies.start(e_hbm, e_ref)
        arrivals.append((key, copies.start(v_hbm.at[:, part], v_ref.at[:, part])))
    row = lax.broadcasted_iota(jnp.int32, (half, half), 0)
    col = lax.broadcasted_iota(jnp.int32, (half, half), 1)
    eye = (row == col).astype(F32)
    masks = []
    width = MB
    while width < half:
        masks.append((row // (2 * width) == col // (2 * width)) & (row // width > col // width))
        width *= 2
    sent = []
    ks, es, blocks, crosses, scaled = [], [], [], [], []
    for first, (key, _) in zip(range(0, heads, BATCH), arrivals):
        key.wait()
        if first == 0:
            rates.wait()
        for h in range(first, first + BATCH):
            k = k_ref[:, columns(h)]
            e = e_ref[h : h + 1, :]
            top = -(dot_nt(k[:half], k[:half]) * e[:, :half])
            bottom = -(dot_nt(k[half:], k) * e)
            blocks += [top, bottom[:, half:]]
            crosses.append(low(bottom[:, :half]))
            ks.append(k)
            es.append(e)
    inverses = [low(eye + jnp.where(masks[0], b, 0.0)) for b in blocks]
    for mask in masks[1:]:
        mids = [low(dot(low(jnp.where(mask, b, 0.0)), t)) for b, t in zip(blocks, inverses)]
        inverses = [t + low(dot(t, m)) for t, m in zip(inverses, mids)]
    for h in range(heads):
        t_ref[h, 0] = inverses[2 * h]
        t_ref[h, 1] = inverses[2 * h + 1]
        n_ref[h] = crosses[h]
    sent.append(copies.start(t_ref, t_hbm))
    sent.append(copies.start(n_ref, n_hbm))
    for _, value in arrivals:
        value.wait()
    kvs = [jnp.concatenate([ks[h], v_ref[:, columns(h)]], axis=1) for h in range(heads)]
    tops = [low(dot(t, kv[:half])) for t, kv in zip(inverses[::2], kvs)]
    scaled = [low(jnp.transpose(k.astype(F32)) * e) for k, e in zip(ks, es)]
    mids = [low(kv[half:].astype(F32) + dot(c, x)) for kv, c, x in zip(kvs, crosses, tops)]
    bottoms = [low(dot(t, m)) for t, m in zip(inverses[1::2], mids)]
    for h in range(heads):
        tkv_ref[h, :half] = tops[h]
        tkv_ref[h, half:] = bottoms[h]
    sent.append(copies.start(tkv_ref, tkv_hbm))
    for h in range(heads):
        ab = dot(scaled[h], tkv_ref[h])
        ab_ref[h, :, :HEAD] = eye - ab[:, :HEAD]
        ab_ref[h, :, HEAD:] = ab[:, HEAD:]
        if h % 2 == 1:
            sent.append(copies.start(ab_ref.at[h - 1 : h + 1], ab_hbm.at[h - 1 : h + 1]))
    for copy in sent:
        copy.wait()


def prepare_kernel(
    q_ref, k_ref, e_ref, t_ref, n_ref, tkv_ref, init_hbm,
    qt_ref, qtt_ref, c_ref, st_ref, tek_ref, own_hbm, token_ref, sems,
):
    initial = Copies(sems).start(init_hbm.at[lax.axis_index("ctx") % GROUP], own_hbm)
    n = k_ref.shape[0]
    half = n // 2
    heads = e_ref.shape[0]
    row = lax.broadcasted_iota(jnp.int32, (n, n), 0)
    col = lax.broadcasted_iota(jnp.int32, (n, n), 1)
    causal = row >= col
    token_ref[...] = jnp.zeros_like(token_ref)
    for h in range(heads):
        q = q_ref[:, columns(h)]
        k = k_ref[:, columns(h)]
        e = e_ref[h : h + 1, :]
        se = low(jnp.where(causal, dot_nt(q, k) * e, 0.0))
        sx = dot(se, tkv_ref[h])
        qt = q.astype(F32) - sx[:, :HEAD]
        qt_ref[h] = low(qt)
        qtt_ref[h] = low(jnp.transpose(qt))
        c_ref[h] = sx[:, HEAD:]
        top, bottom = t_ref[h, 0], t_ref[h, 1]
        cross = low(dot(bottom, low(dot(n_ref[h], top))))
        t = jnp.concatenate(
            [
                jnp.concatenate([top, jnp.zeros((half, half), BF16)], axis=1),
                jnp.concatenate([cross, bottom], axis=1),
            ],
            axis=0,
        )
        st_ref[h] = low(-dot(se, t))
        wide = jnp.transpose(jnp.broadcast_to(e, (HEAD, n)))
        tek_ref[h] = low(dot_tn(t, low(k.astype(F32) * wide)))
    initial.wait()


def compose(early, late):
    wide = exact(halves(late[:, :HEAD]), halves(early))
    return jnp.concatenate([wide[:, :HEAD], wide[:, HEAD:] + late[:, HEAD:]], axis=1)


def broadcast(copies, source, targets):
    sent = [copies.start(source, targets.at[i]) for i in range(GROUP)]
    for copy in sent:
        copy.wait()


def level():
    group = lax.axis_index("ctx") // GROUP
    return group // 2, group % 2


def group_kernel(ab_ref, token_ref, whole_ref, tree_ref, factors_ref):
    pairs = [compose(ab_ref[2 * i], ab_ref[2 * i + 1]) for i in range(4)]
    quads = [compose(pairs[2 * i], pairs[2 * i + 1]) for i in range(2)]
    for i, a in enumerate(pairs + quads):
        factors_ref[i] = a[:, :HEAD]
    for i, a in enumerate((pairs[0], pairs[2], quads[0])):
        tree_ref[i] = a
    whole_ref[...] = compose(quads[0], quads[1])


def pair_kernel(own_ref, other_ref, all_ref):
    _, late = level()
    own, other = own_ref[...], other_ref[...]
    early = jnp.where(late == 1, other, own)
    pair = compose(early, jnp.where(late == 1, own, other))
    for i in range(PLANES):
        all_ref[i] = pair


def apply_map(ab, w):
    return exact(halves(ab[:, :HEAD]), halves(w)) + ab[:, HEAD:]


def start_kernel(
    ab_ref, tree_ref, pairs_ref, other_ref, init_ref, gain_hbm, w_ref, gain_ref, sems
):
    weight = Copies(sems).start(gain_hbm, gain_ref)
    plane, late = level()
    w0 = lax.fori_loop(0, plane, lambda z, w: apply_map(pairs_ref[z], w), init_ref[...])
    w0 = lax.fori_loop(0, late, lambda _, w: apply_map(other_ref[...], w), w0)
    w4 = apply_map(tree_ref[2], w0)
    w2 = apply_map(tree_ref[0], w0)
    w6 = apply_map(tree_ref[1], w4)
    for i, w in zip((0, 2, 4, 6), (w0, w2, w4, w6)):
        w_ref[i] = w
        w_ref[i + 1] = apply_map(ab_ref[i], w)
    weight.wait()


def adjoint_kernel(
    pairs_ref, ab_ref, factors_ref, other_ref, after_ref, first_ref, early_ref, up_ref
):
    eye = (
        lax.broadcasted_iota(jnp.int32, (HEAD, HEAD), 0)
        == lax.broadcasted_iota(jnp.int32, (HEAD, HEAD), 1)
    ).astype(F32)
    first = after = eye
    plane, late = level()
    own = exact(halves(factors_ref[5]), halves(factors_ref[4]))
    early_ref[...] = jnp.transpose(jnp.where(late == 1, other_ref[:, :HEAD], own))
    for i in range(4):
        up_ref[i] = jnp.transpose(ab_ref[2 * i, :, :HEAD])
    for i, a in enumerate((0, 2, 4)):
        up_ref[4 + i] = jnp.transpose(factors_ref[a])
    for z in range(PLANES):
        first_ref[z] = first
        later = z > plane
        after_ref[z] = jnp.where(later, after, 0.0)
        if z < PLANES - 1:
            step = halves(pairs_ref[z, :, :HEAD])
            first = exact(halves(first), step, dot_nt)
            after = jnp.where(later, exact(halves(after), step, dot_nt), eye)


def hidden_kernel(qt_ref, c_ref, cot_ref, gain_ref, w_ref, z_ref, stats_ref):
    heads, n = qt_ref.shape[:2]
    squares = jnp.zeros((n, HEAD), F32)
    products = jnp.zeros((n, HEAD), F32)
    for h in range(heads):
        z = dot(qt_ref[h], low(w_ref[h])) + c_ref[h]
        z_ref[:, columns(h)] = z
        squares += z * z
        products += z * (cot_ref[:, columns(h)].astype(F32) * gain_ref[:, columns(h)])
    lane = lax.broadcasted_iota(jnp.int32, (n, HEAD), 1)
    stats_ref[...] = jnp.where(
        lane < HEAD // 2,
        jnp.sum(squares, axis=1, keepdims=True),
        jnp.sum(products, axis=1, keepdims=True),
    )


def norm_kernel(
    z_ref, cot_ref, gain_ref, own_ref, other_ref, qtt_ref,
    normed_hbm, dz_hbm, g_hbm, normed_ref, dz_ref, g_ref, sems,
):
    heads = qtt_ref.shape[0]
    width = 2 * z_ref.shape[1]
    copies = Copies(sems)
    stats = own_ref[...] + other_ref[...]
    inv = lax.rsqrt(stats[:, 0:1] / width + EPSILON)
    shift = inv * inv * inv * stats[:, HEAD // 2 : HEAD // 2 + 1] / width
    for h in range(heads):
        go = cot_ref[:, columns(h)].astype(F32) * gain_ref[:, columns(h)]
        dz = low(inv * go - z_ref[:, columns(h)] * shift)
        dz_ref[:, columns(h)] = dz
        g_ref[h] = dot(qtt_ref[h], dz)
        normed_ref[:, columns(h)] = low(z_ref[:, columns(h)] * inv * gain_ref[:, columns(h)])
        if h % BATCH == BATCH - 1:
            part = slice(h + 1 - BATCH, h + 1)
            flat = span(h + 1 - BATCH, h + 1)
            copies.start(g_ref.at[part], g_hbm.at[part])
            copies.start(dz_ref.at[:, flat], dz_hbm.at[:, flat])
            copies.start(normed_ref.at[:, flat], normed_hbm.at[:, flat])
    for copy in copies.started:
        copy.wait()


def query_kernel(
    q_hbm, k_hbm, e_hbm, tkv_hbm, st_hbm, dz_hbm, w_ref,
    dq_hbm, u_hbm, dk_hbm, er_hbm, token_ref,
    q_ref, k_ref, e_ref, tkv_ref, st_ref, dz_ref, dq_ref, u_ref, dk_ref, er_ref, sems,
):
    n = k_ref.shape[0]
    heads = e_ref.shape[0]
    copies = Copies(sems)
    rates = copies.start(e_hbm, e_ref)
    arrivals = []
    for first in range(0, heads, BATCH):
        part = slice(first, first + BATCH)
        flat = span(first, first + BATCH)
        arrivals.append((
            copies.start(tkv_hbm.at[part], tkv_ref.at[part]),
            copies.start(dz_hbm.at[:, flat], dz_ref.at[:, flat]),
            copies.start(k_hbm.at[:, flat], k_ref.at[:, flat]),
            copies.start(q_hbm.at[:, flat], q_ref.at[:, flat]),
            copies.start(st_hbm.at[part], st_ref.at[part]),
        ))
    row = lax.broadcasted_iota(jnp.int32, (n, n), 0)
    col = lax.broadcasted_iota(jnp.int32, (n, n), 1)
    causal = row >= col
    token_ref[...] = jnp.zeros_like(token_ref)
    rates.wait()
    sent = []
    for first, arrival in zip(range(0, heads, BATCH), arrivals):
        batch = range(first, first + BATCH)
        ws = [low(w_ref[h]) for h in batch]
        rates_wide = [
            jnp.transpose(jnp.broadcast_to(e_ref[h : h + 1, :], (HEAD, n))) for h in batch
        ]
        for copy in arrival:
            copy.wait()
        for h, w, wide in zip(batch, ws, rates_wide):
            r = dot(tkv_ref[h, :, :HEAD], w) - tkv_ref[h, :, HEAD:].astype(F32)
            er_ref[h] = low(r * wide)
        dss = [
            low(jnp.where(causal, -dot_nt(dz_ref[:, columns(h)], er_ref[h]), 0.0)) for h in batch
        ]
        for h, w, ds in zip(batch, ws, dss):
            dq_ref[:, columns(h)] = low(
                dot_nt(dz_ref[:, columns(h)], w) + dot(ds, k_ref[:, columns(h)])
            )
            dk_ref[h] = low(dot_tn(ds, q_ref[:, columns(h)]))
            u_ref[h] = low(dot_tn(st_ref[h], dz_ref[:, columns(h)]))
        part = slice(first, first + BATCH)
        flat = span(first, first + BATCH)
        sent.append(copies.start(dq_ref.at[:, flat], dq_hbm.at[:, flat]))
        for source, target in ((u_ref, u_hbm), (dk_ref, dk_hbm), (er_ref, er_hbm)):
            sent.append(copies.start(source.at[part], target.at[part]))
    for copy in sent:
        copy.wait()


def transposed_map(a, later, own):
    return exact(halves(a), halves(later), dot_tn) + own


def turned_map(a, later, own):
    return exact(halves(a), halves(later)) + own


def gather_kernel(up_ref, g_ref, token_ref, whole_ref, sums_ref):
    pairs = [turned_map(up_ref[i], g_ref[2 * i + 1], g_ref[2 * i]) for i in range(4)]
    quads = [turned_map(up_ref[4 + i], pairs[2 * i + 1], pairs[2 * i]) for i in range(2)]
    for i, a in enumerate(pairs + quads):
        sums_ref[i] = a
    whole_ref[...] = turned_map(up_ref[6], quads[1], quads[0])


def pair_gradient_kernel(early_ref, own_ref, other_ref, all_ref):
    _, late = level()
    own, other = own_ref[...], other_ref[...]
    pair = turned_map(
        early_ref[...], jnp.where(late == 1, own, other), jnp.where(late == 1, other, own)
    )
    for i in range(PLANES):
        all_ref[i] = pair


def end_kernel(
    after_ref, first_ref, ab_ref, factors_ref, g_ref, sums_ref, other_map_ref, other_ref, later_ref,
    d_ref, init_ref,
):
    parts = [halves(later_ref[z]) for z in range(PLANES)]
    _, late = level()
    end = exact(halves(after_ref[1]), parts[1])
    for z in range(2, PLANES):
        end += exact(halves(after_ref[z]), parts[z])
    inner = transposed_map(other_map_ref[:, :HEAD], end, other_ref[...])
    d7 = jnp.where(late == 1, end, inner)
    d3 = transposed_map(factors_ref[5], d7, sums_ref[5])
    d5 = transposed_map(factors_ref[3], d7, sums_ref[3])
    d1 = transposed_map(factors_ref[1], d3, sums_ref[1])
    start = later_ref[0]
    for z in range(1, PLANES):
        start += exact(halves(first_ref[z]), parts[z])
    init_ref[...] = start
    rows = init_ref[pl.ds(pl.multiple_of(lax.axis_index("ctx") // GROUP * 16, 16), 16), :]
    for i, d in zip((7, 5, 3, 1), (d7, d5, d3, d1)):
        d_ref[i, :HEAD, :] = d
        d_ref[i - 1, :HEAD, :] = transposed_map(ab_ref[i, :, :HEAD], d, g_ref[i])
    for i in range(GROUP):
        d_ref[i, HEAD:, :] = jnp.zeros((8, HEAD), F32)
        d_ref[i, HEAD : HEAD + 2, :] = rows[2 * i : 2 * i + 2]


def key_kernel(
    k_ref, e_ref, tek_ref, er_ref, u_ref, dkp_ref, w_ref, d_ref,
    dk_hbm, dv_hbm, de_ref, gi_ref, dk_ref, dv_ref, sems,
):
    n = k_ref.shape[0]
    heads = e_ref.shape[0]
    copies = Copies(sems)
    row = lax.broadcasted_iota(jnp.int32, (n, n), 0) // MB
    col = lax.broadcasted_iota(jnp.int32, (n, n), 1) // MB
    before = row > col
    after = row < col
    ones = jnp.ones((8, HEAD), BF16)
    for h in range(heads):
        gi_ref[h : h + 1, :HEAD] = d_ref[h, HEAD : HEAD + 1, :]
        gi_ref[h : h + 1, HEAD:] = d_ref[h, HEAD + 1 : HEAD + 2, :]
    for first in range(0, heads, BATCH):
        batch = range(first, first + BATCH)
        ds = [low(d_ref[h, :HEAD, :]) for h in batch]
        both = [jnp.concatenate([low(w_ref[h]), -d], axis=1) for h, d in zip(batch, ds)]
        ers = [er_ref[h] for h in batch]
        us = [u_ref[h].astype(F32) - dot(tek_ref[h], d) for h, d in zip(batch, ds)]
        lows = [low(u) for u in us]
        for h, u in zip(batch, lows):
            dv_ref[:, columns(h)] = -u
        flat = span(first, first + BATCH)
        copies.start(dv_ref.at[:, flat], dv_hbm.at[:, flat])
        ps = [low(u * er.astype(F32)) for u, er in zip(us, ers)]
        xs = [
            low(jnp.where(before, dot_nt(u, er), jnp.where(after, dot_nt(er, u), 0.0)))
            for u, er in zip(lows, ers)
        ]
        dks = [
            dkp_ref[h].astype(F32) + dot_nt(jnp.concatenate([u, er], axis=1), b)
            for h, u, er, b in zip(batch, lows, ers, both)
        ]
        for h, dk, x, p in zip(batch, dks, xs, ps):
            e = e_ref[h : h + 1, :]
            dk_ref[:, columns(h)] = low(dk - dot(x, k_ref[:, columns(h)]))
            de_ref[h : h + 1, :] = dot_nt(ones, p)[0:1] / (e * e)
        copies.start(dk_ref.at[:, flat], dk_hbm.at[:, flat])
    for copy in copies.started:
        copy.wait()


def local(queries, keys, values, rates, init_weight, gain, cotangent):
    n, width = keys.shape
    heads = width // HEAD
    count = lax.axis_size("ctx") // GROUP
    near = [[g * GROUP + i for i in range(GROUP)] for g in range(count)]
    stride = 2 * GROUP
    far = [[z * stride + i for z in range(PLANES)] for i in range(stride)]
    across = [(i, i + GROUP if i % stride < GROUP else i - GROUP) for i in range(count * GROUP)]
    gain_row = gain.reshape(1, width)

    def swap(a, groups):
        return lax.all_to_all(a, "ctx", 0, 0, axis_index_groups=groups)

    square = (GROUP, HEAD, HEAD)
    wide = (GROUP, HEAD, 2 * HEAD)
    tall = (heads, n, HEAD)
    full = (heads, n, n)
    flat = (n, width)
    token = ((8, HEAD), F32, "v")
    parts = heads // BATCH
    vm = pltpu.VMEM

    half = n // 2
    inner = (heads, 2, half, half)
    corner = (heads, half, half)
    turned = (heads, HEAD, n)
    maps, inverse, cross, tkv = call(
        map_kernel,
        [
            (wide, F32, "h"), (inner, BF16, "h"), (corner, BF16, "h"),
            ((heads, n, 2 * HEAD), BF16, "h"),
        ],
        [(keys, "h"), (values, "h"), (rates, "h")],
        [
            vm(flat, BF16), vm(flat, BF16), vm((heads, n), F32),
            vm(wide, F32), vm(inner, BF16), vm(corner, BF16), vm((heads, n, 2 * HEAD), BF16),
        ],
        copies=4 + 2 * parts + heads // 2,
    )
    own_maps = swap(maps, near)
    qt, qt_turned, offset, scores, tek, own_init, prepared = call(
        prepare_kernel,
        [
            (tall, BF16, "a"), (turned, BF16, "a"), (tall, F32, "a"), (full, BF16, "a"),
            (tall, BF16, "a"), ((HEAD, HEAD), F32, "h"), token,
        ],
        [
            (queries, "a"), (keys, "a"), (rates, "a"), (inverse, "a"), (cross, "a"), (tkv, "a"),
            (init_weight, "h"),
        ],
        copies=1,
    )
    slab = (HEAD, 2 * HEAD)
    block = (HEAD, HEAD)
    whole, tree, factors = call(
        group_kernel,
        [(slab, F32, "v"), ((3, HEAD, 2 * HEAD), F32, "v"), ((6, HEAD, HEAD), F32, "v")],
        [(own_maps, "v"), (prepared, "v")],
    )
    other_map = lax.ppermute(whole, "ctx", across)
    (sent,) = call(
        pair_kernel,
        [((PLANES, HEAD, 2 * HEAD), F32, "v")],
        [(whole, "v"), (other_map, "v")],
    )
    pair_maps = swap(sent, far)
    starts, gain_row = call(
        start_kernel,
        [(square, F32, "v"), ((1, width), F32, "v")],
        [
            (own_maps, "v"), (tree, "v"), (pair_maps, "v"), (other_map, "v"), (own_init, "v"),
            (gain_row, "h"),
        ],
        copies=1,
    )
    weights = swap(starts, near)
    hidden, stats = call(
        hidden_kernel,
        [(flat, F32, "v"), ((n, HEAD), F32, "v")],
        [(qt, "v"), (offset, "v"), (cotangent, "v"), (gain_row, "v"), (weights, "v")],
    )
    other = lax.ppermute(stats, "tensor", [(0, 1), (1, 0)])
    normed, dz, local_grad = call(
        norm_kernel,
        [(flat, BF16, "h"), (flat, BF16, "h"), (square, F32, "h")],
        [
            (hidden, "v"), (cotangent, "v"), (gain_row, "v"), (stats, "v"), (other, "v"),
            (qt_turned, "v"),
        ],
        [vm(flat, BF16), vm(flat, BF16), vm(square, F32)],
        copies=3 * parts,
    )
    own_grads = swap(local_grad, near)
    pair = (heads, n, 2 * HEAD)
    grad_queries, u, dk_part, scaled_residual, queried = call(
        query_kernel,
        [(flat, BF16, "h"), (tall, BF16, "h"), (tall, BF16, "h"), (tall, BF16, "h"), token],
        [
            (queries, "h"), (keys, "h"), (rates, "h"), (tkv, "h"), (scores, "h"), (dz, "h"),
            (weights, "v"),
        ],
        [
            vm(flat, BF16), vm(flat, BF16), vm((heads, n), F32), vm(pair, BF16), vm(full, BF16),
            vm(flat, BF16), vm(flat, BF16), vm(tall, BF16), vm(tall, BF16), vm(tall, BF16),
        ],
        copies=1 + 9 * parts,
    )
    steps = (PLANES, HEAD, HEAD)
    after, first, early, up = call(
        adjoint_kernel,
        [(steps, F32, "a"), (steps, F32, "a"), (block, F32, "a"), ((7, HEAD, HEAD), F32, "v")],
        [(pair_maps, "v"), (own_maps, "v"), (factors, "v"), (other_map, "v")],
    )
    whole, sums = call(
        gather_kernel,
        [(block, F32, "v"), ((6, HEAD, HEAD), F32, "v")],
        [(up, "v"), (own_grads, "v"), (queried, "v")],
    )
    other_grad = lax.ppermute(whole, "ctx", across)
    (sent,) = call(
        pair_gradient_kernel,
        [(steps, F32, "v")],
        [(early, "v"), (whole, "v"), (other_grad, "v")],
    )
    pair_grads = swap(sent, far)
    (ends,) = call(
        end_kernel,
        [((GROUP, HEAD + 8, HEAD), F32, "v")],
        [
            (after, "v"), (first, "v"), (own_maps, "v"), (factors, "v"), (own_grads, "v"),
            (sums, "v"), (other_map, "v"), (other_grad, "v"), (pair_grads, "v"),
        ],
        [vm(block, F32)],
    )
    adjoint = swap(ends, near)
    grad_keys, grad_values, grad_rates, grad_init = call(
        key_kernel,
        [(flat, BF16, "h"), (flat, BF16, "h"), ((heads, n), F32, "v"), ((heads, n), F32, "v")],
        [
            (keys, "v"), (rates, "v"), (tek, "v"), (scaled_residual, "v"), (u, "v"),
            (dk_part, "v"), (weights, "v"), (adjoint, "v"),
        ],
        [vm(flat, BF16), vm(flat, BF16)],
        copies=2 * parts,
    )
    return (normed, grad_queries, grad_keys, grad_values, grad_rates, grad_init)


def solution(mesh):
    in_specs = (
        P("ctx", "tensor"),
        P("ctx", "tensor"),
        P("ctx", "tensor"),
        P("tensor", "ctx"),
        P("tensor", None, None),
        P("tensor"),
        P("ctx", "tensor"),
    )
    out_specs = (
        P("ctx", "tensor"),
        P("ctx", "tensor"),
        P("ctx", "tensor"),
        P("ctx", "tensor"),
        P("tensor", "ctx"),
        P("tensor", "ctx"),
    )
    return jax.shard_map(local, mesh=mesh, in_specs=in_specs, out_specs=out_specs, check_vma=False)
```

```python
import jax
import jax.numpy as jnp
from jax import lax
from jax.experimental import pallas as pl
from jax.experimental.pallas import tpu as pltpu
from jax.sharding import PartitionSpec as P

HEAD = 128
MB = 16
EPSILON = 1e-06
GROUP = 8
PLANES = 4
F32 = jnp.float32
BF16 = jnp.bfloat16


def low(a):
    return a.astype(BF16)


def dot(a, b):
    return jnp.dot(a, b, preferred_element_type=F32)


def dot_nt(a, b):
    return lax.dot_general(a, b, (((1,), (1,)), ((), ())), preferred_element_type=F32)


def dot_tn(a, b):
    return lax.dot_general(a, b, (((0,), (0,)), ((), ())), preferred_element_type=F32)


def halves(a):
    high = low(a)
    return high, low(a - high.astype(F32))


def exact(a, b, product=dot):
    (ah, al), (bh, bl) = a, b
    return product(ah, bh) + (product(ah, bl) + product(al, bh))


def call(kernel, outs, args, scratch=(), copies=0, limit=24):
    spaces = {"s": pltpu.SMEM, "v": pltpu.VMEM, "h": pltpu.HBM, "a": pltpu.VMEM}
    values = [pltpu.with_memory_space_constraint(a, pltpu.HBM) if p in "ha" else a for a, p in args]
    results = [
        pltpu.HBM(shape, dtype) if p in "ha" else jax.ShapeDtypeStruct(shape, dtype)
        for shape, dtype, p in outs
    ]
    size = sum(a.size * a.dtype.itemsize for a in values)
    scratch = list(scratch)
    if copies:
        scratch.append(pltpu.SemaphoreType.DMA((copies,)))
    return pl.pallas_call(
        kernel,
        out_shape=results,
        in_specs=[pl.BlockSpec(memory_space=spaces[p]) for _, p in args],
        out_specs=[pl.BlockSpec(memory_space=spaces[p]) for _, _, p in outs],
        scratch_shapes=scratch,
        compiler_params=pltpu.CompilerParams(vmem_limit_bytes=limit * 2**20),
        cost_estimate=pl.CostEstimate(
            flops=2 * 10**9, bytes_accessed=2 * size, transcendentals=0
        ),
        name=kernel.__name__,
    )(*values)


class Copies:
    def __init__(self, semaphores):
        self.semaphores = semaphores
        self.started = []

    def start(self, source, target):
        copy = pltpu.make_async_copy(source, target, self.semaphores.at[len(self.started)])
        copy.start()
        self.started.append(copy)
        return copy


def columns(h):
    return slice(h * HEAD, (h + 1) * HEAD)


def span(first, last):
    return slice(first * HEAD, last * HEAD)


BATCH = 4


def map_kernel(
    k_hbm, v_hbm, e_hbm, ab_ref, t_hbm, n_hbm, tkv_hbm,
    k_ref, v_ref, e_ref, t_ref, n_ref, tkv_ref, sems,
):
    heads = e_ref.shape[0]
    half = t_ref.shape[-1]
    copies = Copies(sems)
    arrivals = []
    for first in range(0, heads, BATCH):
        part = span(first, first + BATCH)
        key = copies.start(k_hbm.at[:, part], k_ref.at[:, part])
        if first == 0:
            rates = copies.start(e_hbm, e_ref)
        arrivals.append((key, copies.start(v_hbm.at[:, part], v_ref.at[:, part])))
    row = lax.broadcasted_iota(jnp.int32, (half, half), 0)
    col = lax.broadcasted_iota(jnp.int32, (half, half), 1)
    eye = (row == col).astype(F32)
    masks = []
    width = MB
    while width < half:
        masks.append((row // (2 * width) == col // (2 * width)) & (row // width > col // width))
        width *= 2
    sent = []
    ks, es, blocks, crosses, scaled = [], [], [], [], []
    for first, (key, _) in zip(range(0, heads, BATCH), arrivals):
        key.wait()
        if first == 0:
            rates.wait()
        for h in range(first, first + BATCH):
            k = k_ref[:, columns(h)]
            e = e_ref[h : h + 1, :]
            top = -(dot_nt(k[:half], k[:half]) * e[:, :half])
            bottom = -(dot_nt(k[half:], k) * e)
            blocks += [top, bottom[:, half:]]
            crosses.append(low(bottom[:, :half]))
            ks.append(k)
            es.append(e)
    inverses = [low(eye + jnp.where(masks[0], b, 0.0)) for b in blocks]
    for mask in masks[1:]:
        mids = [low(dot(low(jnp.where(mask, b, 0.0)), t)) for b, t in zip(blocks, inverses)]
        inverses = [t + low(dot(t, m)) for t, m in zip(inverses, mids)]
    for h in range(heads):
        t_ref[h, 0] = inverses[2 * h]
        t_ref[h, 1] = inverses[2 * h + 1]
        n_ref[h] = crosses[h]
    sent.append(copies.start(t_ref, t_hbm))
    sent.append(copies.start(n_ref, n_hbm))
    for _, value in arrivals:
        value.wait()
    kvs = [jnp.concatenate([ks[h], v_ref[:, columns(h)]], axis=1) for h in range(heads)]
    tops = [low(dot(t, kv[:half])) for t, kv in zip(inverses[::2], kvs)]
    scaled = [low(jnp.transpose(k.astype(F32)) * e) for k, e in zip(ks, es)]
    mids = [low(kv[half:].astype(F32) + dot(c, x)) for kv, c, x in zip(kvs, crosses, tops)]
    bottoms = [low(dot(t, m)) for t, m in zip(inverses[1::2], mids)]
    for h in range(heads):
        tkv_ref[h, :half] = tops[h]
        tkv_ref[h, half:] = bottoms[h]
    sent.append(copies.start(tkv_ref, tkv_hbm))
    for h in range(heads):
        ab = dot(scaled[h], tkv_ref[h])
        ab_ref[h, :, :HEAD] = eye - ab[:, :HEAD]
        ab_ref[h, :, HEAD:] = ab[:, HEAD:]
    for copy in sent:
        copy.wait()


def causal_scores(q, k, e):
    n = q.shape[0]
    row = lax.broadcasted_iota(jnp.int32, (n, n), 0)
    col = lax.broadcasted_iota(jnp.int32, (n, n), 1)
    return low(jnp.where(row >= col, dot_nt(q, k) * e, 0.0))


def prepare_kernel(
    q_hbm, k_hbm, e_hbm, tkv_hbm, init_hbm,
    qt_hbm, qtt_hbm, c_hbm, se_hbm, own_hbm, token_ref,
    q_ref, k_ref, e_ref, tkv_ref, qt_ref, qtt_ref, c_ref, se_ref, sems,
):
    heads = e_ref.shape[0]
    copies = Copies(sems)
    sent = [copies.start(init_hbm.at[lax.axis_index("ctx") % GROUP], own_hbm)]
    rates = copies.start(e_hbm, e_ref)
    arrivals = []
    for first in range(0, heads, BATCH):
        part = slice(first, first + BATCH)
        flat = span(first, first + BATCH)
        arrivals.append((
            copies.start(q_hbm.at[:, flat], q_ref.at[:, flat]),
            copies.start(k_hbm.at[:, flat], k_ref.at[:, flat]),
            copies.start(tkv_hbm.at[part], tkv_ref.at[part]),
        ))
    token_ref[...] = jnp.zeros_like(token_ref)
    rates.wait()
    for first, arrival in zip(range(0, heads, BATCH), arrivals):
        batch = range(first, first + BATCH)
        for copy in arrival:
            copy.wait()
        scores = [
            causal_scores(q_ref[:, columns(h)], k_ref[:, columns(h)], e_ref[h : h + 1, :])
            for h in batch
        ]
        for h, se in zip(batch, scores):
            se_ref[h] = se
            sx = dot(se, tkv_ref[h])
            qt = q_ref[:, columns(h)].astype(F32) - sx[:, :HEAD]
            qt_ref[h] = low(qt)
            qtt_ref[h] = low(jnp.transpose(qt))
            c_ref[h] = sx[:, HEAD:]
        part = slice(first, first + BATCH)
        for source, target in (
            (qt_ref, qt_hbm), (qtt_ref, qtt_hbm), (c_ref, c_hbm), (se_ref, se_hbm)
        ):
            sent.append(copies.start(source.at[part], target.at[part]))
    for copy in sent:
        copy.wait()


def adjoint_residual_kernel(
    k_hbm, e_hbm, se_hbm, t_hbm, n_hbm, dz_hbm, u_hbm, tek_hbm, token_ref,
    k_ref, e_ref, se_ref, t_ref, n_ref, dz_ref, u_ref, tek_ref, sems,
):
    heads, n = e_ref.shape
    half = n // 2
    copies = Copies(sems)
    rates = copies.start(e_hbm, e_ref)
    arrivals = []
    for first in range(0, heads, BATCH):
        part = slice(first, first + BATCH)
        flat = span(first, first + BATCH)
        arrivals.append((
            copies.start(t_hbm.at[part], t_ref.at[part]),
            copies.start(n_hbm.at[part], n_ref.at[part]),
            copies.start(k_hbm.at[:, flat], k_ref.at[:, flat]),
            copies.start(se_hbm.at[part], se_ref.at[part]),
            copies.start(dz_hbm.at[:, flat], dz_ref.at[:, flat]),
        ))
    token_ref[...] = jnp.zeros_like(token_ref)
    rates.wait()
    sent = []
    for first, arrival in zip(range(0, heads, BATCH), arrivals):
        batch = range(first, first + BATCH)
        wides = [jnp.transpose(jnp.broadcast_to(e_ref[h : h + 1, :], (HEAD, n))) for h in batch]
        for copy in arrival:
            copy.wait()
        mids = [low(dot(n_ref[h], t_ref[h, 0])) for h in batch]
        ys = [
            jnp.concatenate(
                [
                    low(dot_tn(se_ref[h], dz_ref[:, columns(h)])),
                    low(k_ref[:, columns(h)].astype(F32) * wide),
                ],
                axis=1,
            )
            for h, wide in zip(batch, wides)
        ]
        lowers = [dot_tn(t_ref[h, 1], y[half:]) for h, y in zip(batch, ys)]
        uppers = [
            dot_tn(t_ref[h, 0], y[:half]) + dot_tn(m, low(x))
            for h, y, m, x in zip(batch, ys, mids, lowers)
        ]
        for h, upper, lower in zip(batch, uppers, lowers):
            u_ref[h, :half] = low(-upper[:, :HEAD])
            u_ref[h, half:] = low(-lower[:, :HEAD])
            tek_ref[h, :half] = low(upper[:, HEAD:])
            tek_ref[h, half:] = low(lower[:, HEAD:])
        part = slice(first, first + BATCH)
        for source, target in ((u_ref, u_hbm), (tek_ref, tek_hbm)):
            sent.append(copies.start(source.at[part], target.at[part]))
    for copy in sent:
        copy.wait()


def compose(early, late):
    wide = exact(halves(late[:, :HEAD]), halves(early))
    return jnp.concatenate([wide[:, :HEAD], wide[:, HEAD:] + late[:, HEAD:]], axis=1)


def broadcast(copies, source, targets):
    sent = [copies.start(source, targets.at[i]) for i in range(GROUP)]
    for copy in sent:
        copy.wait()


def level():
    group = lax.axis_index("ctx") // GROUP
    return group // 2, group % 2


def group_kernel(ab_ref, whole_ref, tree_ref, factors_ref):
    pairs = [compose(ab_ref[2 * i], ab_ref[2 * i + 1]) for i in range(4)]
    quads = [compose(pairs[2 * i], pairs[2 * i + 1]) for i in range(2)]
    for i, a in enumerate(pairs + quads):
        factors_ref[i] = a[:, :HEAD]
    for i, a in enumerate((pairs[0], pairs[2], quads[0])):
        tree_ref[i] = a
    whole_ref[...] = compose(quads[0], quads[1])


def pair_kernel(own_ref, other_ref, token_ref, all_ref):
    _, late = level()
    own, other = own_ref[...], other_ref[...]
    early = jnp.where(late == 1, other, own)
    pair = compose(early, jnp.where(late == 1, own, other))
    for i in range(PLANES):
        all_ref[i] = pair


def apply_map(ab, w):
    return exact(halves(ab[:, :HEAD]), halves(w)) + ab[:, HEAD:]


def start_kernel(
    ab_ref, tree_ref, pairs_ref, other_ref, init_ref, gain_hbm, w_ref, gain_ref, sems
):
    weight = Copies(sems).start(gain_hbm, gain_ref)
    plane, late = level()
    w0 = lax.fori_loop(0, plane, lambda z, w: apply_map(pairs_ref[z], w), init_ref[...])
    w0 = lax.fori_loop(0, late, lambda _, w: apply_map(other_ref[...], w), w0)
    w4 = apply_map(tree_ref[2], w0)
    w2 = apply_map(tree_ref[0], w0)
    w6 = apply_map(tree_ref[1], w4)
    for i, w in zip((0, 2, 4, 6), (w0, w2, w4, w6)):
        w_ref[i] = w
        w_ref[i + 1] = apply_map(ab_ref[i], w)
    weight.wait()


def adjoint_kernel(
    pairs_ref, ab_ref, factors_ref, other_ref, after_ref, first_ref, early_ref, up_ref
):
    eye = (
        lax.broadcasted_iota(jnp.int32, (HEAD, HEAD), 0)
        == lax.broadcasted_iota(jnp.int32, (HEAD, HEAD), 1)
    ).astype(F32)
    first = after = eye
    plane, late = level()
    own = exact(halves(factors_ref[5]), halves(factors_ref[4]))
    early_ref[...] = jnp.transpose(jnp.where(late == 1, other_ref[:, :HEAD], own))
    for i in range(4):
        up_ref[i] = jnp.transpose(ab_ref[2 * i, :, :HEAD])
    for i, a in enumerate((0, 2, 4)):
        up_ref[4 + i] = jnp.transpose(factors_ref[a])
    for z in range(PLANES):
        first_ref[z] = first
        later = z > plane
        after_ref[z] = jnp.where(later, after, 0.0)
        if z < PLANES - 1:
            step = halves(pairs_ref[z, :, :HEAD])
            first = exact(halves(first), step, dot_nt)
            after = jnp.where(later, exact(halves(after), step, dot_nt), eye)


def hidden_kernel(qt_ref, c_ref, cot_ref, gain_ref, w_ref, z_ref, stats_ref):
    heads, n = qt_ref.shape[:2]
    squares = jnp.zeros((n, HEAD), F32)
    products = jnp.zeros((n, HEAD), F32)
    for h in range(heads):
        z = dot(qt_ref[h], low(w_ref[h])) + c_ref[h]
        z_ref[:, columns(h)] = z
        squares += z * z
        products += z * (cot_ref[:, columns(h)].astype(F32) * gain_ref[:, columns(h)])
    lane = lax.broadcasted_iota(jnp.int32, (n, HEAD), 1)
    stats_ref[...] = jnp.where(
        lane < HEAD // 2,
        jnp.sum(squares, axis=1, keepdims=True),
        jnp.sum(products, axis=1, keepdims=True),
    )


def norm_kernel(
    z_ref, cot_ref, gain_ref, own_ref, other_ref, qtt_ref,
    normed_hbm, dz_hbm, g_hbm, normed_ref, dz_ref, g_ref, sems,
):
    heads = qtt_ref.shape[0]
    width = 2 * z_ref.shape[1]
    copies = Copies(sems)
    stats = own_ref[...] + other_ref[...]
    inv = lax.rsqrt(stats[:, 0:1] / width + EPSILON)
    shift = inv * inv * inv * stats[:, HEAD // 2 : HEAD // 2 + 1] / width
    for h in range(heads):
        go = cot_ref[:, columns(h)].astype(F32) * gain_ref[:, columns(h)]
        dz = low(inv * go - z_ref[:, columns(h)] * shift)
        dz_ref[:, columns(h)] = dz
        g_ref[h] = dot(qtt_ref[h], dz)
        normed_ref[:, columns(h)] = low(z_ref[:, columns(h)] * inv * gain_ref[:, columns(h)])
        if h % BATCH == BATCH - 1:
            part = slice(h + 1 - BATCH, h + 1)
            flat = span(h + 1 - BATCH, h + 1)
            copies.start(g_ref.at[part], g_hbm.at[part])
            copies.start(dz_ref.at[:, flat], dz_hbm.at[:, flat])
            copies.start(normed_ref.at[:, flat], normed_hbm.at[:, flat])
    for copy in copies.started:
        copy.wait()


def query_kernel(
    q_hbm, k_hbm, e_hbm, tkv_hbm, dz_hbm, w_ref, dq_hbm, dk_hbm, er_hbm, token_ref,
    q_ref, k_ref, e_ref, tkv_ref, dz_ref, dq_ref, dk_ref, er_ref, sems,
):
    n = k_ref.shape[0]
    heads = e_ref.shape[0]
    copies = Copies(sems)
    rates = copies.start(e_hbm, e_ref)
    arrivals = []
    for first in range(0, heads, BATCH):
        part = slice(first, first + BATCH)
        flat = span(first, first + BATCH)
        arrivals.append((
            copies.start(tkv_hbm.at[part], tkv_ref.at[part]),
            copies.start(dz_hbm.at[:, flat], dz_ref.at[:, flat]),
            copies.start(k_hbm.at[:, flat], k_ref.at[:, flat]),
            copies.start(q_hbm.at[:, flat], q_ref.at[:, flat]),
        ))
    row = lax.broadcasted_iota(jnp.int32, (n, n), 0)
    col = lax.broadcasted_iota(jnp.int32, (n, n), 1)
    causal = row >= col
    token_ref[...] = jnp.zeros_like(token_ref)
    rates.wait()
    sent = []
    for first, arrival in zip(range(0, heads, BATCH), arrivals):
        batch = range(first, first + BATCH)
        ws = [low(w_ref[h]) for h in batch]
        rates_wide = [
            jnp.transpose(jnp.broadcast_to(e_ref[h : h + 1, :], (HEAD, n))) for h in batch
        ]
        for copy in arrival:
            copy.wait()
        for h, w, wide in zip(batch, ws, rates_wide):
            r = dot(tkv_ref[h, :, :HEAD], w) - tkv_ref[h, :, HEAD:].astype(F32)
            er_ref[h] = low(r * wide)
        dss = [
            low(jnp.where(causal, -dot_nt(dz_ref[:, columns(h)], er_ref[h]), 0.0)) for h in batch
        ]
        for h, w, ds in zip(batch, ws, dss):
            dq_ref[:, columns(h)] = low(
                dot_nt(dz_ref[:, columns(h)], w) + dot(ds, k_ref[:, columns(h)])
            )
            dk_ref[h] = low(dot_tn(ds, q_ref[:, columns(h)]))
        part = slice(first, first + BATCH)
        flat = span(first, first + BATCH)
        sent.append(copies.start(dq_ref.at[:, flat], dq_hbm.at[:, flat]))
        for source, target in ((dk_ref, dk_hbm), (er_ref, er_hbm)):
            sent.append(copies.start(source.at[part], target.at[part]))
    for copy in sent:
        copy.wait()


def transposed_map(a, later, own):
    return exact(halves(a), halves(later), dot_tn) + own


def turned_map(a, later, own):
    return exact(halves(a), halves(later)) + own


def gather_kernel(up_ref, g_ref, token_ref, whole_ref, sums_ref):
    pairs = [turned_map(up_ref[i], g_ref[2 * i + 1], g_ref[2 * i]) for i in range(4)]
    quads = [turned_map(up_ref[4 + i], pairs[2 * i + 1], pairs[2 * i]) for i in range(2)]
    for i, a in enumerate(pairs + quads):
        sums_ref[i] = a
    whole_ref[...] = turned_map(up_ref[6], quads[1], quads[0])


def pair_gradient_kernel(early_ref, own_ref, other_ref, token_ref, all_ref):
    _, late = level()
    own, other = own_ref[...], other_ref[...]
    pair = turned_map(
        early_ref[...], jnp.where(late == 1, own, other), jnp.where(late == 1, other, own)
    )
    for i in range(PLANES):
        all_ref[i] = pair


def end_kernel(
    after_ref, first_ref, ab_ref, factors_ref, g_ref, sums_ref, other_map_ref, other_ref, later_ref,
    d_ref, init_ref,
):
    parts = [halves(later_ref[z]) for z in range(PLANES)]
    _, late = level()
    end = exact(halves(after_ref[1]), parts[1])
    for z in range(2, PLANES):
        end += exact(halves(after_ref[z]), parts[z])
    inner = transposed_map(other_map_ref[:, :HEAD], end, other_ref[...])
    d7 = jnp.where(late == 1, end, inner)
    d3 = transposed_map(factors_ref[5], d7, sums_ref[5])
    d5 = transposed_map(factors_ref[3], d7, sums_ref[3])
    d1 = transposed_map(factors_ref[1], d3, sums_ref[1])
    start = later_ref[0]
    for z in range(1, PLANES):
        start += exact(halves(first_ref[z]), parts[z])
    init_ref[...] = start
    rows = init_ref[pl.ds(pl.multiple_of(lax.axis_index("ctx") // GROUP * 16, 16), 16), :]
    for i, d in zip((7, 5, 3, 1), (d7, d5, d3, d1)):
        d_ref[i, :HEAD, :] = d
        d_ref[i - 1, :HEAD, :] = transposed_map(ab_ref[i, :, :HEAD], d, g_ref[i])
    for i in range(GROUP):
        d_ref[i, HEAD:, :] = jnp.zeros((8, HEAD), F32)
        d_ref[i, HEAD : HEAD + 2, :] = rows[2 * i : 2 * i + 2]


def key_kernel(
    k_ref, e_ref, tek_ref, er_ref, u_ref, dkp_ref, w_ref, d_ref,
    dk_hbm, dv_hbm, de_ref, gi_ref, dk_ref, dv_ref, sems,
):
    n = k_ref.shape[0]
    heads = e_ref.shape[0]
    copies = Copies(sems)
    row = lax.broadcasted_iota(jnp.int32, (n, n), 0) // MB
    col = lax.broadcasted_iota(jnp.int32, (n, n), 1) // MB
    before = row > col
    after = row < col
    ones = jnp.ones((8, HEAD), BF16)
    for h in range(heads):
        gi_ref[h : h + 1, :HEAD] = d_ref[h, HEAD : HEAD + 1, :]
        gi_ref[h : h + 1, HEAD:] = d_ref[h, HEAD + 1 : HEAD + 2, :]
    for first in range(0, heads, BATCH):
        batch = range(first, first + BATCH)
        ds = [low(d_ref[h, :HEAD, :]) for h in batch]
        both = [jnp.concatenate([low(w_ref[h]), -d], axis=1) for h, d in zip(batch, ds)]
        ers = [er_ref[h] for h in batch]
        us = [u_ref[h].astype(F32) - dot(tek_ref[h], d) for h, d in zip(batch, ds)]
        lows = [low(u) for u in us]
        for h, u in zip(batch, lows):
            dv_ref[:, columns(h)] = -u
        flat = span(first, first + BATCH)
        copies.start(dv_ref.at[:, flat], dv_hbm.at[:, flat])
        ps = [low(u * er.astype(F32)) for u, er in zip(us, ers)]
        xs = [
            low(jnp.where(before, dot_nt(u, er), jnp.where(after, dot_nt(er, u), 0.0)))
            for u, er in zip(lows, ers)
        ]
        dks = [
            dkp_ref[h].astype(F32) + dot_nt(jnp.concatenate([u, er], axis=1), b)
            for h, u, er, b in zip(batch, lows, ers, both)
        ]
        for h, dk, x, p in zip(batch, dks, xs, ps):
            e = e_ref[h : h + 1, :]
            dk_ref[:, columns(h)] = low(dk - dot(x, k_ref[:, columns(h)]))
            de_ref[h : h + 1, :] = dot_nt(ones, p)[0:1] / (e * e)
        copies.start(dk_ref.at[:, flat], dk_hbm.at[:, flat])
    for copy in copies.started:
        copy.wait()


def local(queries, keys, values, rates, init_weight, gain, cotangent):
    n, width = keys.shape
    heads = width // HEAD
    count = lax.axis_size("ctx") // GROUP
    near = [[g * GROUP + i for i in range(GROUP)] for g in range(count)]
    stride = 2 * GROUP
    far = [[z * stride + i for z in range(PLANES)] for i in range(stride)]
    across = [(i, i + GROUP if i % stride < GROUP else i - GROUP) for i in range(count * GROUP)]
    gain_row = gain.reshape(1, width)

    def swap(a, groups):
        return lax.all_to_all(a, "ctx", 0, 0, axis_index_groups=groups)

    square = (GROUP, HEAD, HEAD)
    wide = (GROUP, HEAD, 2 * HEAD)
    tall = (heads, n, HEAD)
    full = (heads, n, n)
    flat = (n, width)
    token = ((8, HEAD), F32, "v")
    parts = heads // BATCH
    vm = pltpu.VMEM

    half = n // 2
    inner = (heads, 2, half, half)
    corner = (heads, half, half)
    pair = (heads, n, 2 * HEAD)
    turned = (heads, HEAD, n)
    maps, inverse, cross, tkv = call(
        map_kernel,
        [
            (wide, F32, "v"), (inner, BF16, "h"), (corner, BF16, "h"),
            ((heads, n, 2 * HEAD), BF16, "h"),
        ],
        [(keys, "h"), (values, "h"), (rates, "h")],
        [
            vm(flat, BF16), vm(flat, BF16), vm((heads, n), F32),
            vm(inner, BF16), vm(corner, BF16), vm((heads, n, 2 * HEAD), BF16),
        ],
        copies=4 + 2 * parts,
    )
    own_maps = swap(maps, near)
    qt, qt_turned, offset, scores, own_init, prepared = call(
        prepare_kernel,
        [
            (tall, BF16, "h"), (turned, BF16, "h"), (tall, F32, "h"), (full, BF16, "h"),
            ((HEAD, HEAD), F32, "h"), token,
        ],
        [(queries, "h"), (keys, "h"), (rates, "h"), (tkv, "h"), (init_weight, "h")],
        [
            vm(flat, BF16), vm(flat, BF16), vm((heads, n), F32), vm(pair, BF16), vm(tall, BF16),
            vm(turned, BF16), vm(tall, F32), vm(full, BF16),
        ],
        copies=2 + 7 * parts,
    )
    slab = (HEAD, 2 * HEAD)
    block = (HEAD, HEAD)
    whole, tree, factors = call(
        group_kernel,
        [(slab, F32, "v"), ((3, HEAD, 2 * HEAD), F32, "v"), ((6, HEAD, HEAD), F32, "v")],
        [(own_maps, "v")],
    )
    other_map = lax.ppermute(whole, "ctx", across)
    (sent,) = call(
        pair_kernel,
        [((PLANES, HEAD, 2 * HEAD), F32, "v")],
        [(whole, "v"), (other_map, "v"), (prepared, "v")],
    )
    pair_maps = swap(sent, far)
    starts, gain_row = call(
        start_kernel,
        [(square, F32, "v"), ((1, width), F32, "v")],
        [
            (own_maps, "v"), (tree, "v"), (pair_maps, "v"), (other_map, "v"), (own_init, "v"),
            (gain_row, "h"),
        ],
        copies=1,
    )
    weights = swap(starts, near)
    hidden, stats = call(
        hidden_kernel,
        [(flat, F32, "v"), ((n, HEAD), F32, "v")],
        [(qt, "v"), (offset, "v"), (cotangent, "v"), (gain_row, "v"), (weights, "v")],
    )
    other = lax.ppermute(stats, "tensor", [(0, 1), (1, 0)])
    normed, dz, local_grad = call(
        norm_kernel,
        [(flat, BF16, "h"), (flat, BF16, "h"), (square, F32, "h")],
        [
            (hidden, "v"), (cotangent, "v"), (gain_row, "v"), (stats, "v"), (other, "v"),
            (qt_turned, "v"),
        ],
        [vm(flat, BF16), vm(flat, BF16), vm(square, F32)],
        copies=3 * parts,
    )
    own_grads = swap(local_grad, near)
    grad_queries, dk_part, scaled_residual, queried = call(
        query_kernel,
        [(flat, BF16, "h"), (tall, BF16, "h"), (tall, BF16, "h"), token],
        [
            (queries, "h"), (keys, "h"), (rates, "h"), (tkv, "h"), (dz, "h"), (weights, "v"),
        ],
        [
            vm(flat, BF16), vm(flat, BF16), vm((heads, n), F32), vm(pair, BF16),
            vm(flat, BF16), vm(flat, BF16), vm(tall, BF16), vm(tall, BF16),
        ],
        copies=1 + 7 * parts,
    )
    u, tek, settled = call(
        adjoint_residual_kernel,
        [(tall, BF16, "h"), (tall, BF16, "h"), token],
        [
            (keys, "h"), (rates, "h"), (scores, "h"), (inverse, "h"), (cross, "h"), (dz, "h"),
        ],
        [
            vm(flat, BF16), vm((heads, n), F32), vm(full, BF16), vm(inner, BF16),
            vm(corner, BF16), vm(flat, BF16), vm(tall, BF16), vm(tall, BF16),
        ],
        copies=1 + 7 * parts,
    )
    steps = (PLANES, HEAD, HEAD)
    after, first, early, up = call(
        adjoint_kernel,
        [(steps, F32, "a"), (steps, F32, "a"), (block, F32, "a"), ((7, HEAD, HEAD), F32, "v")],
        [(pair_maps, "v"), (own_maps, "v"), (factors, "v"), (other_map, "v")],
    )
    whole, sums = call(
        gather_kernel,
        [(block, F32, "v"), ((6, HEAD, HEAD), F32, "v")],
        [(up, "v"), (own_grads, "v"), (queried, "v")],
    )
    other_grad = lax.ppermute(whole, "ctx", across)
    (sent,) = call(
        pair_gradient_kernel,
        [(steps, F32, "v")],
        [(early, "v"), (whole, "v"), (other_grad, "v"), (settled, "v")],
    )
    pair_grads = swap(sent, far)
    (ends,) = call(
        end_kernel,
        [((GROUP, HEAD + 8, HEAD), F32, "v")],
        [
            (after, "v"), (first, "v"), (own_maps, "v"), (factors, "v"), (own_grads, "v"),
            (sums, "v"), (other_map, "v"), (other_grad, "v"), (pair_grads, "v"),
        ],
        [vm(block, F32)],
    )
    adjoint = swap(ends, near)
    grad_keys, grad_values, grad_rates, grad_init = call(
        key_kernel,
        [(flat, BF16, "h"), (flat, BF16, "h"), ((heads, n), F32, "v"), ((heads, n), F32, "v")],
        [
            (keys, "v"), (rates, "v"), (tek, "v"), (scaled_residual, "v"), (u, "v"),
            (dk_part, "v"), (weights, "v"), (adjoint, "v"),
        ],
        [vm(flat, BF16), vm(flat, BF16)],
        copies=2 * parts,
    )
    return (normed, grad_queries, grad_keys, grad_values, grad_rates, grad_init)


def solution(mesh):
    in_specs = (
        P("ctx", "tensor"),
        P("ctx", "tensor"),
        P("ctx", "tensor"),
        P("tensor", "ctx"),
        P("tensor", None, None),
        P("tensor"),
        P("ctx", "tensor"),
    )
    out_specs = (
        P("ctx", "tensor"),
        P("ctx", "tensor"),
        P("ctx", "tensor"),
        P("ctx", "tensor"),
        P("tensor", "ctx"),
        P("tensor", "ctx"),
    )
    return jax.shard_map(local, mesh=mesh, in_specs=in_specs, out_specs=out_specs, check_vma=False)
```

```python
import jax
import jax.numpy as jnp
from jax import lax
from jax.experimental import pallas as pl
from jax.experimental.pallas import tpu as pltpu
from jax.sharding import PartitionSpec as P

HEAD = 128
MB = 16
EPSILON = 1e-06
GROUP = 8
PLANES = 4
F32 = jnp.float32
BF16 = jnp.bfloat16


def low(a):
    return a.astype(BF16)


def dot(a, b):
    return jnp.dot(a, b, preferred_element_type=F32)


def dot_nt(a, b):
    return lax.dot_general(a, b, (((1,), (1,)), ((), ())), preferred_element_type=F32)


def dot_tn(a, b):
    return lax.dot_general(a, b, (((0,), (0,)), ((), ())), preferred_element_type=F32)


def halves(a):
    high = low(a)
    return high, low(a - high.astype(F32))


def exact(a, b, product=dot):
    (ah, al), (bh, bl) = a, b
    return product(ah, bh) + (product(ah, bl) + product(al, bh))


def call(kernel, outs, args, scratch=(), copies=0, limit=24):
    spaces = {"s": pltpu.SMEM, "v": pltpu.VMEM, "h": pltpu.HBM, "a": pltpu.VMEM}
    values = [pltpu.with_memory_space_constraint(a, pltpu.HBM) if p in "ha" else a for a, p in args]
    results = [
        pltpu.HBM(shape, dtype) if p in "ha" else jax.ShapeDtypeStruct(shape, dtype)
        for shape, dtype, p in outs
    ]
    size = sum(a.size * a.dtype.itemsize for a in values)
    scratch = list(scratch)
    if copies:
        scratch.append(pltpu.SemaphoreType.DMA((copies,)))
    return pl.pallas_call(
        kernel,
        out_shape=results,
        in_specs=[pl.BlockSpec(memory_space=spaces[p]) for _, p in args],
        out_specs=[pl.BlockSpec(memory_space=spaces[p]) for _, _, p in outs],
        scratch_shapes=scratch,
        compiler_params=pltpu.CompilerParams(vmem_limit_bytes=limit * 2**20),
        cost_estimate=pl.CostEstimate(
            flops=2 * 10**9, bytes_accessed=2 * size, transcendentals=0
        ),
        name=kernel.__name__,
    )(*values)


class Copies:
    def __init__(self, semaphores):
        self.semaphores = semaphores
        self.started = []

    def start(self, source, target):
        copy = pltpu.make_async_copy(source, target, self.semaphores.at[len(self.started)])
        copy.start()
        self.started.append(copy)
        return copy


def columns(h):
    return slice(h * HEAD, (h + 1) * HEAD)


def span(first, last):
    return slice(first * HEAD, last * HEAD)


BATCH = 4


def map_kernel(
    k_hbm, v_hbm, e_hbm, ab_ref, t_hbm, n_hbm, tkv_hbm,
    k_ref, v_ref, e_ref, t_ref, n_ref, tkv_ref, sems,
):
    heads = e_ref.shape[0]
    half = t_ref.shape[-1]
    copies = Copies(sems)
    arrivals = []
    for first in range(0, heads, BATCH):
        part = span(first, first + BATCH)
        key = copies.start(k_hbm.at[:, part], k_ref.at[:, part])
        if first == 0:
            rates = copies.start(e_hbm, e_ref)
        arrivals.append((key, copies.start(v_hbm.at[:, part], v_ref.at[:, part])))
    row = lax.broadcasted_iota(jnp.int32, (half, half), 0)
    col = lax.broadcasted_iota(jnp.int32, (half, half), 1)
    eye = (row == col).astype(F32)
    masks = []
    width = MB
    while width < half:
        masks.append((row // (2 * width) == col // (2 * width)) & (row // width > col // width))
        width *= 2
    sent = []
    ks, es, blocks, crosses, scaled = [], [], [], [], []
    for first, (key, _) in zip(range(0, heads, BATCH), arrivals):
        key.wait()
        if first == 0:
            rates.wait()
        for h in range(first, first + BATCH):
            k = k_ref[:, columns(h)]
            e = e_ref[h : h + 1, :]
            top = -(dot_nt(k[:half], k[:half]) * e[:, :half])
            bottom = -(dot_nt(k[half:], k) * e)
            blocks += [top, bottom[:, half:]]
            crosses.append(low(bottom[:, :half]))
            ks.append(k)
            es.append(e)
    inverses = [low(eye + jnp.where(masks[0], b, 0.0)) for b in blocks]
    for mask in masks[1:]:
        mids = [low(dot(low(jnp.where(mask, b, 0.0)), t)) for b, t in zip(blocks, inverses)]
        inverses = [t + low(dot(t, m)) for t, m in zip(inverses, mids)]
    for h in range(heads):
        t_ref[h, 0] = inverses[2 * h]
        t_ref[h, 1] = inverses[2 * h + 1]
        n_ref[h] = crosses[h]
    sent.append(copies.start(t_ref, t_hbm))
    sent.append(copies.start(n_ref, n_hbm))
    for _, value in arrivals:
        value.wait()
    kvs = [jnp.concatenate([ks[h], v_ref[:, columns(h)]], axis=1) for h in range(heads)]
    tops = [low(dot(t, kv[:half])) for t, kv in zip(inverses[::2], kvs)]
    for h in range(heads):
        tkv_ref[h, :half] = tops[h]
    sent.append(copies.start(tkv_ref.at[:, :half], tkv_hbm.at[:, :half]))
    scaled = [low(jnp.transpose(k.astype(F32)) * e) for k, e in zip(ks, es)]
    mids = [low(kv[half:].astype(F32) + dot(c, x)) for kv, c, x in zip(kvs, crosses, tops)]
    bottoms = [low(dot(t, m)) for t, m in zip(inverses[1::2], mids)]
    for h in range(heads):
        tkv_ref[h, half:] = bottoms[h]
    sent.append(copies.start(tkv_ref.at[:, half:], tkv_hbm.at[:, half:]))
    for h in range(heads):
        ab = dot(scaled[h], tkv_ref[h])
        ab_ref[h, :, :HEAD] = eye - ab[:, :HEAD]
        ab_ref[h, :, HEAD:] = ab[:, HEAD:]
    for copy in sent:
        copy.wait()


def causal_scores(q, k, e):
    n = q.shape[0]
    row = lax.broadcasted_iota(jnp.int32, (n, n), 0)
    col = lax.broadcasted_iota(jnp.int32, (n, n), 1)
    return low(jnp.where(row >= col, dot_nt(q, k) * e, 0.0))


def prepare_kernel(
    q_hbm, k_hbm, e_hbm, tkv_hbm, init_hbm,
    qt_hbm, qtt_hbm, c_hbm, se_hbm, own_hbm, token_ref,
    q_ref, k_ref, e_ref, tkv_ref, qt_ref, qtt_ref, c_ref, se_ref, sems,
):
    heads = e_ref.shape[0]
    copies = Copies(sems)
    sent = [copies.start(init_hbm.at[lax.axis_index("ctx") % GROUP], own_hbm)]
    rates = copies.start(e_hbm, e_ref)
    arrivals = []
    for first in range(0, heads, BATCH):
        part = slice(first, first + BATCH)
        flat = span(first, first + BATCH)
        arrivals.append((
            copies.start(q_hbm.at[:, flat], q_ref.at[:, flat]),
            copies.start(k_hbm.at[:, flat], k_ref.at[:, flat]),
            copies.start(tkv_hbm.at[part], tkv_ref.at[part]),
        ))
    token_ref[...] = jnp.zeros_like(token_ref)
    rates.wait()
    for first, arrival in zip(range(0, heads, BATCH), arrivals):
        batch = range(first, first + BATCH)
        for copy in arrival:
            copy.wait()
        scores = [
            causal_scores(q_ref[:, columns(h)], k_ref[:, columns(h)], e_ref[h : h + 1, :])
            for h in batch
        ]
        for h, se in zip(batch, scores):
            se_ref[h] = se
            sx = dot(se, tkv_ref[h])
            qt = q_ref[:, columns(h)].astype(F32) - sx[:, :HEAD]
            qt_ref[h] = low(qt)
            qtt_ref[h] = low(jnp.transpose(qt))
            c_ref[h] = sx[:, HEAD:]
        part = slice(first, first + BATCH)
        for source, target in (
            (qt_ref, qt_hbm), (qtt_ref, qtt_hbm), (c_ref, c_hbm), (se_ref, se_hbm)
        ):
            sent.append(copies.start(source.at[part], target.at[part]))
    for copy in sent:
        copy.wait()


def adjoint_residual_kernel(
    k_hbm, e_hbm, se_hbm, t_hbm, n_hbm, dz_hbm, u_hbm, tek_hbm, token_ref,
    k_ref, e_ref, se_ref, t_ref, n_ref, dz_ref, u_ref, tek_ref, sems,
):
    heads, n = e_ref.shape
    half = n // 2
    copies = Copies(sems)
    rates = copies.start(e_hbm, e_ref)
    arrivals = []
    for first in range(0, heads, BATCH):
        part = slice(first, first + BATCH)
        flat = span(first, first + BATCH)
        arrivals.append((
            copies.start(t_hbm.at[part], t_ref.at[part]),
            copies.start(n_hbm.at[part], n_ref.at[part]),
            copies.start(k_hbm.at[:, flat], k_ref.at[:, flat]),
            copies.start(se_hbm.at[part], se_ref.at[part]),
            copies.start(dz_hbm.at[:, flat], dz_ref.at[:, flat]),
        ))
    token_ref[...] = jnp.zeros_like(token_ref)
    rates.wait()
    sent = []
    for first, arrival in zip(range(0, heads, BATCH), arrivals):
        batch = range(first, first + BATCH)
        wides = [jnp.transpose(jnp.broadcast_to(e_ref[h : h + 1, :], (HEAD, n))) for h in batch]
        for copy in arrival:
            copy.wait()
        mids = [low(dot(n_ref[h], t_ref[h, 0])) for h in batch]
        ys = [
            jnp.concatenate(
                [
                    low(dot_tn(se_ref[h], dz_ref[:, columns(h)])),
                    low(k_ref[:, columns(h)].astype(F32) * wide),
                ],
                axis=1,
            )
            for h, wide in zip(batch, wides)
        ]
        lowers = [dot_tn(t_ref[h, 1], y[half:]) for h, y in zip(batch, ys)]
        uppers = [
            dot_tn(t_ref[h, 0], y[:half]) + dot_tn(m, low(x))
            for h, y, m, x in zip(batch, ys, mids, lowers)
        ]
        for h, upper, lower in zip(batch, uppers, lowers):
            u_ref[h, :half] = low(-upper[:, :HEAD])
            u_ref[h, half:] = low(-lower[:, :HEAD])
            tek_ref[h, :half] = low(upper[:, HEAD:])
            tek_ref[h, half:] = low(lower[:, HEAD:])
        part = slice(first, first + BATCH)
        for source, target in ((u_ref, u_hbm), (tek_ref, tek_hbm)):
            sent.append(copies.start(source.at[part], target.at[part]))
    for copy in sent:
        copy.wait()


def compose(early, late):
    wide = exact(halves(late[:, :HEAD]), halves(early))
    return jnp.concatenate([wide[:, :HEAD], wide[:, HEAD:] + late[:, HEAD:]], axis=1)


def broadcast(copies, source, targets):
    sent = [copies.start(source, targets.at[i]) for i in range(GROUP)]
    for copy in sent:
        copy.wait()


def level():
    group = lax.axis_index("ctx") // GROUP
    return group // 2, group % 2


def group_kernel(ab_ref, whole_ref, tree_ref, factors_ref):
    pairs = [compose(ab_ref[2 * i], ab_ref[2 * i + 1]) for i in range(4)]
    quads = [compose(pairs[2 * i], pairs[2 * i + 1]) for i in range(2)]
    for i, a in enumerate(pairs + quads):
        factors_ref[i] = a[:, :HEAD]
    for i, a in enumerate((pairs[0], pairs[2], quads[0])):
        tree_ref[i] = a
    whole_ref[...] = compose(quads[0], quads[1])


def pair_kernel(own_ref, other_ref, token_ref, all_ref):
    _, late = level()
    own, other = own_ref[...], other_ref[...]
    early = jnp.where(late == 1, other, own)
    pair = compose(early, jnp.where(late == 1, own, other))
    for i in range(PLANES):
        all_ref[i] = pair


def apply_map(ab, w):
    return exact(halves(ab[:, :HEAD]), halves(w)) + ab[:, HEAD:]


def start_kernel(
    ab_ref, tree_ref, pairs_ref, other_ref, init_ref, gain_hbm, w_ref, gain_ref, sems
):
    weight = Copies(sems).start(gain_hbm, gain_ref)
    plane, late = level()
    w0 = lax.fori_loop(0, plane, lambda z, w: apply_map(pairs_ref[z], w), init_ref[...])
    w0 = lax.fori_loop(0, late, lambda _, w: apply_map(other_ref[...], w), w0)
    w4 = apply_map(tree_ref[2], w0)
    w2 = apply_map(tree_ref[0], w0)
    w6 = apply_map(tree_ref[1], w4)
    for i, w in zip((0, 2, 4, 6), (w0, w2, w4, w6)):
        w_ref[i] = w
        w_ref[i + 1] = apply_map(ab_ref[i], w)
    weight.wait()


def adjoint_kernel(
    pairs_ref, ab_ref, factors_ref, other_ref, after_ref, first_ref, early_ref, up_ref
):
    eye = (
        lax.broadcasted_iota(jnp.int32, (HEAD, HEAD), 0)
        == lax.broadcasted_iota(jnp.int32, (HEAD, HEAD), 1)
    ).astype(F32)
    first = after = eye
    plane, late = level()
    own = exact(halves(factors_ref[5]), halves(factors_ref[4]))
    early_ref[...] = jnp.transpose(jnp.where(late == 1, other_ref[:, :HEAD], own))
    for i in range(4):
        up_ref[i] = jnp.transpose(ab_ref[2 * i, :, :HEAD])
    for i, a in enumerate((0, 2, 4)):
        up_ref[4 + i] = jnp.transpose(factors_ref[a])
    for z in range(PLANES):
        first_ref[z] = first
        later = z > plane
        after_ref[z] = jnp.where(later, after, 0.0)
        if z < PLANES - 1:
            step = halves(pairs_ref[z, :, :HEAD])
            first = exact(halves(first), step, dot_nt)
            after = jnp.where(later, exact(halves(after), step, dot_nt), eye)


def hidden_kernel(qt_ref, c_ref, cot_ref, gain_ref, w_ref, z_ref, stats_ref):
    heads, n = qt_ref.shape[:2]
    squares = jnp.zeros((n, HEAD), F32)
    products = jnp.zeros((n, HEAD), F32)
    for h in range(heads):
        z = dot(qt_ref[h], low(w_ref[h])) + c_ref[h]
        z_ref[:, columns(h)] = z
        squares += z * z
        products += z * (cot_ref[:, columns(h)].astype(F32) * gain_ref[:, columns(h)])
    lane = lax.broadcasted_iota(jnp.int32, (n, HEAD), 1)
    stats_ref[...] = jnp.where(
        lane < HEAD // 2,
        jnp.sum(squares, axis=1, keepdims=True),
        jnp.sum(products, axis=1, keepdims=True),
    )


def norm_kernel(
    z_ref, cot_ref, gain_ref, own_ref, other_ref, qtt_ref,
    normed_hbm, dz_hbm, g_hbm, normed_ref, dz_ref, g_ref, sems,
):
    heads = qtt_ref.shape[0]
    width = 2 * z_ref.shape[1]
    copies = Copies(sems)
    stats = own_ref[...] + other_ref[...]
    inv = lax.rsqrt(stats[:, 0:1] / width + EPSILON)
    shift = inv * inv * inv * stats[:, HEAD // 2 : HEAD // 2 + 1] / width
    for h in range(heads):
        go = cot_ref[:, columns(h)].astype(F32) * gain_ref[:, columns(h)]
        dz = low(inv * go - z_ref[:, columns(h)] * shift)
        dz_ref[:, columns(h)] = dz
        g_ref[h] = dot(qtt_ref[h], dz)
        normed_ref[:, columns(h)] = low(z_ref[:, columns(h)] * inv * gain_ref[:, columns(h)])
        if h % BATCH == BATCH - 1:
            part = slice(h + 1 - BATCH, h + 1)
            flat = span(h + 1 - BATCH, h + 1)
            copies.start(g_ref.at[part], g_hbm.at[part])
            copies.start(dz_ref.at[:, flat], dz_hbm.at[:, flat])
            copies.start(normed_ref.at[:, flat], normed_hbm.at[:, flat])
    for copy in copies.started:
        copy.wait()


def query_kernel(
    q_hbm, k_hbm, e_hbm, tkv_hbm, dz_hbm, w_ref, dq_hbm, dk_hbm, er_hbm, token_ref,
    q_ref, k_ref, e_ref, tkv_ref, dz_ref, dq_ref, dk_ref, er_ref, sems,
):
    n = k_ref.shape[0]
    heads = e_ref.shape[0]
    copies = Copies(sems)
    rates = copies.start(e_hbm, e_ref)
    arrivals = []
    for first in range(0, heads, BATCH):
        part = slice(first, first + BATCH)
        flat = span(first, first + BATCH)
        arrivals.append((
            copies.start(tkv_hbm.at[part], tkv_ref.at[part]),
            copies.start(dz_hbm.at[:, flat], dz_ref.at[:, flat]),
            copies.start(k_hbm.at[:, flat], k_ref.at[:, flat]),
            copies.start(q_hbm.at[:, flat], q_ref.at[:, flat]),
        ))
    row = lax.broadcasted_iota(jnp.int32, (n, n), 0)
    col = lax.broadcasted_iota(jnp.int32, (n, n), 1)
    causal = row >= col
    token_ref[...] = jnp.zeros_like(token_ref)
    rates.wait()
    sent = []
    for first, arrival in zip(range(0, heads, BATCH), arrivals):
        batch = range(first, first + BATCH)
        ws = [low(w_ref[h]) for h in batch]
        rates_wide = [
            jnp.transpose(jnp.broadcast_to(e_ref[h : h + 1, :], (HEAD, n))) for h in batch
        ]
        for copy in arrival:
            copy.wait()
        for h, w, wide in zip(batch, ws, rates_wide):
            r = dot(tkv_ref[h, :, :HEAD], w) - tkv_ref[h, :, HEAD:].astype(F32)
            er_ref[h] = low(r * wide)
        dss = [
            low(jnp.where(causal, -dot_nt(dz_ref[:, columns(h)], er_ref[h]), 0.0)) for h in batch
        ]
        for h, w, ds in zip(batch, ws, dss):
            dq_ref[:, columns(h)] = low(
                dot_nt(dz_ref[:, columns(h)], w) + dot(ds, k_ref[:, columns(h)])
            )
            dk_ref[h] = low(dot_tn(ds, q_ref[:, columns(h)]))
        part = slice(first, first + BATCH)
        flat = span(first, first + BATCH)
        sent.append(copies.start(dq_ref.at[:, flat], dq_hbm.at[:, flat]))
        for source, target in ((dk_ref, dk_hbm), (er_ref, er_hbm)):
            sent.append(copies.start(source.at[part], target.at[part]))
    for copy in sent:
        copy.wait()


def transposed_map(a, later, own):
    return exact(halves(a), halves(later), dot_tn) + own


def turned_map(a, later, own):
    return exact(halves(a), halves(later)) + own


def gather_kernel(up_ref, g_ref, token_ref, whole_ref, sums_ref):
    pairs = [turned_map(up_ref[i], g_ref[2 * i + 1], g_ref[2 * i]) for i in range(4)]
    quads = [turned_map(up_ref[4 + i], pairs[2 * i + 1], pairs[2 * i]) for i in range(2)]
    for i, a in enumerate(pairs + quads):
        sums_ref[i] = a
    whole_ref[...] = turned_map(up_ref[6], quads[1], quads[0])


def pair_gradient_kernel(early_ref, own_ref, other_ref, token_ref, all_ref):
    _, late = level()
    own, other = own_ref[...], other_ref[...]
    pair = turned_map(
        early_ref[...], jnp.where(late == 1, own, other), jnp.where(late == 1, other, own)
    )
    for i in range(PLANES):
        all_ref[i] = pair


def end_kernel(
    after_ref, first_ref, ab_ref, factors_ref, g_ref, sums_ref, other_map_ref, other_ref, later_ref,
    d_ref, init_ref,
):
    parts = [halves(later_ref[z]) for z in range(PLANES)]
    _, late = level()
    end = exact(halves(after_ref[1]), parts[1])
    for z in range(2, PLANES):
        end += exact(halves(after_ref[z]), parts[z])
    inner = transposed_map(other_map_ref[:, :HEAD], end, other_ref[...])
    d7 = jnp.where(late == 1, end, inner)
    d3 = transposed_map(factors_ref[5], d7, sums_ref[5])
    d5 = transposed_map(factors_ref[3], d7, sums_ref[3])
    d1 = transposed_map(factors_ref[1], d3, sums_ref[1])
    start = later_ref[0]
    for z in range(1, PLANES):
        start += exact(halves(first_ref[z]), parts[z])
    init_ref[...] = start
    rows = init_ref[pl.ds(pl.multiple_of(lax.axis_index("ctx") // GROUP * 16, 16), 16), :]
    for i, d in zip((7, 5, 3, 1), (d7, d5, d3, d1)):
        d_ref[i, :HEAD, :] = d
        d_ref[i - 1, :HEAD, :] = transposed_map(ab_ref[i, :, :HEAD], d, g_ref[i])
    for i in range(GROUP):
        d_ref[i, HEAD:, :] = jnp.zeros((8, HEAD), F32)
        d_ref[i, HEAD : HEAD + 2, :] = rows[2 * i : 2 * i + 2]


def key_kernel(
    k_ref, e_ref, tek_ref, er_ref, u_ref, dkp_ref, w_ref, d_ref,
    dk_hbm, dv_hbm, de_ref, gi_ref, dk_ref, dv_ref, sems,
):
    n = k_ref.shape[0]
    heads = e_ref.shape[0]
    copies = Copies(sems)
    row = lax.broadcasted_iota(jnp.int32, (n, n), 0) // MB
    col = lax.broadcasted_iota(jnp.int32, (n, n), 1) // MB
    before = row > col
    after = row < col
    ones = jnp.ones((8, HEAD), BF16)
    for h in range(heads):
        gi_ref[h : h + 1, :HEAD] = d_ref[h, HEAD : HEAD + 1, :]
        gi_ref[h : h + 1, HEAD:] = d_ref[h, HEAD + 1 : HEAD + 2, :]
    for first in range(0, heads, heads):
        batch = range(first, first + heads)
        ds = [low(d_ref[h, :HEAD, :]) for h in batch]
        both = [jnp.concatenate([low(w_ref[h]), -d], axis=1) for h, d in zip(batch, ds)]
        ers = [er_ref[h] for h in batch]
        us = [u_ref[h].astype(F32) - dot(tek_ref[h], d) for h, d in zip(batch, ds)]
        lows = [low(u) for u in us]
        for h, u in zip(batch, lows):
            dv_ref[:, columns(h)] = -u
        flat = span(first, first + heads)
        copies.start(dv_ref.at[:, flat], dv_hbm.at[:, flat])
        ps = [low(u * er.astype(F32)) for u, er in zip(us, ers)]
        xs = [
            low(jnp.where(before, dot_nt(u, er), jnp.where(after, dot_nt(er, u), 0.0)))
            for u, er in zip(lows, ers)
        ]
        dks = [
            dkp_ref[h].astype(F32) + dot_nt(jnp.concatenate([u, er], axis=1), b)
            for h, u, er, b in zip(batch, lows, ers, both)
        ]
        for h, dk, x, p in zip(batch, dks, xs, ps):
            e = e_ref[h : h + 1, :]
            dk_ref[:, columns(h)] = low(dk - dot(x, k_ref[:, columns(h)]))
            if h % 2 == 1:
                flat = span(h - 1, h + 1)
                copies.start(dk_ref.at[:, flat], dk_hbm.at[:, flat])
            de_ref[h : h + 1, :] = dot_nt(ones, p)[0:1] / (e * e)
    for copy in copies.started:
        copy.wait()


def local(queries, keys, values, rates, init_weight, gain, cotangent):
    n, width = keys.shape
    heads = width // HEAD
    count = lax.axis_size("ctx") // GROUP
    near = [[g * GROUP + i for i in range(GROUP)] for g in range(count)]
    stride = 2 * GROUP
    far = [[z * stride + i for z in range(PLANES)] for i in range(stride)]
    across = [(i, i + GROUP if i % stride < GROUP else i - GROUP) for i in range(count * GROUP)]
    gain_row = gain.reshape(1, width)

    def swap(a, groups):
        return lax.all_to_all(a, "ctx", 0, 0, axis_index_groups=groups)

    square = (GROUP, HEAD, HEAD)
    wide = (GROUP, HEAD, 2 * HEAD)
    tall = (heads, n, HEAD)
    full = (heads, n, n)
    flat = (n, width)
    token = ((8, HEAD), F32, "v")
    parts = heads // BATCH
    vm = pltpu.VMEM

    half = n // 2
    inner = (heads, 2, half, half)
    corner = (heads, half, half)
    pair = (heads, n, 2 * HEAD)
    turned = (heads, HEAD, n)
    maps, inverse, cross, tkv = call(
        map_kernel,
        [
            (wide, F32, "v"), (inner, BF16, "h"), (corner, BF16, "h"),
            ((heads, n, 2 * HEAD), BF16, "h"),
        ],
        [(keys, "h"), (values, "h"), (rates, "h")],
        [
            vm(flat, BF16), vm(flat, BF16), vm((heads, n), F32),
            vm(inner, BF16), vm(corner, BF16), vm((heads, n, 2 * HEAD), BF16),
        ],
        copies=5 + 2 * parts,
    )
    own_maps = swap(maps, near)
    qt, qt_turned, offset, scores, own_init, prepared = call(
        prepare_kernel,
        [
            (tall, BF16, "h"), (turned, BF16, "h"), (tall, F32, "h"), (full, BF16, "h"),
            ((HEAD, HEAD), F32, "h"), token,
        ],
        [(queries, "h"), (keys, "h"), (rates, "h"), (tkv, "h"), (init_weight, "h")],
        [
            vm(flat, BF16), vm(flat, BF16), vm((heads, n), F32), vm(pair, BF16), vm(tall, BF16),
            vm(turned, BF16), vm(tall, F32), vm(full, BF16),
        ],
        copies=2 + 7 * parts,
    )
    slab = (HEAD, 2 * HEAD)
    block = (HEAD, HEAD)
    whole, tree, factors = call(
        group_kernel,
        [(slab, F32, "v"), ((3, HEAD, 2 * HEAD), F32, "v"), ((6, HEAD, HEAD), F32, "v")],
        [(own_maps, "v")],
    )
    other_map = lax.ppermute(whole, "ctx", across)
    (sent,) = call(
        pair_kernel,
        [((PLANES, HEAD, 2 * HEAD), F32, "v")],
        [(whole, "v"), (other_map, "v"), (prepared, "v")],
    )
    pair_maps = swap(sent, far)
    starts, gain_row = call(
        start_kernel,
        [(square, F32, "v"), ((1, width), F32, "v")],
        [
            (own_maps, "v"), (tree, "v"), (pair_maps, "v"), (other_map, "v"), (own_init, "v"),
            (gain_row, "h"),
        ],
        copies=1,
    )
    weights = swap(starts, near)
    hidden, stats = call(
        hidden_kernel,
        [(flat, F32, "v"), ((n, HEAD), F32, "v")],
        [(qt, "v"), (offset, "v"), (cotangent, "v"), (gain_row, "v"), (weights, "v")],
    )
    other = lax.ppermute(stats, "tensor", [(0, 1), (1, 0)])
    normed, dz, local_grad = call(
        norm_kernel,
        [(flat, BF16, "h"), (flat, BF16, "h"), (square, F32, "h")],
        [
            (hidden, "v"), (cotangent, "v"), (gain_row, "v"), (stats, "v"), (other, "v"),
            (qt_turned, "v"),
        ],
        [vm(flat, BF16), vm(flat, BF16), vm(square, F32)],
        copies=3 * parts,
    )
    own_grads = swap(local_grad, near)
    grad_queries, dk_part, scaled_residual, queried = call(
        query_kernel,
        [(flat, BF16, "h"), (tall, BF16, "h"), (tall, BF16, "h"), token],
        [
            (queries, "h"), (keys, "h"), (rates, "h"), (tkv, "h"), (dz, "h"), (weights, "v"),
        ],
        [
            vm(flat, BF16), vm(flat, BF16), vm((heads, n), F32), vm(pair, BF16),
            vm(flat, BF16), vm(flat, BF16), vm(tall, BF16), vm(tall, BF16),
        ],
        copies=1 + 7 * parts,
    )
    u, tek, settled = call(
        adjoint_residual_kernel,
        [(tall, BF16, "h"), (tall, BF16, "h"), token],
        [
            (keys, "h"), (rates, "h"), (scores, "h"), (inverse, "h"), (cross, "h"), (dz, "h"),
        ],
        [
            vm(flat, BF16), vm((heads, n), F32), vm(full, BF16), vm(inner, BF16),
            vm(corner, BF16), vm(flat, BF16), vm(tall, BF16), vm(tall, BF16),
        ],
        copies=1 + 7 * parts,
    )
    steps = (PLANES, HEAD, HEAD)
    after, first, early, up = call(
        adjoint_kernel,
        [(steps, F32, "a"), (steps, F32, "a"), (block, F32, "a"), ((7, HEAD, HEAD), F32, "v")],
        [(pair_maps, "v"), (own_maps, "v"), (factors, "v"), (other_map, "v")],
    )
    whole, sums = call(
        gather_kernel,
        [(block, F32, "v"), ((6, HEAD, HEAD), F32, "v")],
        [(up, "v"), (own_grads, "v"), (queried, "v")],
    )
    other_grad = lax.ppermute(whole, "ctx", across)
    (sent,) = call(
        pair_gradient_kernel,
        [(steps, F32, "v")],
        [(early, "v"), (whole, "v"), (other_grad, "v"), (settled, "v")],
    )
    pair_grads = swap(sent, far)
    (ends,) = call(
        end_kernel,
        [((GROUP, HEAD + 8, HEAD), F32, "v")],
        [
            (after, "v"), (first, "v"), (own_maps, "v"), (factors, "v"), (own_grads, "v"),
            (sums, "v"), (other_map, "v"), (other_grad, "v"), (pair_grads, "v"),
        ],
        [vm(block, F32)],
    )
    adjoint = swap(ends, near)
    grad_keys, grad_values, grad_rates, grad_init = call(
        key_kernel,
        [(flat, BF16, "h"), (flat, BF16, "h"), ((heads, n), F32, "v"), ((heads, n), F32, "v")],
        [
            (keys, "v"), (rates, "v"), (tek, "v"), (scaled_residual, "v"), (u, "v"),
            (dk_part, "v"), (weights, "v"), (adjoint, "v"),
        ],
        [vm(flat, BF16), vm(flat, BF16)],
        copies=1 + heads // 2,
    )
    return (normed, grad_queries, grad_keys, grad_values, grad_rates, grad_init)


def solution(mesh):
    in_specs = (
        P("ctx", "tensor"),
        P("ctx", "tensor"),
        P("ctx", "tensor"),
        P("tensor", "ctx"),
        P("tensor", None, None),
        P("tensor"),
        P("ctx", "tensor"),
    )
    out_specs = (
        P("ctx", "tensor"),
        P("ctx", "tensor"),
        P("ctx", "tensor"),
        P("ctx", "tensor"),
        P("tensor", "ctx"),
        P("tensor", "ctx"),
    )
    return jax.shard_map(local, mesh=mesh, in_specs=in_specs, out_specs=out_specs, check_vma=False)
```

```python
import jax
import jax.numpy as jnp
from jax import lax
from jax.experimental import pallas as pl
from jax.experimental.pallas import tpu as pltpu
from jax.sharding import PartitionSpec as P

HEAD = 128
MB = 16
EPSILON = 1e-06
GROUP = 8
PLANES = 4
F32 = jnp.float32
BF16 = jnp.bfloat16


def low(a):
    return a.astype(BF16)


def dot(a, b):
    return jnp.dot(a, b, preferred_element_type=F32)


def dot_nt(a, b):
    return lax.dot_general(a, b, (((1,), (1,)), ((), ())), preferred_element_type=F32)


def dot_tn(a, b):
    return lax.dot_general(a, b, (((0,), (0,)), ((), ())), preferred_element_type=F32)


def halves(a):
    high = low(a)
    return high, low(a - high.astype(F32))


def exact(a, b, product=dot):
    (ah, al), (bh, bl) = a, b
    return product(ah, bh) + (product(ah, bl) + product(al, bh))


def call(kernel, outs, args, scratch=(), copies=0, limit=24):
    spaces = {"s": pltpu.SMEM, "v": pltpu.VMEM, "h": pltpu.HBM, "a": pltpu.VMEM}
    values = [pltpu.with_memory_space_constraint(a, pltpu.HBM) if p in "ha" else a for a, p in args]
    results = [
        pltpu.HBM(shape, dtype) if p in "ha" else jax.ShapeDtypeStruct(shape, dtype)
        for shape, dtype, p in outs
    ]
    size = sum(a.size * a.dtype.itemsize for a in values)
    scratch = list(scratch)
    if copies:
        scratch.append(pltpu.SemaphoreType.DMA((copies,)))
    return pl.pallas_call(
        kernel,
        out_shape=results,
        in_specs=[pl.BlockSpec(memory_space=spaces[p]) for _, p in args],
        out_specs=[pl.BlockSpec(memory_space=spaces[p]) for _, _, p in outs],
        scratch_shapes=scratch,
        compiler_params=pltpu.CompilerParams(vmem_limit_bytes=limit * 2**20),
        cost_estimate=pl.CostEstimate(
            flops=2 * 10**9, bytes_accessed=2 * size, transcendentals=0
        ),
        name=kernel.__name__,
    )(*values)


class Copies:
    def __init__(self, semaphores):
        self.semaphores = semaphores
        self.started = []

    def start(self, source, target):
        copy = pltpu.make_async_copy(source, target, self.semaphores.at[len(self.started)])
        copy.start()
        self.started.append(copy)
        return copy


def columns(h):
    return slice(h * HEAD, (h + 1) * HEAD)


def span(first, last):
    return slice(first * HEAD, last * HEAD)


BATCH = 4


def map_kernel(
    k_hbm, v_hbm, e_hbm, ab_ref, t_hbm, n_hbm, tkv_hbm,
    k_ref, v_ref, e_ref, t_ref, n_ref, tkv_ref, sems,
):
    heads = e_ref.shape[0]
    half = t_ref.shape[-1]
    copies = Copies(sems)
    arrivals = []
    for first in range(0, heads, BATCH):
        part = span(first, first + BATCH)
        key = copies.start(k_hbm.at[:, part], k_ref.at[:, part])
        if first == 0:
            rates = copies.start(e_hbm, e_ref)
        arrivals.append((key, copies.start(v_hbm.at[:, part], v_ref.at[:, part])))
    row = lax.broadcasted_iota(jnp.int32, (half, half), 0)
    col = lax.broadcasted_iota(jnp.int32, (half, half), 1)
    eye = (row == col).astype(F32)
    masks = []
    width = MB
    while width < half:
        masks.append((row // (2 * width) == col // (2 * width)) & (row // width > col // width))
        width *= 2
    sent = []
    ks, es, blocks, crosses, scaled = [], [], [], [], []
    for first, (key, _) in zip(range(0, heads, BATCH), arrivals):
        key.wait()
        if first == 0:
            rates.wait()
        for h in range(first, first + BATCH):
            k = k_ref[:, columns(h)]
            e = e_ref[h : h + 1, :]
            top = -(dot_nt(k[:half], k[:half]) * e[:, :half])
            bottom = -(dot_nt(k[half:], k) * e)
            blocks += [top, bottom[:, half:]]
            crosses.append(low(bottom[:, :half]))
            ks.append(k)
            es.append(e)
    inverses = [low(eye + jnp.where(masks[0], b, 0.0)) for b in blocks]
    for mask in masks[1:]:
        mids = [low(dot(low(jnp.where(mask, b, 0.0)), t)) for b, t in zip(blocks, inverses)]
        inverses = [t + low(dot(t, m)) for t, m in zip(inverses, mids)]
    for h in range(heads):
        t_ref[h, 0] = inverses[2 * h]
        t_ref[h, 1] = inverses[2 * h + 1]
        n_ref[h] = crosses[h]
    sent.append(copies.start(t_ref, t_hbm))
    sent.append(copies.start(n_ref, n_hbm))
    for _, value in arrivals:
        value.wait()
    kvs = [jnp.concatenate([ks[h], v_ref[:, columns(h)]], axis=1) for h in range(heads)]
    tops = [low(dot(t, kv[:half])) for t, kv in zip(inverses[::2], kvs)]
    for h in range(heads):
        tkv_ref[h, :half] = tops[h]
    sent.append(copies.start(tkv_ref.at[:, :half], tkv_hbm.at[:, :half]))
    scaled = [low(jnp.transpose(k.astype(F32)) * e) for k, e in zip(ks, es)]
    mids = [low(kv[half:].astype(F32) + dot(c, x)) for kv, c, x in zip(kvs, crosses, tops)]
    bottoms = [low(dot(t, m)) for t, m in zip(inverses[1::2], mids)]
    for h in range(heads):
        tkv_ref[h, half:] = bottoms[h]
    sent.append(copies.start(tkv_ref.at[:, half:], tkv_hbm.at[:, half:]))
    for h in range(heads):
        ab = dot(scaled[h], tkv_ref[h])
        ab_ref[h, :, :HEAD] = eye - ab[:, :HEAD]
        ab_ref[h, :, HEAD:] = ab[:, HEAD:]
    for copy in sent:
        copy.wait()


def causal_scores(q, k, e):
    n = q.shape[0]
    row = lax.broadcasted_iota(jnp.int32, (n, n), 0)
    col = lax.broadcasted_iota(jnp.int32, (n, n), 1)
    return low(jnp.where(row >= col, dot_nt(q, k) * e, 0.0))


def prepare_kernel(
    q_hbm, k_hbm, e_hbm, tkv_hbm, init_hbm,
    qt_hbm, qtt_hbm, c_hbm, se_hbm, own_hbm, token_ref,
    q_ref, k_ref, e_ref, tkv_ref, qt_ref, qtt_ref, c_ref, se_ref, sems,
):
    heads = e_ref.shape[0]
    copies = Copies(sems)
    sent = [copies.start(init_hbm.at[lax.axis_index("ctx") % GROUP], own_hbm)]
    rates = copies.start(e_hbm, e_ref)
    arrivals = []
    for first in range(0, heads, BATCH):
        part = slice(first, first + BATCH)
        flat = span(first, first + BATCH)
        arrivals.append((
            copies.start(q_hbm.at[:, flat], q_ref.at[:, flat]),
            copies.start(k_hbm.at[:, flat], k_ref.at[:, flat]),
            copies.start(tkv_hbm.at[part], tkv_ref.at[part]),
        ))
    token_ref[...] = jnp.zeros_like(token_ref)
    rates.wait()
    for first, arrival in zip(range(0, heads, BATCH), arrivals):
        batch = range(first, first + BATCH)
        for copy in arrival:
            copy.wait()
        scores = [
            causal_scores(q_ref[:, columns(h)], k_ref[:, columns(h)], e_ref[h : h + 1, :])
            for h in batch
        ]
        for h, se in zip(batch, scores):
            se_ref[h] = se
            sx = dot(se, tkv_ref[h])
            qt = q_ref[:, columns(h)].astype(F32) - sx[:, :HEAD]
            qt_ref[h] = low(qt)
            qtt_ref[h] = low(jnp.transpose(qt))
            c_ref[h] = sx[:, HEAD:]
        part = slice(first, first + BATCH)
        for source, target in (
            (qt_ref, qt_hbm), (qtt_ref, qtt_hbm), (c_ref, c_hbm), (se_ref, se_hbm)
        ):
            sent.append(copies.start(source.at[part], target.at[part]))
    for copy in sent:
        copy.wait()


def adjoint_residual_kernel(
    k_hbm, e_hbm, se_hbm, t_hbm, n_hbm, dz_hbm, u_hbm, tek_hbm, token_ref,
    k_ref, e_ref, se_ref, t_ref, n_ref, dz_ref, u_ref, tek_ref, sems,
):
    heads, n = e_ref.shape
    half = n // 2
    copies = Copies(sems)
    rates = copies.start(e_hbm, e_ref)
    arrivals = []
    for first in range(0, heads, BATCH):
        part = slice(first, first + BATCH)
        flat = span(first, first + BATCH)
        arrivals.append((
            copies.start(t_hbm.at[part], t_ref.at[part]),
            copies.start(n_hbm.at[part], n_ref.at[part]),
            copies.start(k_hbm.at[:, flat], k_ref.at[:, flat]),
            copies.start(se_hbm.at[part], se_ref.at[part]),
            copies.start(dz_hbm.at[:, flat], dz_ref.at[:, flat]),
        ))
    token_ref[...] = jnp.zeros_like(token_ref)
    rates.wait()
    sent = []
    for first, arrival in zip(range(0, heads, BATCH), arrivals):
        batch = range(first, first + BATCH)
        wides = [jnp.transpose(jnp.broadcast_to(e_ref[h : h + 1, :], (HEAD, n))) for h in batch]
        for copy in arrival:
            copy.wait()
        mids = [low(dot(n_ref[h], t_ref[h, 0])) for h in batch]
        ys = [
            jnp.concatenate(
                [
                    low(dot_tn(se_ref[h], dz_ref[:, columns(h)])),
                    low(k_ref[:, columns(h)].astype(F32) * wide),
                ],
                axis=1,
            )
            for h, wide in zip(batch, wides)
        ]
        lowers = [dot_tn(t_ref[h, 1], y[half:]) for h, y in zip(batch, ys)]
        uppers = [
            dot_tn(t_ref[h, 0], y[:half]) + dot_tn(m, low(x))
            for h, y, m, x in zip(batch, ys, mids, lowers)
        ]
        for h, upper, lower in zip(batch, uppers, lowers):
            u_ref[h, :half] = low(-upper[:, :HEAD])
            u_ref[h, half:] = low(-lower[:, :HEAD])
            tek_ref[h, :half] = low(upper[:, HEAD:])
            tek_ref[h, half:] = low(lower[:, HEAD:])
        part = slice(first, first + BATCH)
        for source, target in ((u_ref, u_hbm), (tek_ref, tek_hbm)):
            sent.append(copies.start(source.at[part], target.at[part]))
    for copy in sent:
        copy.wait()


def compose(early, late):
    wide = exact(halves(late[:, :HEAD]), halves(early))
    return jnp.concatenate([wide[:, :HEAD], wide[:, HEAD:] + late[:, HEAD:]], axis=1)


def broadcast(copies, source, targets):
    sent = [copies.start(source, targets.at[i]) for i in range(GROUP)]
    for copy in sent:
        copy.wait()


def level():
    group = lax.axis_index("ctx") // GROUP
    return group // 2, group % 2


def group_kernel(ab_ref, whole_ref, tree_ref, factors_ref):
    pairs = [compose(ab_ref[2 * i], ab_ref[2 * i + 1]) for i in range(4)]
    quads = [compose(pairs[2 * i], pairs[2 * i + 1]) for i in range(2)]
    for i, a in enumerate(pairs + quads):
        factors_ref[i] = a[:, :HEAD]
    for i, a in enumerate((pairs[0], pairs[2], quads[0])):
        tree_ref[i] = a
    whole_ref[...] = compose(quads[0], quads[1])


def pair_kernel(own_ref, other_ref, token_ref, all_ref):
    _, late = level()
    own, other = own_ref[...], other_ref[...]
    early = jnp.where(late == 1, other, own)
    pair = compose(early, jnp.where(late == 1, own, other))
    for i in range(PLANES):
        all_ref[i] = pair


def apply_map(ab, w):
    return exact(halves(ab[:, :HEAD]), halves(w)) + ab[:, HEAD:]


def start_kernel(
    ab_ref, tree_ref, pairs_ref, other_ref, init_ref, gain_hbm, w_ref, gain_ref, sems
):
    weight = Copies(sems).start(gain_hbm, gain_ref)
    plane, late = level()
    w0 = lax.fori_loop(0, plane, lambda z, w: apply_map(pairs_ref[z], w), init_ref[...])
    w0 = lax.fori_loop(0, late, lambda _, w: apply_map(other_ref[...], w), w0)
    w4 = apply_map(tree_ref[2], w0)
    w2 = apply_map(tree_ref[0], w0)
    w6 = apply_map(tree_ref[1], w4)
    for i, w in zip((0, 2, 4, 6), (w0, w2, w4, w6)):
        w_ref[i] = w
        w_ref[i + 1] = apply_map(ab_ref[i], w)
    weight.wait()


def adjoint_kernel(
    pairs_ref, ab_ref, factors_ref, other_ref, after_ref, first_ref, early_ref, up_ref
):
    eye = (
        lax.broadcasted_iota(jnp.int32, (HEAD, HEAD), 0)
        == lax.broadcasted_iota(jnp.int32, (HEAD, HEAD), 1)
    ).astype(F32)
    first = after = eye
    plane, late = level()
    own = exact(halves(factors_ref[5]), halves(factors_ref[4]))
    early_ref[...] = jnp.transpose(jnp.where(late == 1, other_ref[:, :HEAD], own))
    for i in range(4):
        up_ref[i] = jnp.transpose(ab_ref[2 * i, :, :HEAD])
    for i, a in enumerate((0, 2, 4)):
        up_ref[4 + i] = jnp.transpose(factors_ref[a])
    for z in range(PLANES):
        first_ref[z] = first
        later = z > plane
        after_ref[z] = jnp.where(later, after, 0.0)
        if z < PLANES - 1:
            step = halves(pairs_ref[z, :, :HEAD])
            first = exact(halves(first), step, dot_nt)
            after = jnp.where(later, exact(halves(after), step, dot_nt), eye)


def hidden_kernel(qt_ref, c_ref, cot_ref, gain_ref, w_ref, z_ref, stats_ref):
    heads, n = qt_ref.shape[:2]
    squares = jnp.zeros((n, HEAD), F32)
    products = jnp.zeros((n, HEAD), F32)
    for h in range(heads):
        z = dot(qt_ref[h], low(w_ref[h])) + c_ref[h]
        z_ref[:, columns(h)] = z
        squares += z * z
        products += z * (cot_ref[:, columns(h)].astype(F32) * gain_ref[:, columns(h)])
    ones = jnp.ones((8, HEAD), BF16)
    sums = [dot_nt(ones, high) + dot_nt(ones, rest) for high, rest in map(halves, (squares, products))]
    place = lax.broadcasted_iota(jnp.int32, (8, n), 0)
    stats_ref[...] = jnp.where(place < 4, sums[0], sums[1])


def norm_kernel(
    z_ref, cot_ref, gain_ref, own_ref, other_ref, qtt_ref,
    normed_hbm, dz_hbm, g_hbm, normed_ref, dz_ref, g_ref, sems,
):
    heads = qtt_ref.shape[0]
    width = 2 * z_ref.shape[1]
    copies = Copies(sems)
    stats = own_ref[...] + other_ref[...]
    inv = lax.rsqrt(stats[0:1] / width + EPSILON)
    shift = inv * inv * inv * stats[4:5] / width
    inv, shift = (
        jnp.transpose(jnp.broadcast_to(a, (HEAD, a.shape[1]))) for a in (inv, shift)
    )
    for h in range(heads):
        go = cot_ref[:, columns(h)].astype(F32) * gain_ref[:, columns(h)]
        dz = low(inv * go - z_ref[:, columns(h)] * shift)
        dz_ref[:, columns(h)] = dz
        g_ref[h] = dot(qtt_ref[h], dz)
        normed_ref[:, columns(h)] = low(z_ref[:, columns(h)] * inv * gain_ref[:, columns(h)])
        if h % BATCH == BATCH - 1:
            part = slice(h + 1 - BATCH, h + 1)
            flat = span(h + 1 - BATCH, h + 1)
            copies.start(g_ref.at[part], g_hbm.at[part])
            copies.start(dz_ref.at[:, flat], dz_hbm.at[:, flat])
            copies.start(normed_ref.at[:, flat], normed_hbm.at[:, flat])
    for copy in copies.started:
        copy.wait()


def query_kernel(
    q_hbm, k_hbm, e_hbm, tkv_hbm, dz_hbm, w_ref, dq_hbm, dk_hbm, er_hbm, token_ref,
    q_ref, k_ref, e_ref, tkv_ref, dz_ref, dq_ref, dk_ref, er_ref, sems,
):
    n = k_ref.shape[0]
    heads = e_ref.shape[0]
    copies = Copies(sems)
    rates = copies.start(e_hbm, e_ref)
    arrivals = []
    for first in range(0, heads, BATCH):
        part = slice(first, first + BATCH)
        flat = span(first, first + BATCH)
        arrivals.append((
            copies.start(tkv_hbm.at[part], tkv_ref.at[part]),
            copies.start(dz_hbm.at[:, flat], dz_ref.at[:, flat]),
            copies.start(k_hbm.at[:, flat], k_ref.at[:, flat]),
            copies.start(q_hbm.at[:, flat], q_ref.at[:, flat]),
        ))
    row = lax.broadcasted_iota(jnp.int32, (n, n), 0)
    col = lax.broadcasted_iota(jnp.int32, (n, n), 1)
    causal = row >= col
    token_ref[...] = jnp.zeros_like(token_ref)
    rates.wait()
    sent = []
    for first, arrival in zip(range(0, heads, BATCH), arrivals):
        batch = range(first, first + BATCH)
        ws = [low(w_ref[h]) for h in batch]
        rates_wide = [
            jnp.transpose(jnp.broadcast_to(e_ref[h : h + 1, :], (HEAD, n))) for h in batch
        ]
        for copy in arrival:
            copy.wait()
        for h, w, wide in zip(batch, ws, rates_wide):
            r = dot(tkv_ref[h, :, :HEAD], w) - tkv_ref[h, :, HEAD:].astype(F32)
            er_ref[h] = low(r * wide)
        dss = [
            low(jnp.where(causal, -dot_nt(dz_ref[:, columns(h)], er_ref[h]), 0.0)) for h in batch
        ]
        for h, w, ds in zip(batch, ws, dss):
            dq_ref[:, columns(h)] = low(
                dot_nt(dz_ref[:, columns(h)], w) + dot(ds, k_ref[:, columns(h)])
            )
            dk_ref[h] = low(dot_tn(ds, q_ref[:, columns(h)]))
        part = slice(first, first + BATCH)
        flat = span(first, first + BATCH)
        sent.append(copies.start(dq_ref.at[:, flat], dq_hbm.at[:, flat]))
        for source, target in ((dk_ref, dk_hbm), (er_ref, er_hbm)):
            sent.append(copies.start(source.at[part], target.at[part]))
    for copy in sent:
        copy.wait()


def transposed_map(a, later, own):
    return exact(halves(a), halves(later), dot_tn) + own


def turned_map(a, later, own):
    return exact(halves(a), halves(later)) + own


def gather_kernel(up_ref, g_ref, token_ref, whole_ref, sums_ref):
    pairs = [turned_map(up_ref[i], g_ref[2 * i + 1], g_ref[2 * i]) for i in range(4)]
    quads = [turned_map(up_ref[4 + i], pairs[2 * i + 1], pairs[2 * i]) for i in range(2)]
    for i, a in enumerate(pairs + quads):
        sums_ref[i] = a
    whole_ref[...] = turned_map(up_ref[6], quads[1], quads[0])


def pair_gradient_kernel(early_ref, own_ref, other_ref, token_ref, all_ref):
    _, late = level()
    own, other = own_ref[...], other_ref[...]
    pair = turned_map(
        early_ref[...], jnp.where(late == 1, own, other), jnp.where(late == 1, other, own)
    )
    for i in range(PLANES):
        all_ref[i] = pair


def end_kernel(
    after_ref, first_ref, ab_ref, factors_ref, g_ref, sums_ref, other_map_ref, other_ref, later_ref,
    d_ref, init_ref,
):
    parts = [halves(later_ref[z]) for z in range(PLANES)]
    _, late = level()
    end = exact(halves(after_ref[1]), parts[1])
    for z in range(2, PLANES):
        end += exact(halves(after_ref[z]), parts[z])
    inner = transposed_map(other_map_ref[:, :HEAD], end, other_ref[...])
    d7 = jnp.where(late == 1, end, inner)
    d3 = transposed_map(factors_ref[5], d7, sums_ref[5])
    d5 = transposed_map(factors_ref[3], d7, sums_ref[3])
    d1 = transposed_map(factors_ref[1], d3, sums_ref[1])
    start = later_ref[0]
    for z in range(1, PLANES):
        start += exact(halves(first_ref[z]), parts[z])
    init_ref[...] = start
    rows = init_ref[pl.ds(pl.multiple_of(lax.axis_index("ctx") // GROUP * 16, 16), 16), :]
    for i, d in zip((7, 5, 3, 1), (d7, d5, d3, d1)):
        d_ref[i, :HEAD, :] = d
        d_ref[i - 1, :HEAD, :] = transposed_map(ab_ref[i, :, :HEAD], d, g_ref[i])
    for i in range(GROUP):
        d_ref[i, HEAD:, :] = jnp.zeros((8, HEAD), F32)
        d_ref[i, HEAD : HEAD + 2, :] = rows[2 * i : 2 * i + 2]


def key_kernel(
    k_ref, e_ref, tek_ref, er_ref, u_ref, dkp_ref, w_ref, d_ref,
    dk_hbm, dv_hbm, de_ref, gi_ref, dk_ref, dv_ref, sems,
):
    n = k_ref.shape[0]
    heads = e_ref.shape[0]
    copies = Copies(sems)
    row = lax.broadcasted_iota(jnp.int32, (n, n), 0) // MB
    col = lax.broadcasted_iota(jnp.int32, (n, n), 1) // MB
    before = row > col
    after = row < col
    ones = jnp.ones((8, HEAD), BF16)
    for h in range(heads):
        gi_ref[h : h + 1, :HEAD] = d_ref[h, HEAD : HEAD + 1, :]
        gi_ref[h : h + 1, HEAD:] = d_ref[h, HEAD + 1 : HEAD + 2, :]
    for first in range(0, heads, heads):
        batch = range(first, first + heads)
        ds = [low(d_ref[h, :HEAD, :]) for h in batch]
        both = [jnp.concatenate([low(w_ref[h]), -d], axis=1) for h, d in zip(batch, ds)]
        ers = [er_ref[h] for h in batch]
        us = [u_ref[h].astype(F32) - dot(tek_ref[h], d) for h, d in zip(batch, ds)]
        lows = [low(u) for u in us]
        for h, u in zip(batch, lows):
            dv_ref[:, columns(h)] = -u
        flat = span(first, first + heads)
        copies.start(dv_ref.at[:, flat], dv_hbm.at[:, flat])
        ps = [low(u * er.astype(F32)) for u, er in zip(us, ers)]
        xs = [
            low(jnp.where(before, dot_nt(u, er), jnp.where(after, dot_nt(er, u), 0.0)))
            for u, er in zip(lows, ers)
        ]
        dks = [
            dkp_ref[h].astype(F32) + dot_nt(jnp.concatenate([u, er], axis=1), b)
            for h, u, er, b in zip(batch, lows, ers, both)
        ]
        for h, dk, x, p in zip(batch, dks, xs, ps):
            e = e_ref[h : h + 1, :]
            dk_ref[:, columns(h)] = low(dk - dot(x, k_ref[:, columns(h)]))
            if h % 2 == 1:
                flat = span(h - 1, h + 1)
                copies.start(dk_ref.at[:, flat], dk_hbm.at[:, flat])
            de_ref[h : h + 1, :] = dot_nt(ones, p)[0:1] / (e * e)
    for copy in copies.started:
        copy.wait()


def local(queries, keys, values, rates, init_weight, gain, cotangent):
    n, width = keys.shape
    heads = width // HEAD
    count = lax.axis_size("ctx") // GROUP
    near = [[g * GROUP + i for i in range(GROUP)] for g in range(count)]
    stride = 2 * GROUP
    far = [[z * stride + i for z in range(PLANES)] for i in range(stride)]
    across = [(i, i + GROUP if i % stride < GROUP else i - GROUP) for i in range(count * GROUP)]
    gain_row = gain.reshape(1, width)

    def swap(a, groups):
        return lax.all_to_all(a, "ctx", 0, 0, axis_index_groups=groups)

    square = (GROUP, HEAD, HEAD)
    wide = (GROUP, HEAD, 2 * HEAD)
    tall = (heads, n, HEAD)
    full = (heads, n, n)
    flat = (n, width)
    token = ((8, HEAD), F32, "v")
    parts = heads // BATCH
    vm = pltpu.VMEM

    half = n // 2
    inner = (heads, 2, half, half)
    corner = (heads, half, half)
    pair = (heads, n, 2 * HEAD)
    turned = (heads, HEAD, n)
    maps, inverse, cross, tkv = call(
        map_kernel,
        [
            (wide, F32, "v"), (inner, BF16, "h"), (corner, BF16, "h"),
            ((heads, n, 2 * HEAD), BF16, "h"),
        ],
        [(keys, "h"), (values, "h"), (rates, "h")],
        [
            vm(flat, BF16), vm(flat, BF16), vm((heads, n), F32),
            vm(inner, BF16), vm(corner, BF16), vm((heads, n, 2 * HEAD), BF16),
        ],
        copies=5 + 2 * parts,
    )
    own_maps = swap(maps, near)
    qt, qt_turned, offset, scores, own_init, prepared = call(
        prepare_kernel,
        [
            (tall, BF16, "h"), (turned, BF16, "h"), (tall, F32, "h"), (full, BF16, "h"),
            ((HEAD, HEAD), F32, "h"), token,
        ],
        [(queries, "h"), (keys, "h"), (rates, "h"), (tkv, "h"), (init_weight, "h")],
        [
            vm(flat, BF16), vm(flat, BF16), vm((heads, n), F32), vm(pair, BF16), vm(tall, BF16),
            vm(turned, BF16), vm(tall, F32), vm(full, BF16),
        ],
        copies=2 + 7 * parts,
    )
    slab = (HEAD, 2 * HEAD)
    block = (HEAD, HEAD)
    whole, tree, factors = call(
        group_kernel,
        [(slab, F32, "v"), ((3, HEAD, 2 * HEAD), F32, "v"), ((6, HEAD, HEAD), F32, "v")],
        [(own_maps, "v")],
    )
    other_map = lax.ppermute(whole, "ctx", across)
    (sent,) = call(
        pair_kernel,
        [((PLANES, HEAD, 2 * HEAD), F32, "v")],
        [(whole, "v"), (other_map, "v"), (prepared, "v")],
    )
    pair_maps = swap(sent, far)
    starts, gain_row = call(
        start_kernel,
        [(square, F32, "v"), ((1, width), F32, "v")],
        [
            (own_maps, "v"), (tree, "v"), (pair_maps, "v"), (other_map, "v"), (own_init, "v"),
            (gain_row, "h"),
        ],
        copies=1,
    )
    weights = swap(starts, near)
    hidden, stats = call(
        hidden_kernel,
        [(flat, F32, "v"), ((8, n), F32, "v")],
        [(qt, "v"), (offset, "v"), (cotangent, "v"), (gain_row, "v"), (weights, "v")],
    )
    other = lax.ppermute(stats, "tensor", [(0, 1), (1, 0)])
    normed, dz, local_grad = call(
        norm_kernel,
        [(flat, BF16, "h"), (flat, BF16, "h"), (square, F32, "h")],
        [
            (hidden, "v"), (cotangent, "v"), (gain_row, "v"), (stats, "v"), (other, "v"),
            (qt_turned, "v"),
        ],
        [vm(flat, BF16), vm(flat, BF16), vm(square, F32)],
        copies=3 * parts,
    )
    own_grads = swap(local_grad, near)
    grad_queries, dk_part, scaled_residual, queried = call(
        query_kernel,
        [(flat, BF16, "h"), (tall, BF16, "h"), (tall, BF16, "h"), token],
        [
            (queries, "h"), (keys, "h"), (rates, "h"), (tkv, "h"), (dz, "h"), (weights, "v"),
        ],
        [
            vm(flat, BF16), vm(flat, BF16), vm((heads, n), F32), vm(pair, BF16),
            vm(flat, BF16), vm(flat, BF16), vm(tall, BF16), vm(tall, BF16),
        ],
        copies=1 + 7 * parts,
    )
    u, tek, settled = call(
        adjoint_residual_kernel,
        [(tall, BF16, "h"), (tall, BF16, "h"), token],
        [
            (keys, "h"), (rates, "h"), (scores, "h"), (inverse, "h"), (cross, "h"), (dz, "h"),
        ],
        [
            vm(flat, BF16), vm((heads, n), F32), vm(full, BF16), vm(inner, BF16),
            vm(corner, BF16), vm(flat, BF16), vm(tall, BF16), vm(tall, BF16),
        ],
        copies=1 + 7 * parts,
    )
    steps = (PLANES, HEAD, HEAD)
    after, first, early, up = call(
        adjoint_kernel,
        [(steps, F32, "a"), (steps, F32, "a"), (block, F32, "a"), ((7, HEAD, HEAD), F32, "v")],
        [(pair_maps, "v"), (own_maps, "v"), (factors, "v"), (other_map, "v")],
    )
    whole, sums = call(
        gather_kernel,
        [(block, F32, "v"), ((6, HEAD, HEAD), F32, "v")],
        [(up, "v"), (own_grads, "v"), (queried, "v")],
    )
    other_grad = lax.ppermute(whole, "ctx", across)
    (sent,) = call(
        pair_gradient_kernel,
        [(steps, F32, "v")],
        [(early, "v"), (whole, "v"), (other_grad, "v"), (settled, "v")],
    )
    pair_grads = swap(sent, far)
    (ends,) = call(
        end_kernel,
        [((GROUP, HEAD + 8, HEAD), F32, "v")],
        [
            (after, "v"), (first, "v"), (own_maps, "v"), (factors, "v"), (own_grads, "v"),
            (sums, "v"), (other_map, "v"), (other_grad, "v"), (pair_grads, "v"),
        ],
        [vm(block, F32)],
    )
    adjoint = swap(ends, near)
    grad_keys, grad_values, grad_rates, grad_init = call(
        key_kernel,
        [(flat, BF16, "h"), (flat, BF16, "h"), ((heads, n), F32, "v"), ((heads, n), F32, "v")],
        [
            (keys, "v"), (rates, "v"), (tek, "v"), (scaled_residual, "v"), (u, "v"),
            (dk_part, "v"), (weights, "v"), (adjoint, "v"),
        ],
        [vm(flat, BF16), vm(flat, BF16)],
        copies=1 + heads // 2,
    )
    return (normed, grad_queries, grad_keys, grad_values, grad_rates, grad_init)


def solution(mesh):
    in_specs = (
        P("ctx", "tensor"),
        P("ctx", "tensor"),
        P("ctx", "tensor"),
        P("tensor", "ctx"),
        P("tensor", None, None),
        P("tensor"),
        P("ctx", "tensor"),
    )
    out_specs = (
        P("ctx", "tensor"),
        P("ctx", "tensor"),
        P("ctx", "tensor"),
        P("ctx", "tensor"),
        P("tensor", "ctx"),
        P("tensor", "ctx"),
    )
    return jax.shard_map(local, mesh=mesh, in_specs=in_specs, out_specs=out_specs, check_vma=False)
```

```python
import jax
import jax.numpy as jnp
from jax import lax
from jax.experimental import pallas as pl
from jax.experimental.pallas import tpu as pltpu
from jax.sharding import PartitionSpec as P

HEAD = 128
MB = 16
EPSILON = 1e-06
GROUP = 8
PLANES = 4
F32 = jnp.float32
BF16 = jnp.bfloat16


def low(a):
    return a.astype(BF16)


def dot(a, b):
    return jnp.dot(a, b, preferred_element_type=F32)


def dot_nt(a, b):
    return lax.dot_general(a, b, (((1,), (1,)), ((), ())), preferred_element_type=F32)


def dot_tn(a, b):
    return lax.dot_general(a, b, (((0,), (0,)), ((), ())), preferred_element_type=F32)


def halves(a):
    high = low(a)
    return high, low(a - high.astype(F32))


def exact(a, b, product=dot):
    (ah, al), (bh, bl) = a, b
    return product(ah, bh) + (product(ah, bl) + product(al, bh))


def call(kernel, outs, args, scratch=(), copies=0, limit=24):
    spaces = {"s": pltpu.SMEM, "v": pltpu.VMEM, "h": pltpu.HBM, "a": pltpu.VMEM}
    values = [pltpu.with_memory_space_constraint(a, pltpu.HBM) if p in "ha" else a for a, p in args]
    results = [
        pltpu.HBM(shape, dtype) if p in "ha" else jax.ShapeDtypeStruct(shape, dtype)
        for shape, dtype, p in outs
    ]
    size = sum(a.size * a.dtype.itemsize for a in values)
    scratch = list(scratch)
    if copies:
        scratch.append(pltpu.SemaphoreType.DMA((copies,)))
    return pl.pallas_call(
        kernel,
        out_shape=results,
        in_specs=[pl.BlockSpec(memory_space=spaces[p]) for _, p in args],
        out_specs=[pl.BlockSpec(memory_space=spaces[p]) for _, _, p in outs],
        scratch_shapes=scratch,
        compiler_params=pltpu.CompilerParams(vmem_limit_bytes=limit * 2**20),
        cost_estimate=pl.CostEstimate(
            flops=2 * 10**9, bytes_accessed=2 * size, transcendentals=0
        ),
        name=kernel.__name__,
    )(*values)


class Copies:
    def __init__(self, semaphores):
        self.semaphores = semaphores
        self.started = []

    def start(self, source, target):
        copy = pltpu.make_async_copy(source, target, self.semaphores.at[len(self.started)])
        copy.start()
        self.started.append(copy)
        return copy


def columns(h):
    return slice(h * HEAD, (h + 1) * HEAD)


def span(first, last):
    return slice(first * HEAD, last * HEAD)


BATCH = 4


def map_kernel(
    k_hbm, v_hbm, e_hbm, ab_ref, t_hbm, n_hbm, tkv_hbm,
    k_ref, v_ref, e_ref, t_ref, n_ref, tkv_ref, sems,
):
    heads = e_ref.shape[0]
    half = t_ref.shape[-1]
    copies = Copies(sems)
    arrivals = []
    for first in range(0, heads, BATCH):
        part = span(first, first + BATCH)
        key = copies.start(k_hbm.at[:, part], k_ref.at[:, part])
        if first == 0:
            rates = copies.start(e_hbm, e_ref)
        arrivals.append((key, copies.start(v_hbm.at[:, part], v_ref.at[:, part])))
    row = lax.broadcasted_iota(jnp.int32, (half, half), 0)
    col = lax.broadcasted_iota(jnp.int32, (half, half), 1)
    eye = (row == col).astype(F32)
    masks = []
    width = MB
    while width < half:
        masks.append((row // (2 * width) == col // (2 * width)) & (row // width > col // width))
        width *= 2
    sent = []
    ks, es, blocks, crosses, scaled = [], [], [], [], []
    for first, (key, _) in zip(range(0, heads, BATCH), arrivals):
        key.wait()
        if first == 0:
            rates.wait()
        for h in range(first, first + BATCH):
            k = k_ref[:, columns(h)]
            e = e_ref[h : h + 1, :]
            top = -(dot_nt(k[:half], k[:half]) * e[:, :half])
            bottom = -(dot_nt(k[half:], k) * e)
            blocks += [top, bottom[:, half:]]
            crosses.append(low(bottom[:, :half]))
            ks.append(k)
            es.append(e)
    inverses = [low(eye + jnp.where(masks[0], b, 0.0)) for b in blocks]
    for mask in masks[1:]:
        mids = [low(dot(low(jnp.where(mask, b, 0.0)), t)) for b, t in zip(blocks, inverses)]
        inverses = [t + low(dot(t, m)) for t, m in zip(inverses, mids)]
    for h in range(heads):
        t_ref[h, 0] = inverses[2 * h]
        t_ref[h, 1] = inverses[2 * h + 1]
        n_ref[h] = crosses[h]
    sent.append(copies.start(t_ref, t_hbm))
    sent.append(copies.start(n_ref, n_hbm))
    scaled = [low(jnp.transpose(k.astype(F32)) * e) for k, e in zip(ks, es)]
    for _, value in arrivals:
        value.wait()
    kvs = [jnp.concatenate([ks[h], v_ref[:, columns(h)]], axis=1) for h in range(heads)]
    tops = [low(dot(t, kv[:half])) for t, kv in zip(inverses[::2], kvs)]
    for h in range(heads):
        tkv_ref[h, :half] = tops[h]
    sent.append(copies.start(tkv_ref.at[:, :half], tkv_hbm.at[:, :half]))
    mids = [low(kv[half:].astype(F32) + dot(c, x)) for kv, c, x in zip(kvs, crosses, tops)]
    bottoms = [low(dot(t, m)) for t, m in zip(inverses[1::2], mids)]
    for h in range(heads):
        tkv_ref[h, half:] = bottoms[h]
    sent.append(copies.start(tkv_ref.at[:, half:], tkv_hbm.at[:, half:]))
    for h in range(heads):
        ab = dot(scaled[h], tkv_ref[h])
        ab_ref[h, :, :HEAD] = eye - ab[:, :HEAD]
        ab_ref[h, :, HEAD:] = ab[:, HEAD:]
    for copy in sent:
        copy.wait()


def causal_scores(q, k, e):
    n = q.shape[0]
    row = lax.broadcasted_iota(jnp.int32, (n, n), 0)
    col = lax.broadcasted_iota(jnp.int32, (n, n), 1)
    return low(jnp.where(row >= col, dot_nt(q, k) * e, 0.0))


def prepare_kernel(
    q_hbm, k_hbm, e_hbm, tkv_hbm, init_hbm,
    qt_hbm, qtt_hbm, c_hbm, se_hbm, own_hbm, token_ref,
    q_ref, k_ref, e_ref, tkv_ref, qt_ref, qtt_ref, c_ref, se_ref, sems,
):
    heads = e_ref.shape[0]
    copies = Copies(sems)
    sent = [copies.start(init_hbm.at[lax.axis_index("ctx") % GROUP], own_hbm)]
    rates = copies.start(e_hbm, e_ref)
    arrivals = []
    for first in range(0, heads, BATCH):
        part = slice(first, first + BATCH)
        flat = span(first, first + BATCH)
        arrivals.append((
            copies.start(q_hbm.at[:, flat], q_ref.at[:, flat]),
            copies.start(k_hbm.at[:, flat], k_ref.at[:, flat]),
            copies.start(tkv_hbm.at[part], tkv_ref.at[part]),
        ))
    token_ref[...] = jnp.zeros_like(token_ref)
    rates.wait()
    for first, arrival in zip(range(0, heads, BATCH), arrivals):
        batch = range(first, first + BATCH)
        for copy in arrival:
            copy.wait()
        scores = [
            causal_scores(q_ref[:, columns(h)], k_ref[:, columns(h)], e_ref[h : h + 1, :])
            for h in batch
        ]
        for h, se in zip(batch, scores):
            se_ref[h] = se
            sx = dot(se, tkv_ref[h])
            qt = q_ref[:, columns(h)].astype(F32) - sx[:, :HEAD]
            qt_ref[h] = low(qt)
            qtt_ref[h] = low(jnp.transpose(qt))
            c_ref[h] = sx[:, HEAD:]
        part = slice(first, first + BATCH)
        for source, target in (
            (qt_ref, qt_hbm), (qtt_ref, qtt_hbm), (c_ref, c_hbm), (se_ref, se_hbm)
        ):
            sent.append(copies.start(source.at[part], target.at[part]))
    for copy in sent:
        copy.wait()


def adjoint_residual_kernel(
    k_hbm, e_hbm, se_hbm, t_hbm, n_hbm, dz_hbm, u_hbm, tek_hbm, token_ref,
    k_ref, e_ref, se_ref, t_ref, n_ref, dz_ref, u_ref, tek_ref, sems,
):
    heads, n = e_ref.shape
    half = n // 2
    copies = Copies(sems)
    rates = copies.start(e_hbm, e_ref)
    arrivals = []
    for first in range(0, heads, BATCH):
        part = slice(first, first + BATCH)
        flat = span(first, first + BATCH)
        arrivals.append((
            copies.start(t_hbm.at[part], t_ref.at[part]),
            copies.start(n_hbm.at[part], n_ref.at[part]),
            copies.start(k_hbm.at[:, flat], k_ref.at[:, flat]),
            copies.start(se_hbm.at[part], se_ref.at[part]),
            copies.start(dz_hbm.at[:, flat], dz_ref.at[:, flat]),
        ))
    token_ref[...] = jnp.zeros_like(token_ref)
    rates.wait()
    sent = []
    for first, arrival in zip(range(0, heads, BATCH), arrivals):
        batch = range(first, first + BATCH)
        wides = [jnp.transpose(jnp.broadcast_to(e_ref[h : h + 1, :], (HEAD, n))) for h in batch]
        for copy in arrival:
            copy.wait()
        mids = [low(dot(n_ref[h], t_ref[h, 0])) for h in batch]
        ys = [
            jnp.concatenate(
                [
                    low(dot_tn(se_ref[h], dz_ref[:, columns(h)])),
                    low(k_ref[:, columns(h)].astype(F32) * wide),
                ],
                axis=1,
            )
            for h, wide in zip(batch, wides)
        ]
        lowers = [dot_tn(t_ref[h, 1], y[half:]) for h, y in zip(batch, ys)]
        uppers = [
            dot_tn(t_ref[h, 0], y[:half]) + dot_tn(m, low(x))
            for h, y, m, x in zip(batch, ys, mids, lowers)
        ]
        for h, upper, lower in zip(batch, uppers, lowers):
            u_ref[h, :half] = low(-upper[:, :HEAD])
            u_ref[h, half:] = low(-lower[:, :HEAD])
            tek_ref[h, :half] = low(upper[:, HEAD:])
            tek_ref[h, half:] = low(lower[:, HEAD:])
        part = slice(first, first + BATCH)
        for source, target in ((u_ref, u_hbm), (tek_ref, tek_hbm)):
            sent.append(copies.start(source.at[part], target.at[part]))
    for copy in sent:
        copy.wait()


def compose(early, late):
    wide = exact(halves(late[:, :HEAD]), halves(early))
    return jnp.concatenate([wide[:, :HEAD], wide[:, HEAD:] + late[:, HEAD:]], axis=1)


def broadcast(copies, source, targets):
    sent = [copies.start(source, targets.at[i]) for i in range(GROUP)]
    for copy in sent:
        copy.wait()


def level():
    group = lax.axis_index("ctx") // GROUP
    return group // 2, group % 2


def group_kernel(ab_ref, whole_ref, tree_ref, factors_ref):
    pairs = [compose(ab_ref[2 * i], ab_ref[2 * i + 1]) for i in range(4)]
    quads = [compose(pairs[2 * i], pairs[2 * i + 1]) for i in range(2)]
    for i, a in enumerate(pairs + quads):
        factors_ref[i] = a[:, :HEAD]
    for i, a in enumerate((pairs[0], pairs[2], quads[0])):
        tree_ref[i] = a
    whole_ref[...] = compose(quads[0], quads[1])


def pair_kernel(own_ref, other_ref, token_ref, all_ref):
    _, late = level()
    own, other = own_ref[...], other_ref[...]
    early = jnp.where(late == 1, other, own)
    pair = compose(early, jnp.where(late == 1, own, other))
    for i in range(PLANES):
        all_ref[i] = pair


def apply_map(ab, w):
    return exact(halves(ab[:, :HEAD]), halves(w)) + ab[:, HEAD:]


def start_kernel(
    ab_ref, tree_ref, pairs_ref, other_ref, init_ref, gain_hbm, w_ref, gain_ref, sems
):
    weight = Copies(sems).start(gain_hbm, gain_ref)
    plane, late = level()
    w0 = lax.fori_loop(0, plane, lambda z, w: apply_map(pairs_ref[z], w), init_ref[...])
    w0 = lax.fori_loop(0, late, lambda _, w: apply_map(other_ref[...], w), w0)
    w4 = apply_map(tree_ref[2], w0)
    w2 = apply_map(tree_ref[0], w0)
    w6 = apply_map(tree_ref[1], w4)
    for i, w in zip((0, 2, 4, 6), (w0, w2, w4, w6)):
        w_ref[i] = w
        w_ref[i + 1] = apply_map(ab_ref[i], w)
    weight.wait()


def adjoint_kernel(
    pairs_ref, ab_ref, factors_ref, other_ref, after_ref, first_ref, early_ref, up_ref
):
    eye = (
        lax.broadcasted_iota(jnp.int32, (HEAD, HEAD), 0)
        == lax.broadcasted_iota(jnp.int32, (HEAD, HEAD), 1)
    ).astype(F32)
    first = after = eye
    plane, late = level()
    own = exact(halves(factors_ref[5]), halves(factors_ref[4]))
    early_ref[...] = jnp.transpose(jnp.where(late == 1, other_ref[:, :HEAD], own))
    for i in range(4):
        up_ref[i] = jnp.transpose(ab_ref[2 * i, :, :HEAD])
    for i, a in enumerate((0, 2, 4)):
        up_ref[4 + i] = jnp.transpose(factors_ref[a])
    for z in range(PLANES):
        first_ref[z] = first
        later = z > plane
        after_ref[z] = jnp.where(later, after, 0.0)
        if z < PLANES - 1:
            step = halves(pairs_ref[z, :, :HEAD])
            first = exact(halves(first), step, dot_nt)
            after = jnp.where(later, exact(halves(after), step, dot_nt), eye)


def hidden_kernel(qt_ref, c_ref, cot_ref, gain_ref, w_ref, z_ref, stats_ref):
    heads, n = qt_ref.shape[:2]
    squares = jnp.zeros((n, HEAD), F32)
    products = jnp.zeros((n, HEAD), F32)
    for h in range(heads):
        z = dot(qt_ref[h], low(w_ref[h])) + c_ref[h]
        z_ref[:, columns(h)] = z
        squares += z * z
        products += z * (cot_ref[:, columns(h)].astype(F32) * gain_ref[:, columns(h)])
    ones = jnp.ones((8, HEAD), BF16)
    sums = [dot_nt(ones, high) + dot_nt(ones, rest) for high, rest in map(halves, (squares, products))]
    place = lax.broadcasted_iota(jnp.int32, (8, n), 0)
    stats_ref[...] = jnp.where(place < 4, sums[0], sums[1])


def norm_kernel(
    z_ref, cot_ref, gain_ref, own_ref, other_ref, qtt_ref,
    normed_hbm, dz_hbm, g_hbm, normed_ref, dz_ref, g_ref, sems,
):
    heads = qtt_ref.shape[0]
    width = 2 * z_ref.shape[1]
    copies = Copies(sems)
    stats = own_ref[...] + other_ref[...]
    inv = lax.rsqrt(stats[0:1] / width + EPSILON)
    shift = inv * inv * inv * stats[4:5] / width
    inv, shift = (
        jnp.transpose(jnp.broadcast_to(a, (HEAD, a.shape[1]))) for a in (inv, shift)
    )
    for h in range(heads):
        go = cot_ref[:, columns(h)].astype(F32) * gain_ref[:, columns(h)]
        dz = low(inv * go - z_ref[:, columns(h)] * shift)
        dz_ref[:, columns(h)] = dz
        g_ref[h] = dot(qtt_ref[h], dz)
        normed_ref[:, columns(h)] = low(z_ref[:, columns(h)] * inv * gain_ref[:, columns(h)])
        if h % BATCH == BATCH - 1:
            part = slice(h + 1 - BATCH, h + 1)
            flat = span(h + 1 - BATCH, h + 1)
            copies.start(g_ref.at[part], g_hbm.at[part])
            copies.start(dz_ref.at[:, flat], dz_hbm.at[:, flat])
            copies.start(normed_ref.at[:, flat], normed_hbm.at[:, flat])
    for copy in copies.started:
        copy.wait()


def query_kernel(
    q_hbm, k_hbm, e_hbm, tkv_hbm, dz_hbm, w_ref, dq_hbm, dk_hbm, er_hbm, token_ref,
    q_ref, k_ref, e_ref, tkv_ref, dz_ref, dq_ref, dk_ref, er_ref, sems,
):
    n = k_ref.shape[0]
    heads = e_ref.shape[0]
    copies = Copies(sems)
    rates = copies.start(e_hbm, e_ref)
    arrivals = []
    for first in range(0, heads, BATCH):
        part = slice(first, first + BATCH)
        flat = span(first, first + BATCH)
        arrivals.append((
            copies.start(tkv_hbm.at[part], tkv_ref.at[part]),
            copies.start(dz_hbm.at[:, flat], dz_ref.at[:, flat]),
            copies.start(k_hbm.at[:, flat], k_ref.at[:, flat]),
            copies.start(q_hbm.at[:, flat], q_ref.at[:, flat]),
        ))
    row = lax.broadcasted_iota(jnp.int32, (n, n), 0)
    col = lax.broadcasted_iota(jnp.int32, (n, n), 1)
    causal = row >= col
    token_ref[...] = jnp.zeros_like(token_ref)
    rates.wait()
    sent = []
    for first, arrival in zip(range(0, heads, BATCH), arrivals):
        batch = range(first, first + BATCH)
        ws = [low(w_ref[h]) for h in batch]
        rates_wide = [
            jnp.transpose(jnp.broadcast_to(e_ref[h : h + 1, :], (HEAD, n))) for h in batch
        ]
        for copy in arrival:
            copy.wait()
        for h, w, wide in zip(batch, ws, rates_wide):
            r = dot(tkv_ref[h, :, :HEAD], w) - tkv_ref[h, :, HEAD:].astype(F32)
            er_ref[h] = low(r * wide)
        dss = [
            low(jnp.where(causal, -dot_nt(dz_ref[:, columns(h)], er_ref[h]), 0.0)) for h in batch
        ]
        for h, w, ds in zip(batch, ws, dss):
            dq_ref[:, columns(h)] = low(
                dot_nt(dz_ref[:, columns(h)], w) + dot(ds, k_ref[:, columns(h)])
            )
            dk_ref[h] = low(dot_tn(ds, q_ref[:, columns(h)]))
        part = slice(first, first + BATCH)
        flat = span(first, first + BATCH)
        sent.append(copies.start(dq_ref.at[:, flat], dq_hbm.at[:, flat]))
        for source, target in ((dk_ref, dk_hbm), (er_ref, er_hbm)):
            sent.append(copies.start(source.at[part], target.at[part]))
    for copy in sent:
        copy.wait()


def transposed_map(a, later, own):
    return exact(halves(a), halves(later), dot_tn) + own


def turned_map(a, later, own):
    return exact(halves(a), halves(later)) + own


def gather_kernel(up_ref, g_ref, token_ref, whole_ref, sums_ref):
    pairs = [turned_map(up_ref[i], g_ref[2 * i + 1], g_ref[2 * i]) for i in range(4)]
    quads = [turned_map(up_ref[4 + i], pairs[2 * i + 1], pairs[2 * i]) for i in range(2)]
    for i, a in enumerate(pairs + quads):
        sums_ref[i] = a
    whole_ref[...] = turned_map(up_ref[6], quads[1], quads[0])


def pair_gradient_kernel(early_ref, own_ref, other_ref, token_ref, all_ref):
    _, late = level()
    own, other = own_ref[...], other_ref[...]
    pair = turned_map(
        early_ref[...], jnp.where(late == 1, own, other), jnp.where(late == 1, other, own)
    )
    for i in range(PLANES):
        all_ref[i] = pair


def end_kernel(
    after_ref, first_ref, ab_ref, factors_ref, g_ref, sums_ref, other_map_ref, other_ref, later_ref,
    d_ref, init_ref,
):
    parts = [halves(later_ref[z]) for z in range(PLANES)]
    _, late = level()
    end = exact(halves(after_ref[1]), parts[1])
    for z in range(2, PLANES):
        end += exact(halves(after_ref[z]), parts[z])
    inner = transposed_map(other_map_ref[:, :HEAD], end, other_ref[...])
    d7 = jnp.where(late == 1, end, inner)
    d3 = transposed_map(factors_ref[5], d7, sums_ref[5])
    d5 = transposed_map(factors_ref[3], d7, sums_ref[3])
    d1 = transposed_map(factors_ref[1], d3, sums_ref[1])
    start = later_ref[0]
    for z in range(1, PLANES):
        start += exact(halves(first_ref[z]), parts[z])
    init_ref[...] = start
    rows = init_ref[pl.ds(pl.multiple_of(lax.axis_index("ctx") // GROUP * 16, 16), 16), :]
    for i, d in zip((7, 5, 3, 1), (d7, d5, d3, d1)):
        d_ref[i, :HEAD, :] = d
        d_ref[i - 1, :HEAD, :] = transposed_map(ab_ref[i, :, :HEAD], d, g_ref[i])
    for i in range(GROUP):
        d_ref[i, HEAD:, :] = jnp.zeros((8, HEAD), F32)
        d_ref[i, HEAD : HEAD + 2, :] = rows[2 * i : 2 * i + 2]


def key_kernel(
    k_ref, e_ref, tek_ref, er_ref, u_ref, dkp_ref, w_ref, d_ref,
    dk_hbm, dv_hbm, de_ref, gi_ref, dk_ref, dv_ref, sems,
):
    n = k_ref.shape[0]
    heads = e_ref.shape[0]
    copies = Copies(sems)
    row = lax.broadcasted_iota(jnp.int32, (n, n), 0) // MB
    col = lax.broadcasted_iota(jnp.int32, (n, n), 1) // MB
    before = row > col
    after = row < col
    ones = jnp.ones((8, HEAD), BF16)
    for h in range(heads):
        gi_ref[h : h + 1, :HEAD] = d_ref[h, HEAD : HEAD + 1, :]
        gi_ref[h : h + 1, HEAD:] = d_ref[h, HEAD + 1 : HEAD + 2, :]
    for first in range(0, heads, heads):
        batch = range(first, first + heads)
        ds = [low(d_ref[h, :HEAD, :]) for h in batch]
        both = [jnp.concatenate([low(w_ref[h]), -d], axis=1) for h, d in zip(batch, ds)]
        ers = [er_ref[h] for h in batch]
        us = [u_ref[h].astype(F32) - dot(tek_ref[h], d) for h, d in zip(batch, ds)]
        lows = [low(u) for u in us]
        for h, u in zip(batch, lows):
            dv_ref[:, columns(h)] = -u
        flat = span(first, first + heads)
        copies.start(dv_ref.at[:, flat], dv_hbm.at[:, flat])
        ps = [low(u * er.astype(F32)) for u, er in zip(us, ers)]
        xs = [
            low(jnp.where(before, dot_nt(u, er), jnp.where(after, dot_nt(er, u), 0.0)))
            for u, er in zip(lows, ers)
        ]
        dks = [
            dkp_ref[h].astype(F32) + dot_nt(jnp.concatenate([u, er], axis=1), b)
            for h, u, er, b in zip(batch, lows, ers, both)
        ]
        for h, dk, x, p in zip(batch, dks, xs, ps):
            e = e_ref[h : h + 1, :]
            dk_ref[:, columns(h)] = low(dk - dot(x, k_ref[:, columns(h)]))
            if h % 2 == 1:
                flat = span(h - 1, h + 1)
                copies.start(dk_ref.at[:, flat], dk_hbm.at[:, flat])
            de_ref[h : h + 1, :] = dot_nt(ones, p)[0:1] / (e * e)
    for copy in copies.started:
        copy.wait()


def local(queries, keys, values, rates, init_weight, gain, cotangent):
    n, width = keys.shape
    heads = width // HEAD
    count = lax.axis_size("ctx") // GROUP
    near = [[g * GROUP + i for i in range(GROUP)] for g in range(count)]
    stride = 2 * GROUP
    far = [[z * stride + i for z in range(PLANES)] for i in range(stride)]
    across = [(i, i + GROUP if i % stride < GROUP else i - GROUP) for i in range(count * GROUP)]
    gain_row = gain.reshape(1, width)

    def swap(a, groups):
        return lax.all_to_all(a, "ctx", 0, 0, axis_index_groups=groups)

    square = (GROUP, HEAD, HEAD)
    wide = (GROUP, HEAD, 2 * HEAD)
    tall = (heads, n, HEAD)
    full = (heads, n, n)
    flat = (n, width)
    token = ((8, HEAD), F32, "v")
    parts = heads // BATCH
    vm = pltpu.VMEM

    half = n // 2
    inner = (heads, 2, half, half)
    corner = (heads, half, half)
    pair = (heads, n, 2 * HEAD)
    turned = (heads, HEAD, n)
    maps, inverse, cross, tkv = call(
        map_kernel,
        [
            (wide, F32, "v"), (inner, BF16, "h"), (corner, BF16, "h"),
            ((heads, n, 2 * HEAD), BF16, "h"),
        ],
        [(keys, "h"), (values, "h"), (rates, "h")],
        [
            vm(flat, BF16), vm(flat, BF16), vm((heads, n), F32),
            vm(inner, BF16), vm(corner, BF16), vm((heads, n, 2 * HEAD), BF16),
        ],
        copies=5 + 2 * parts,
    )
    own_maps = swap(maps, near)
    qt, qt_turned, offset, scores, own_init, prepared = call(
        prepare_kernel,
        [
            (tall, BF16, "h"), (turned, BF16, "h"), (tall, F32, "h"), (full, BF16, "h"),
            ((HEAD, HEAD), F32, "h"), token,
        ],
        [(queries, "h"), (keys, "h"), (rates, "h"), (tkv, "h"), (init_weight, "h")],
        [
            vm(flat, BF16), vm(flat, BF16), vm((heads, n), F32), vm(pair, BF16), vm(tall, BF16),
            vm(turned, BF16), vm(tall, F32), vm(full, BF16),
        ],
        copies=2 + 7 * parts,
    )
    slab = (HEAD, 2 * HEAD)
    block = (HEAD, HEAD)
    whole, tree, factors = call(
        group_kernel,
        [(slab, F32, "v"), ((3, HEAD, 2 * HEAD), F32, "v"), ((6, HEAD, HEAD), F32, "v")],
        [(own_maps, "v")],
    )
    other_map = lax.ppermute(whole, "ctx", across)
    (sent,) = call(
        pair_kernel,
        [((PLANES, HEAD, 2 * HEAD), F32, "v")],
        [(whole, "v"), (other_map, "v"), (prepared, "v")],
    )
    pair_maps = swap(sent, far)
    starts, gain_row = call(
        start_kernel,
        [(square, F32, "v"), ((1, width), F32, "v")],
        [
            (own_maps, "v"), (tree, "v"), (pair_maps, "v"), (other_map, "v"), (own_init, "v"),
            (gain_row, "h"),
        ],
        copies=1,
    )
    weights = swap(starts, near)
    hidden, stats = call(
        hidden_kernel,
        [(flat, F32, "v"), ((8, n), F32, "v")],
        [(qt, "v"), (offset, "v"), (cotangent, "v"), (gain_row, "v"), (weights, "v")],
    )
    other = lax.ppermute(stats, "tensor", [(0, 1), (1, 0)])
    normed, dz, local_grad = call(
        norm_kernel,
        [(flat, BF16, "h"), (flat, BF16, "h"), (square, F32, "h")],
        [
            (hidden, "v"), (cotangent, "v"), (gain_row, "v"), (stats, "v"), (other, "v"),
            (qt_turned, "v"),
        ],
        [vm(flat, BF16), vm(flat, BF16), vm(square, F32)],
        copies=3 * parts,
    )
    own_grads = swap(local_grad, near)
    grad_queries, dk_part, scaled_residual, queried = call(
        query_kernel,
        [(flat, BF16, "h"), (tall, BF16, "h"), (tall, BF16, "h"), token],
        [
            (queries, "h"), (keys, "h"), (rates, "h"), (tkv, "h"), (dz, "h"), (weights, "v"),
        ],
        [
            vm(flat, BF16), vm(flat, BF16), vm((heads, n), F32), vm(pair, BF16),
            vm(flat, BF16), vm(flat, BF16), vm(tall, BF16), vm(tall, BF16),
        ],
        copies=1 + 7 * parts,
    )
    u, tek, settled = call(
        adjoint_residual_kernel,
        [(tall, BF16, "h"), (tall, BF16, "h"), token],
        [
            (keys, "h"), (rates, "h"), (scores, "h"), (inverse, "h"), (cross, "h"), (dz, "h"),
        ],
        [
            vm(flat, BF16), vm((heads, n), F32), vm(full, BF16), vm(inner, BF16),
            vm(corner, BF16), vm(flat, BF16), vm(tall, BF16), vm(tall, BF16),
        ],
        copies=1 + 7 * parts,
    )
    steps = (PLANES, HEAD, HEAD)
    after, first, early, up = call(
        adjoint_kernel,
        [(steps, F32, "a"), (steps, F32, "a"), (block, F32, "a"), ((7, HEAD, HEAD), F32, "v")],
        [(pair_maps, "v"), (own_maps, "v"), (factors, "v"), (other_map, "v")],
    )
    whole, sums = call(
        gather_kernel,
        [(block, F32, "v"), ((6, HEAD, HEAD), F32, "v")],
        [(up, "v"), (own_grads, "v"), (queried, "v")],
    )
    other_grad = lax.ppermute(whole, "ctx", across)
    (sent,) = call(
        pair_gradient_kernel,
        [(steps, F32, "v")],
        [(early, "v"), (whole, "v"), (other_grad, "v"), (settled, "v")],
    )
    pair_grads = swap(sent, far)
    (ends,) = call(
        end_kernel,
        [((GROUP, HEAD + 8, HEAD), F32, "v")],
        [
            (after, "v"), (first, "v"), (own_maps, "v"), (factors, "v"), (own_grads, "v"),
            (sums, "v"), (other_map, "v"), (other_grad, "v"), (pair_grads, "v"),
        ],
        [vm(block, F32)],
    )
    adjoint = swap(ends, near)
    grad_keys, grad_values, grad_rates, grad_init = call(
        key_kernel,
        [(flat, BF16, "h"), (flat, BF16, "h"), ((heads, n), F32, "v"), ((heads, n), F32, "v")],
        [
            (keys, "v"), (rates, "v"), (tek, "v"), (scaled_residual, "v"), (u, "v"),
            (dk_part, "v"), (weights, "v"), (adjoint, "v"),
        ],
        [vm(flat, BF16), vm(flat, BF16)],
        copies=1 + heads // 2,
    )
    return (normed, grad_queries, grad_keys, grad_values, grad_rates, grad_init)


def solution(mesh):
    in_specs = (
        P("ctx", "tensor"),
        P("ctx", "tensor"),
        P("ctx", "tensor"),
        P("tensor", "ctx"),
        P("tensor", None, None),
        P("tensor"),
        P("ctx", "tensor"),
    )
    out_specs = (
        P("ctx", "tensor"),
        P("ctx", "tensor"),
        P("ctx", "tensor"),
        P("ctx", "tensor"),
        P("tensor", "ctx"),
        P("tensor", "ctx"),
    )
    return jax.shard_map(local, mesh=mesh, in_specs=in_specs, out_specs=out_specs, check_vma=False)
```
